512 devices in a mesh: grp: 64 (over y, z), rep: 8 (over x, core).
Axes of the slice: x: 4, y: 4, z: 16, core: 2. Of those that a mesh axis runs over, the one named last changes fastest.
Arguments:
- table: float32 [131072, 400], P(('grp', 'rep')), may hold values from -1.2 to 1.2
- row_state: float32 [131072], P(('grp', 'rep')), may hold values from 0.01 to 0.1
- relations: float32 [2, 400, 400], replicated, may hold values from -0.3125 to 0.3125
- touched: int32 [32768, 32], P(('grp', 'rep')), may hold values from 0 to 255
- source: int32 [262144], P(('grp', 'rep')), may hold values from 0 to 2047
- target: int32 [262144], P(('grp', 'rep')), may hold values from 0 to 2047
- neg_slots: int32 [1024], P(('grp', 'rep')), may hold values from 0 to 2047
Outputs:
- new_table: float32 [131072, 400], P(('grp', 'rep'))
- new_state: float32 [131072], P(('grp', 'rep'))
The draws below stay inside these ranges and needn't reach their ends.
Inputs may be any that keep to these rules, and one draw needn't show every extreme that they name: `touched`: local row numbers of the owning device. `source`: slot numbers of the receiving device. `target`: slot numbers of the receiving device. `neg_slots`: slot numbers of the contributing device.
All inputs are finite; a program needn't handle non-finite values.
Results may differ from the reference program's by a relative error of at most 0.0001.
Values sent between devices are 32-bit elements; how exact they have to be, the bound alone decides.
No kernel may reach another device: no remote copies, remote signals or barrier semaphores. Data moves between devices by JAX's collectives and lax.ppermute only.
A program may use at most 64 MiB of HBM per device.

```python
import math
import jax
import jax.numpy as jnp
import numpy as np
from jax import lax

D = 400
ROWS_DEV = 256
SENT = 32
EDGES_DEV = 512
NEG_DEV = 2
REL_COUNT = 2
PER_REL = 256
SLOTS = 2048
NEG = 128
ROWS = 131072
TOUCH_ROWS = 32768
EDGES = 262144
NEG_ALL = 1024
N_GRP = 64
N_REP = 8


def with_ends(drawn, rng, low, high):
    extent = drawn.shape
    spot = [jax.random.randint(jax.random.fold_in(rng, axis), (), 0, extent[axis]) for axis in range(len(extent))]
    drawn = drawn.at[tuple(spot)].set(low)
    longest = extent.index(max(extent))
    spot[longest] = (spot[longest] + 1) % extent[longest]
    return drawn.at[tuple(spot)].set(high)


def shard_levels(rng, extent, shards, least, top_value):
    level = 1.0
    for dim, parts in shards:
        steps = jax.random.uniform(jax.random.fold_in(jax.random.fold_in(rng, 6), dim), (parts,), jnp.float32, least / len(shards), top_value / len(shards))
        level = level * jnp.repeat(jnp.exp(steps), extent[dim] // parts).reshape((-1,) + (1,) * (len(extent) - 1 - dim))
    return level


def cumulative_ranks(number_of, skew):
    portions = [(1 << 20) // math.isqrt(rank ** skew) + 1 for rank in range(1, number_of + 1)]
    scale = 1 + sum(portions) // (1 << 30)
    return np.cumsum(np.array([max(1, weight // scale) for weight in portions]))


def ranked_ids(stream_key, extent, number_of, lean):
    grid = cumulative_ranks(number_of, lean)
    lot = jax.random.randint(jax.random.fold_in(stream_key, 1), extent, 0, int(grid[number_of - 1]))
    standing = jnp.searchsorted(jnp.asarray(grid, jnp.int32), lot, side="right")
    return jax.random.permutation(jax.random.fold_in(stream_key, 2), number_of)[standing].astype(jnp.int32)


def centred(rng, shape, scale, limit, cuts=(), held_as=jnp.bfloat16):
    result = scale * jax.random.normal(rng, shape, jnp.float32)
    if cuts:
        result = result * shard_levels(rng, shape, cuts, -0.22, 0.18)
    return jnp.clip(result, -limit, limit).astype(held_as)


def setup_inputs(seed: int = 0) -> dict:
    keys = jax.random.split(jax.random.key(seed), 8)
    return {
        "table": centred(keys[0], (ROWS, D), 0.2, 1.2, ((0, 512),), jnp.float32),
        "row_state": jnp.clip(jnp.exp(math.log(0.1) - 2.3025851 * jax.random.uniform(keys[1], (ROWS,), jnp.float32) ** shard_levels(keys[1], (ROWS,), ((0, 512),), -0.2, 0.2)), 0.01, 0.1),
        "relations": centred(keys[2], (REL_COUNT, D, D), D ** -0.5, 0.3125, (), jnp.float32),
        "touched": with_ends(jax.random.randint(keys[3], (TOUCH_ROWS, SENT), 0, ROWS_DEV), jax.random.fold_in(keys[3], 1), 0, ROWS_DEV - 1).astype(jnp.int32),
        "source": with_ends(ranked_ids(keys[4], (EDGES,), SLOTS, 2), jax.random.fold_in(keys[4], 3), 0, SLOTS - 1).astype(jnp.int32),
        "target": with_ends(jax.random.randint(keys[5], (EDGES,), 0, SLOTS), jax.random.fold_in(keys[5], 1), 0, SLOTS - 1).astype(jnp.int32),
        "neg_slots": with_ends(jax.random.randint(keys[6], (NEG_ALL,), 0, SLOTS), jax.random.fold_in(keys[6], 1), 0, SLOTS - 1).astype(jnp.int32),
    }


PRECISE = lax.Precision.HIGHEST
LEARN_RATE = 0.1
EPSILON = 1e-06

def gather_rows(source_table, row_index):
    return jnp.take(source_table, row_index, axis=0)

def add_rows(base, row_index, values):
    return base.at[row_index].add(values)

def by_relation(rows, operators):
    width = rows.shape[-1]
    blocked = rows.reshape(N_GRP, REL_COUNT, PER_REL, width)
    moved = jnp.einsum('gked,kdf->gkef', blocked, operators, precision=PRECISE)
    return moved.reshape(N_GRP, EDGES_DEV, width)

def reference(table, row_state, relations, touched, source, target, neg_slots):
    width = table.shape[1]
    owned = table.reshape(N_GRP, N_REP, ROWS_DEV, width)
    lists = touched.reshape(N_GRP, N_REP, N_GRP, SENT)
    sources = source.reshape(N_GRP, N_REP, EDGES_DEV)
    targets = target.reshape(N_GRP, N_REP, EDGES_DEV)
    neg_ids = neg_slots.reshape(N_GRP, N_REP, NEG_DEV)
    picker = jax.vmap(gather_rows)
    adder = jax.vmap(add_rows)
    transposed = jnp.swapaxes(relations, 1, 2)
    grads = []
    for column in range(N_REP):
        ids = lists[:, column]
        fetched = picker(owned[:, column], ids)
        slots = jnp.swapaxes(fetched, 0, 1).reshape(N_GRP, SLOTS, width)
        head = picker(slots, sources[:, column])
        tail = picker(slots, targets[:, column])
        negatives = picker(slots, neg_ids[:, column]).reshape(NEG, width)
        query = by_relation(head, relations)
        positive = lax.optimization_barrier(jnp.sum(query * tail, -1))
        negative = jnp.einsum('ged,nd->gen', query, negatives, precision=PRECISE)
        grad_pos = jax.nn.sigmoid(positive) - 1.0
        grad_neg = jax.nn.sigmoid(negative) / NEG
        grad_query = grad_pos[..., None] * tail + jnp.einsum('gen,nd->ged', grad_neg, negatives, precision=PRECISE)
        grad_tail = grad_pos[..., None] * query
        grad_negs = jnp.einsum('gen,ged->nd', grad_neg, query, precision=PRECISE)
        grad_head = by_relation(grad_query, transposed)
        slot_grad = jnp.zeros((N_GRP, SLOTS, width), jnp.float32)
        slot_grad = adder(slot_grad, sources[:, column], grad_head)
        slot_grad = adder(slot_grad, targets[:, column], grad_tail)
        slot_grad = adder(slot_grad, neg_ids[:, column], grad_negs.reshape(N_GRP, NEG_DEV, width))
        returned = jnp.swapaxes(slot_grad.reshape(N_GRP, N_GRP, SENT, width), 0, 1)
        row_grad = adder(jnp.zeros((N_GRP, ROWS_DEV, width), jnp.float32), ids.reshape(N_GRP, N_GRP * SENT), returned.reshape(N_GRP, N_GRP * SENT, width))
        grads.append(row_grad)
    row_grad = jnp.stack(grads, 1).reshape(ROWS, width)
    new_state = row_state + lax.optimization_barrier(jnp.mean(row_grad * row_grad, -1))
    new_table = table - LEARN_RATE * row_grad / (jnp.sqrt(new_state)[:, None] + EPSILON)
    return (new_table, new_state)
```

```python
import jax
import jax.numpy as jnp
from jax import lax
from jax.sharding import PartitionSpec as P

PRECISE = lax.Precision.HIGHEST
LEARN_RATE = 0.1
EPSILON = 1e-06
LANES = 128


def exchange(blocks):
    return lax.all_to_all(blocks, "grp", split_axis=0, concat_axis=0, tiled=True)


def take_rows(rows, ids):
    return jnp.take(rows, ids, axis=0, mode="clip")


def to_lanes(rows, peers):
    width = rows.shape[1]
    wide = -(-width // LANES) * LANES
    return jnp.pad(rows, ((0, 0), (0, wide - width))).reshape(peers, -1, LANES)


def per_device(table, row_state, relations, touched, source, target, neg_slots):
    width = table.shape[1]
    peers, sent = touched.shape
    kinds = relations.shape[0]
    per_rel = source.shape[0] // kinds
    slot_count = peers * sent
    own_count = neg_slots.shape[0]
    neg_total = peers * own_count
    outgoing = take_rows(table, touched.reshape(-1))
    slots = exchange(outgoing.reshape(peers, -1, LANES)).reshape(slot_count, width)
    own_neg = to_lanes(take_rows(slots, neg_slots), 1)
    gathered = exchange(jnp.broadcast_to(own_neg, (peers,) + own_neg.shape[1:]))
    negatives = gathered.reshape(neg_total, -1)[:, :width]
    head = take_rows(slots, source)
    tail = take_rows(slots, target)
    query = jnp.einsum(
        "ked,kdf->kef", head.reshape(kinds, per_rel, width), relations, precision=PRECISE
    ).reshape(kinds * per_rel, width)
    positive = jnp.sum(query * tail, -1)
    negative = jnp.dot(query, negatives.T, precision=PRECISE)
    grad_pos = jax.nn.sigmoid(positive) - 1.0
    grad_neg = jax.nn.sigmoid(negative) / neg_total
    grad_negs = jnp.dot(grad_neg.T, query, precision=PRECISE)
    shares = exchange(to_lanes(grad_negs, peers))
    mine = jnp.sum(shares, 0).reshape(own_count, -1)[:, :width]
    grad_query = grad_pos[:, None] * tail + jnp.dot(grad_neg, negatives, precision=PRECISE)
    grad_tail = grad_pos[:, None] * query
    grad_head = jnp.einsum(
        "kef,kdf->ked", grad_query.reshape(kinds, per_rel, width), relations, precision=PRECISE
    ).reshape(kinds * per_rel, width)
    slot_grad = jnp.zeros((slot_count, width), jnp.float32).at[source].add(grad_head)
    slot_grad = slot_grad.at[target].add(grad_tail)
    slot_grad = slot_grad.at[neg_slots].add(mine)
    returned = exchange(slot_grad.reshape(peers, -1, LANES)).reshape(slot_count, width)
    row_grad = jnp.zeros(table.shape, jnp.float32).at[touched.reshape(-1)].add(returned)
    new_state = row_state + jnp.mean(row_grad * row_grad, -1)
    new_table = table - LEARN_RATE * row_grad / (jnp.sqrt(new_state)[:, None] + EPSILON)
    return (new_table, new_state)


def solution(mesh):
    return jax.shard_map(
        per_device,
        mesh=mesh,
        in_specs=(
            P(("grp", "rep"), None),
            P(("grp", "rep")),
            P(),
            P(("grp", "rep"), None),
            P(("grp", "rep")),
            P(("grp", "rep")),
            P(("grp", "rep")),
        ),
        out_specs=(P(("grp", "rep"), None), P(("grp", "rep"))),
        check_vma=False,
    )
```

```python
import functools

import jax
import jax.numpy as jnp
from jax import lax
from jax.experimental import pallas as pl
from jax.experimental.pallas import tpu as pltpu
from jax.sharding import PartitionSpec as P

PRECISE = lax.Precision.HIGHEST
LEARN_RATE = 0.1
EPSILON = 1e-06
LANES = 128
VMEM = 56 * 1024 * 1024
F32 = jnp.float32
BF16 = jnp.bfloat16


def exchange(blocks):
    return lax.all_to_all(blocks, "grp", split_axis=0, concat_axis=0, tiled=True)


def take_rows(rows, ids):
    return jnp.take(rows, ids, axis=0, mode="clip")


def to_lanes(rows, peers):
    width = rows.shape[1]
    wide = -(-width // LANES) * LANES
    return jnp.pad(rows, ((0, 0), (0, wide - width))).reshape(peers, -1, LANES)


def full_path(table, row_state, relations, touched, source, target, neg_slots):
    width = table.shape[1]
    peers, sent = touched.shape
    kinds = relations.shape[0]
    per_rel = source.shape[0] // kinds
    slot_count = peers * sent
    own_count = neg_slots.shape[0]
    neg_total = peers * own_count
    outgoing = take_rows(table, touched.reshape(-1))
    slots = exchange(outgoing.reshape(peers, -1, LANES)).reshape(slot_count, width)
    own_neg = to_lanes(take_rows(slots, neg_slots), 1)
    gathered = exchange(jnp.broadcast_to(own_neg, (peers,) + own_neg.shape[1:]))
    negatives = gathered.reshape(neg_total, -1)[:, :width]
    head = take_rows(slots, source)
    tail = take_rows(slots, target)
    query = jnp.einsum(
        "ked,kdf->kef", head.reshape(kinds, per_rel, width), relations, precision=PRECISE
    ).reshape(kinds * per_rel, width)
    positive = jnp.sum(query * tail, -1)
    negative = jnp.dot(query, negatives.T, precision=PRECISE)
    grad_pos = jax.nn.sigmoid(positive) - 1.0
    grad_neg = jax.nn.sigmoid(negative) / neg_total
    grad_negs = jnp.dot(grad_neg.T, query, precision=PRECISE)
    shares = exchange(to_lanes(grad_negs, peers))
    mine = jnp.sum(shares, 0).reshape(own_count, -1)[:, :width]
    grad_query = grad_pos[:, None] * tail + jnp.dot(grad_neg, negatives, precision=PRECISE)
    grad_tail = grad_pos[:, None] * query
    grad_head = jnp.einsum(
        "kef,kdf->ked", grad_query.reshape(kinds, per_rel, width), relations, precision=PRECISE
    ).reshape(kinds * per_rel, width)
    slot_grad = jnp.zeros((slot_count, width), F32).at[source].add(grad_head)
    slot_grad = slot_grad.at[target].add(grad_tail)
    slot_grad = slot_grad.at[neg_slots].add(mine)
    returned = exchange(slot_grad.reshape(peers, -1, LANES)).reshape(slot_count, width)
    row_grad = jnp.zeros(table.shape, F32).at[touched.reshape(-1)].add(returned)
    new_state = row_state + jnp.mean(row_grad * row_grad, -1)
    new_table = table - LEARN_RATE * row_grad / (jnp.sqrt(new_state)[:, None] + EPSILON)
    return new_table.T, new_state.reshape(1, -1)


REGION = 24
CAP = REGION - 1
PARTS = 3
BLOCK = PARTS * REGION
TAIL = 16
PER_LINE = LANES // TAIL
WIDE = (PARTS + 1) * LANES


def iota(shape, dim):
    return lax.broadcasted_iota(jnp.int32, shape, dim)


def pieces(x, count):
    out = []
    for _ in range(count):
        piece = x.astype(BF16)
        out.append(piece)
        x = x - piece.astype(F32)
    return out


def dot(a, b, a_dim=1, b_dim=0):
    return lax.dot_general(a, b, (((a_dim,), (b_dim,)), ((), ())), preferred_element_type=F32)


def pick(onehot, x, count, b_dim=0):
    total = None
    for piece in reversed(pieces(x, count)):
        term = dot(onehot, piece, 1, b_dim)
        total = term if total is None else total + term
    return total


def dot3(a, b, a_dim=1, b_dim=0):
    a_hi, a_lo = a if isinstance(a, tuple) else pieces(a, 2)
    b_hi, b_lo = b if isinstance(b, tuple) else pieces(b, 2)
    small = dot(a_lo, b_hi, a_dim, b_dim) + dot(a_hi, b_lo, a_dim, b_dim)
    return small + dot(a_hi, b_hi, a_dim, b_dim)


def spread(x):
    step = TAIL
    while step < LANES:
        x = x + pltpu.roll(x, step, 1)
        step *= 2
    return x


def call(kernel, outs, **kw):
    return pl.pallas_call(
        kernel,
        out_shape=outs,
        compiler_params=pltpu.CompilerParams(vmem_limit_bytes=VMEM),
        **kw,
    )


def shaped(*shape, dtype=F32):
    return jax.ShapeDtypeStruct(shape, dtype)


def mark_kernel(sent, ids_ref, marks_ref, place_ref):
    peers = marks_ref.shape[0]
    ids = ids_ref[...]
    count = ids.shape[1]
    owner = lax.shift_right_arithmetic(ids, sent.bit_length() - 1)
    within = lax.bitwise_and(ids, sent - 1)
    at_owner = (iota((peers, count), 0) == owner).astype(BF16)
    at_within = (iota((LANES, count), 0) == within).astype(BF16)
    marks = dot(at_owner, at_within, 1, 1)
    used = jnp.where(dot(at_within, at_owner, 1, 1) > 0.0, 1.0, 0.0).astype(BF16)
    upto = (iota((LANES, LANES), 1) <= iota((LANES, LANES), 0)).astype(BF16)
    rank = dot(upto, used)
    flag = jnp.where(jnp.max(rank) > CAP, 1.0, 0.0)
    lane = iota(marks.shape, 1)
    marks_ref[...] = jnp.where(lane == sent, flag, jnp.where(marks > 0.0, 1.0, 0.0))
    mine = dot(rank.astype(BF16), at_owner) * at_within.astype(F32)
    order = jnp.sum(mine, 0, keepdims=True).astype(jnp.int32)
    place_ref[...] = owner * REGION + order - 1


def pack_kernel(sent, marks_ref, touched_ref, table_ref, out_ref, rows_ref, onehot):
    peers = marks_ref.shape[0]
    lane = iota((peers, LANES), 1)
    marks = jnp.where(lane < sent, marks_ref[...], 0.0)
    upto = (iota((LANES, LANES), 0) <= iota((LANES, LANES), 1)).astype(BF16)
    rank = jnp.where(marks > 0.0, dot(marks.astype(BF16), upto), 0.0)
    local = touched_ref[...].astype(F32) + 1.0
    owned = table_ref.shape[1]
    spot = iota((peers, owned), 1)
    rows = jnp.full((peers, LANES), -1, jnp.int32)
    for k in range(CAP):
        chosen = jnp.where(rank == k + 1.0, local, 0.0)
        row = jnp.sum(chosen, 1, keepdims=True).astype(jnp.int32) - 1
        rows = jnp.where(lane == k, row, rows)
        onehot[k * peers : (k + 1) * peers, :] = (spot == row).astype(F32).astype(BF16)
    rows_ref[...] = rows
    table = table_ref[...]
    main = PARTS * LANES
    wide = jnp.concatenate([table[:main]] + [table[main:]] * PER_LINE, 0)
    wide = pieces(wide, 3)
    group = lane // TAIL
    for part in range(PARTS):
        first = part * PER_LINE
        last = min(first + PER_LINE, CAP)
        chosen = onehot[first * peers : last * peers, :]
        got = dot(chosen, wide[2], 1, 1) + dot(chosen, wide[1], 1, 1)
        got = got + dot(chosen, wide[0], 1, 1)
        line = jnp.zeros((peers, LANES), F32)
        for k in range(first, last):
            mine = got[(k - first) * peers : (k - first + 1) * peers]
            for t in range(PARTS):
                out_ref[pl.ds(t * REGION + k, peers, stride=BLOCK), :] = mine[
                    :, t * LANES : (t + 1) * LANES
                ]
            line = line + jnp.where(group == k - first, mine[:, main:], 0.0)
        out_ref[pl.ds(part * REGION + CAP, peers, stride=BLOCK), :] = line


def unpack(ref, peers):
    count = peers * REGION
    parts, tails = [], []
    for t in range(PARTS):
        part = ref[:, t * REGION : (t + 1) * REGION, :]
        parts.append(part.reshape(count, LANES))
        tails.append(jnp.broadcast_to(part[:, CAP:, :], (peers, PER_LINE, LANES)))
    tails = jnp.concatenate(tails, 1)
    own = iota(tails.shape, 2) // TAIL == iota(tails.shape, 1) % PER_LINE
    parts.append(jnp.where(own, tails, 0.0).reshape(count, LANES))
    return parts


def negs_kernel(place_ref, block_ref, out_ref):
    n = pl.program_id(0)
    k = lax.rem(place_ref[n], REGION)
    part = lax.div(k, PER_LINE)
    line = block_ref[0, pl.ds(part * REGION + CAP, 1), :]
    shift = lax.rem(LANES - TAIL * lax.rem(k, PER_LINE), LANES)
    line = pltpu.roll(line, shift, 1)
    line = jnp.where(iota(line.shape, 1) < TAIL, line, 0.0)
    rows = [block_ref[0, pl.ds(t * REGION + k, 1), :] for t in range(PARTS)] + [line]
    peers = out_ref.shape[0]
    depth = PARTS + 1
    for i in range(out_ref.shape[1] // depth):

        @pl.when(n == i)
        def _():
            for t in range(depth):
                out_ref[:, i * depth + t : i * depth + t + 1, :] = jnp.broadcast_to(
                    rows[t].reshape(1, 1, LANES), (peers, 1, LANES)
                )


def query_kernel(block_ref, place_ref, rel_hi_ref, rel_lo_ref, query_ref, tail_ref, pos_ref):
    peers = block_ref.shape[0]
    edges = query_ref.shape[0]
    kinds = rel_hi_ref.shape[0]
    per_rel = edges // kinds
    count = peers * REGION
    slots = [pieces(part, 2) for part in unpack(block_ref, peers)]
    hi = jnp.concatenate([p[0] for p in slots], 1)
    lo = jnp.concatenate([p[1] for p in slots], 1)
    main = PARTS * LANES

    def rows_at(start, size):
        spot = place_ref[start : start + size, :]
        chosen = (iota((size, count), 1) == spot).astype(F32).astype(BF16)
        got = dot(chosen, lo) + dot(chosen, hi)
        return jnp.concatenate([got[:, :main], spread(got[:, main:])], 1)

    for kind in range(kinds):
        start = kind * per_rel
        head = rows_at(start, per_rel)
        query = dot3(head, (rel_hi_ref[kind], rel_lo_ref[kind]))
        tail = rows_at(edges + start, per_rel)
        query_ref[start : start + per_rel, :] = query
        tail_ref[start : start + per_rel, :] = tail
        positive = jnp.sum(query * tail, 1, keepdims=True)
        pos_ref[start : start + per_rel, :] = jax.nn.sigmoid(positive) - 1.0


def negatives_of(ref):
    depth = PARTS + 1
    total = ref.shape[0] // depth
    return jnp.concatenate([ref[pl.ds(t, total, stride=depth), :] for t in range(depth)], 1)


def shares_kernel(query_ref, negs_ref, out_ref):
    negs = negatives_of(negs_ref)
    total = negs.shape[0]
    query = tuple(pieces(query_ref[...], 2))
    logits = dot3(tuple(pieces(negs, 2)), query, 1, 1)
    grad = dot3(jax.nn.sigmoid(logits) / total, query)
    depth = PARTS + 1
    for t in range(depth):
        out_ref[pl.ds(t, total, stride=depth), :] = grad[:, t * LANES : (t + 1) * LANES]


def grads_kernel(
    query_ref, tail_ref, pos_ref, negs_ref, place_ref, rel_hi_ref, rel_lo_ref, out_ref, grad_hi, grad_lo
):
    edges = query_ref.shape[0]
    kinds = rel_hi_ref.shape[0]
    per_rel = edges // kinds
    peers = out_ref.shape[0]
    main = PARTS * LANES
    negs = negatives_of(negs_ref)
    total = negs.shape[0]
    negs = tuple(pieces(negs, 2))

    def keep(start, grad):
        grad = jnp.concatenate([grad[:, :main], spread(grad[:, main:])], 1)
        hi, lo = pieces(grad, 2)
        grad_hi[start : start + per_rel, :] = hi
        grad_lo[start : start + per_rel, :] = lo

    for kind in range(kinds):
        start = kind * per_rel
        span = slice(start, start + per_rel)
        query = query_ref[span, :]
        pos = pos_ref[span, :]
        logits = dot3(query, negs, 1, 1)
        grad_neg = jax.nn.sigmoid(logits) / total
        grad_query = pos * tail_ref[span, :] + dot3(grad_neg, negs)
        keep(start, dot3(grad_query, (rel_hi_ref[kind], rel_lo_ref[kind]), 1, 1))
        keep(edges + start, pos * query)
    spot = place_ref[...]
    half = peers // 2
    count = half * REGION
    for first in (0, half):
        chosen = iota((count, 2 * edges), 0) + first * REGION == spot
        chosen = chosen.astype(F32).astype(BF16)
        got = dot(chosen, grad_lo[...]) + dot(chosen, grad_hi[...])
        tails = got[:, main:].reshape(half * PARTS, PER_LINE, LANES)
        own = iota(tails.shape, 2) // TAIL == iota(tails.shape, 1)
        line = jnp.sum(jnp.where(own, tails, 0.0), 1, keepdims=True)
        line = jnp.broadcast_to(line, tails.shape).reshape(half, REGION, LANES)
        last = iota((half, REGION, LANES), 1) == CAP
        for t in range(PARTS):
            part = got[:, t * LANES : (t + 1) * LANES].reshape(half, REGION, LANES)
            mine = line[:, t * PER_LINE : (t + 1) * PER_LINE, :]
            mine = jnp.concatenate([mine] * PARTS, 1)
            out_ref[first : first + half, t * REGION : (t + 1) * REGION, :] = jnp.where(
                last, mine, part
            )


def add_kernel(place_ref, shares_ref, blocks_ref, out_ref, held, sems):
    depth = PARTS + 1
    mine = jnp.sum(shares_ref[...], 0)
    number = held.shape[0]
    owner = [lax.div(place_ref[n], REGION) for n in range(number)]
    for n in range(number):
        pltpu.make_async_copy(blocks_ref.at[owner[n]], held.at[n], sems.at[n]).start()
    for n in range(number):
        pltpu.make_async_copy(blocks_ref.at[owner[n]], held.at[n], sems.at[n]).wait()
    for n in range(number):
        k = lax.rem(place_ref[n], REGION)
        part = lax.div(k, PER_LINE)
        shift = TAIL * lax.rem(k, PER_LINE)
        lines = [mine[n * depth + t : n * depth + t + 1] for t in range(PARTS)]
        last = pltpu.roll(mine[n * depth + PARTS : (n + 1) * depth], shift, 1)
        slot = jnp.int32(n)
        for other in reversed(range(n)):
            slot = jnp.where(owner[other] == owner[n], other, slot)
        for t in range(PARTS):
            held[slot, pl.ds(t * REGION + k, 1), :] += lines[t]
        held[slot, pl.ds(part * REGION + CAP, 1), :] += last
        for other in range(n):

            @pl.when(owner[other] == owner[n])
            def _():
                held[n] = held[other]

    for n in range(number):
        copy = pltpu.make_async_copy(held.at[n], out_ref.at[owner[n]], sems.at[n])
        copy.start()
        copy.wait()


def update_kernel(blocks_ref, rows_ref, table_ref, state_ref, new_table_ref, new_state_ref):
    peers = blocks_ref.shape[0]
    width, owned = table_ref.shape
    count = peers * REGION
    main = PARTS * LANES
    parts = [pieces(part, 2) for part in unpack(blocks_ref, peers)]
    hi = jnp.concatenate([p[0] for p in parts], 1)
    lo = jnp.concatenate([p[1] for p in parts], 1)
    chosen = (iota((owned, count), 0) == rows_ref[...]).astype(F32).astype(BF16)
    got = dot(chosen, lo) + dot(chosen, hi)
    tails = spread(got[:, main:])
    tails = jnp.where(iota(tails.shape, 1) < TAIL, tails, 0.0)
    grad = jnp.concatenate([got[:, :main], tails], 1).T
    state = state_ref[...] + jnp.sum(grad * grad, 0, keepdims=True) / width
    new_state_ref[...] = state
    grad = grad[:width]
    new_table_ref[...] = table_ref[...] - LEARN_RATE * grad / (jnp.sqrt(state) + EPSILON)


def compact_path(marks, place, table, row_state, relations, touched, neg_slots):
    owned, width = table.shape
    peers, sent = touched.shape
    own_count = neg_slots.shape[0]
    edges = (place.shape[1] - LANES) // 2
    count = peers * REGION
    wide = jnp.pad(relations, ((0, 0), (0, WIDE - width), (0, WIDE - width)))
    rel_hi = lax.reduce_precision(wide, 8, 7)
    rel_lo = (wide - rel_hi).astype(BF16)
    rel_hi = rel_hi.astype(BF16)
    spot = place[:, : 2 * edges]
    spot_column = spot.reshape(2 * edges, 1)
    neg_place = place[0, 2 * edges : 2 * edges + own_count]

    blocks, rows = call(
        functools.partial(pack_kernel, sent),
        (shaped(peers * BLOCK, LANES), shaped(peers, LANES, dtype=jnp.int32)),
        scratch_shapes=[pltpu.VMEM((CAP * peers, owned), BF16)],
    )(marks, jnp.pad(touched, ((0, 0), (0, LANES - sent))), table.T)
    blocks = exchange(blocks.reshape(peers, BLOCK, LANES))
    depth = own_count * (PARTS + 1)
    own_negs = call(
        negs_kernel,
        shaped(peers, depth, LANES),
        grid_spec=pltpu.PrefetchScalarGridSpec(
            num_scalar_prefetch=1,
            grid=(own_count,),
            in_specs=[pl.BlockSpec((1, BLOCK, LANES), lambda n, at: (at[n] // REGION, 0, 0))],
            out_specs=pl.BlockSpec((peers, depth, LANES), lambda n, at: (0, 0, 0)),
        ),
    )(neg_place, blocks)
    negs = exchange(own_negs).reshape(peers * depth, LANES)
    query, tail, pos = call(
        query_kernel,
        (shaped(edges, WIDE), shaped(edges, WIDE), shaped(edges, 1)),
    )(blocks, spot_column, rel_hi, rel_lo)
    shares = call(shares_kernel, shaped(peers * depth, LANES))(query, negs)
    shares = exchange(shares.reshape(peers, depth, LANES))
    grads = call(
        grads_kernel,
        shaped(peers, BLOCK, LANES),
        scratch_shapes=[pltpu.VMEM((2 * edges, WIDE), BF16)] * 2,
    )(query, tail, pos, negs, spot, rel_hi, rel_lo)
    grads = call(
        add_kernel,
        shaped(peers, BLOCK, LANES),
        in_specs=[
            pl.BlockSpec(memory_space=pltpu.SMEM),
            pl.BlockSpec(memory_space=pltpu.VMEM),
            pl.BlockSpec(memory_space=pl.ANY),
        ],
        out_specs=pl.BlockSpec(memory_space=pl.ANY),
        scratch_shapes=[
            pltpu.VMEM((own_count, BLOCK, LANES), F32),
            pltpu.SemaphoreType.DMA((own_count,)),
        ],
        input_output_aliases={2: 0},
    )(neg_place, shares, grads)
    returned = exchange(grads)
    return call(
        update_kernel,
        (shaped(width, owned), shaped(1, owned)),
    )(returned, rows[:, :REGION].reshape(1, count), table.T, row_state.reshape(1, owned))


def per_device(table, row_state, relations, touched, source, target, neg_slots):
    peers, sent = touched.shape
    own_count = neg_slots.shape[0]
    filler = jnp.full((LANES - own_count,), -1, jnp.int32)
    ids = jnp.concatenate([source, target, neg_slots, filler]).reshape(1, -1)
    marks, place = call(
        functools.partial(mark_kernel, sent),
        (shaped(peers, LANES), shaped(1, ids.shape[1], dtype=jnp.int32)),
    )(ids)
    marks = exchange(marks.reshape(peers, 1, LANES)).reshape(peers, LANES)
    crowded = jnp.max(marks[:, sent]) > 0.0
    new_table, new_state = lax.cond(
        crowded,
        lambda: full_path(table, row_state, relations, touched, source, target, neg_slots),
        lambda: compact_path(marks, place, table, row_state, relations, touched, neg_slots),
    )
    return new_table.T, new_state.reshape(-1)


def solution(mesh):
    return jax.shard_map(
        per_device,
        mesh=mesh,
        in_specs=(
            P(("grp", "rep"), None),
            P(("grp", "rep")),
            P(),
            P(("grp", "rep"), None),
            P(("grp", "rep")),
            P(("grp", "rep")),
            P(("grp", "rep")),
        ),
        out_specs=(P(("grp", "rep"), None), P(("grp", "rep"))),
        check_vma=False,
    )
```

```python
import functools

import jax
import jax.numpy as jnp
from jax import lax
from jax.experimental import pallas as pl
from jax.experimental.pallas import tpu as pltpu
from jax.sharding import PartitionSpec as P

PRECISE = lax.Precision.HIGHEST
LEARN_RATE = 0.1
EPSILON = 1e-06
LANES = 128
VMEM = 56 * 1024 * 1024
F32 = jnp.float32
BF16 = jnp.bfloat16


def exchange(blocks):
    return lax.all_to_all(blocks, "grp", split_axis=0, concat_axis=0, tiled=True)


def take_rows(rows, ids):
    return jnp.take(rows, ids, axis=0, mode="clip")


def to_lanes(rows, peers):
    width = rows.shape[1]
    wide = -(-width // LANES) * LANES
    return jnp.pad(rows, ((0, 0), (0, wide - width))).reshape(peers, -1, LANES)


def full_path(table, row_state, relations, touched, source, target, neg_slots):
    width = table.shape[1]
    peers, sent = touched.shape
    kinds = relations.shape[0]
    per_rel = source.shape[0] // kinds
    slot_count = peers * sent
    own_count = neg_slots.shape[0]
    neg_total = peers * own_count
    outgoing = take_rows(table, touched.reshape(-1))
    slots = exchange(outgoing.reshape(peers, -1, LANES)).reshape(slot_count, width)
    own_neg = to_lanes(take_rows(slots, neg_slots), 1)
    gathered = exchange(jnp.broadcast_to(own_neg, (peers,) + own_neg.shape[1:]))
    negatives = gathered.reshape(neg_total, -1)[:, :width]
    head = take_rows(slots, source)
    tail = take_rows(slots, target)
    query = jnp.einsum(
        "ked,kdf->kef", head.reshape(kinds, per_rel, width), relations, precision=PRECISE
    ).reshape(kinds * per_rel, width)
    positive = jnp.sum(query * tail, -1)
    negative = jnp.dot(query, negatives.T, precision=PRECISE)
    grad_pos = jax.nn.sigmoid(positive) - 1.0
    grad_neg = jax.nn.sigmoid(negative) / neg_total
    grad_negs = jnp.dot(grad_neg.T, query, precision=PRECISE)
    shares = exchange(to_lanes(grad_negs, peers))
    mine = jnp.sum(shares, 0).reshape(own_count, -1)[:, :width]
    grad_query = grad_pos[:, None] * tail + jnp.dot(grad_neg, negatives, precision=PRECISE)
    grad_tail = grad_pos[:, None] * query
    grad_head = jnp.einsum(
        "kef,kdf->ked", grad_query.reshape(kinds, per_rel, width), relations, precision=PRECISE
    ).reshape(kinds * per_rel, width)
    slot_grad = jnp.zeros((slot_count, width), F32).at[source].add(grad_head)
    slot_grad = slot_grad.at[target].add(grad_tail)
    slot_grad = slot_grad.at[neg_slots].add(mine)
    returned = exchange(slot_grad.reshape(peers, -1, LANES)).reshape(slot_count, width)
    row_grad = jnp.zeros(table.shape, F32).at[touched.reshape(-1)].add(returned)
    new_state = row_state + jnp.mean(row_grad * row_grad, -1)
    new_table = table - LEARN_RATE * row_grad / (jnp.sqrt(new_state)[:, None] + EPSILON)
    return new_table.T, new_state.reshape(1, -1)


HEAD = 16
CAP = 20
REGION = 24
PARTS = 3
BLOCK = 64
EXTRA = PARTS * HEAD
TAIL = 16
PER_LINE = LANES // TAIL
LINES = EXTRA + PARTS * (CAP - HEAD)
WIDE = (PARTS + 1) * LANES
MATE = 16
SENT = 32
AT_COUNTS = 2 * SENT
AT_NEGS = 3 * SENT


def line_of(part, k):
    if k < HEAD:
        return part * HEAD + k
    return EXTRA + part * (CAP - HEAD) + k - HEAD


def iota(shape, dim):
    return lax.broadcasted_iota(jnp.int32, shape, dim)


def bits(mask):
    return jnp.where(mask, 1.0, 0.0).astype(BF16)


def shift_down(x, by):
    return lax.shift_right_logical(x, jnp.full(x.shape, by, x.dtype))


def pair_of(owner):
    return shift_down(owner, 5) * MATE + lax.bitwise_and(owner, MATE - 1)


def mate_of(owner):
    return lax.bitwise_xor(owner, MATE)


def pieces(x, count):
    out = []
    for _ in range(count):
        piece = x.astype(BF16)
        out.append(piece)
        x = x - piece.astype(F32)
    return out


def dot(a, b, a_dim=1, b_dim=0):
    return lax.dot_general(a, b, (((a_dim,), (b_dim,)), ((), ())), preferred_element_type=F32)


def dot3(a, b, a_dim=1, b_dim=0):
    a_hi, a_lo = a if isinstance(a, tuple) else pieces(a, 2)
    b_hi, b_lo = b if isinstance(b, tuple) else pieces(b, 2)
    small = dot(a_lo, b_hi, a_dim, b_dim) + dot(a_hi, b_lo, a_dim, b_dim)
    return small + dot(a_hi, b_hi, a_dim, b_dim)


def spread(x):
    step = TAIL
    while step < LANES:
        x = x + pltpu.roll(x, step, 1)
        step *= 2
    return x


def call(kernel, outs, **kw):
    return pl.pallas_call(
        kernel,
        out_shape=outs,
        compiler_params=pltpu.CompilerParams(vmem_limit_bytes=VMEM),
        **kw,
    )


def shaped(*shape, dtype=F32):
    return jax.ShapeDtypeStruct(shape, dtype)


VECTOR = pl.BlockSpec(memory_space=pltpu.VMEM)
SCALAR = pl.BlockSpec(memory_space=pltpu.SMEM)


def mark_kernel(negs_ref, source_ref, target_ref, out_ref):
    peers = out_ref.shape[0]
    ids = jnp.concatenate([source_ref[...], target_ref[...]], 1)
    count = ids.shape[1]
    owner = shift_down(ids, 5)
    within = lax.bitwise_and(ids, SENT - 1)
    row = iota((peers, count), 0)
    spot = iota((LANES, count), 0)
    marks = dot(bits(row == owner), bits(spot == within), 1, 1)
    marks = marks + dot(bits(row == mate_of(owner)), bits(spot == within + SENT), 1, 1)
    marks = jnp.where(marks > 0.0, 1.0, 0.0)
    lane = iota(marks.shape, 1)
    used = jnp.sum(jnp.where(lane < SENT, marks, 0.0), 1, keepdims=True)
    at_pair = lane == AT_COUNTS + pair_of(iota(marks.shape, 0))
    marks = marks + jnp.sum(jnp.where(at_pair, used, 0.0), 0, keepdims=True)
    for n in range(negs_ref.shape[0]):
        marks = jnp.where(lane == AT_NEGS + n, negs_ref[n].astype(F32), marks)
    out_ref[...] = marks


def neg_columns(marks, number):
    lane = iota(marks.shape, 1)
    columns = []
    for n in range(number):
        column = jnp.sum(jnp.where(lane == AT_NEGS + n, marks, 0.0), 1, keepdims=True)
        columns.append(jnp.broadcast_to(column.astype(jnp.int32), marks.shape))
    return columns


def before(count):
    return bits(iota((count, count), 1) < iota((count, count), 0))


def pack_kernel(
    number, me_ref, marks_ref, touched_ref, mate_touched_ref, table_ref, mate_table_ref,
    out_ref, rows_ref, flag_ref, onehot,
):
    marks = marks_ref[...]
    peers = marks.shape[0]
    lane = iota(marks.shape, 1)
    negs = neg_columns(marks, number)
    me = me_ref[0]

    at_pair = jnp.zeros(marks.shape, F32)
    at_owner = jnp.zeros(marks.shape, F32)
    for slot in negs:
        owner = shift_down(slot, 5)
        at_pair = at_pair + jnp.where(lane == AT_COUNTS + pair_of(owner), 1.0, 0.0)
        at_owner = at_owner + jnp.where(lane == owner, 1.0, 0.0)
    counts = marks + jnp.sum(at_pair, 0, keepdims=True)
    counts = jnp.where((lane >= AT_COUNTS) & (lane < AT_NEGS), counts, 0.0)
    over = (jnp.max(counts) > 2 * CAP) | (jnp.max(jnp.sum(at_owner, 0, keepdims=True)) > SENT)
    flag_ref[0] = over.astype(jnp.int32)

    def neg_rows(owner, touched):
        total = jnp.zeros((1, LANES), F32)
        rows = jnp.zeros((1, LANES), F32)
        for slot in negs:
            mine = shift_down(slot, 5) == owner
            row = jnp.sum(
                jnp.where(lane == lax.bitwise_and(slot, SENT - 1), touched, 0.0), 1, keepdims=True
            )
            rank = dot(before(peers), bits(mine)) + total
            total = total + jnp.sum(jnp.where(mine, 1.0, 0.0), 0, keepdims=True)
            here = mine & (lane == SENT + rank.astype(jnp.int32))
            rows = rows + jnp.sum(jnp.where(here, row + 1.0, 0.0), 0, keepdims=True)
        return rows

    owned = table_ref.shape[1]
    touched = touched_ref[...].astype(F32)
    mate_touched = mate_touched_ref[...].astype(F32)
    own_negs = jnp.broadcast_to(neg_rows(me, touched), marks.shape)
    mate_negs = jnp.broadcast_to(neg_rows(mate_of(me), mate_touched), marks.shape)
    mate_negs = pltpu.roll(mate_negs, 2 * SENT, 1)
    own = lane < 2 * SENT
    mask = jnp.where(
        lane < SENT,
        marks,
        jnp.where(
            own,
            jnp.where(own_negs > 0.0, 1.0, 0.0),
            jnp.where(
                lane < 3 * SENT,
                pltpu.roll(marks, SENT, 1),
                jnp.where(mate_negs > 0.0, 1.0, 0.0),
            ),
        ),
    )
    local = jnp.where(
        lane < SENT,
        touched + 1.0,
        jnp.where(
            own,
            own_negs,
            jnp.where(
                lane < 3 * SENT, pltpu.roll(mate_touched, 2 * SENT, 1) + 1.0, mate_negs
            )
            + owned,
        ),
    )
    first, second = iota((LANES, LANES), 0), iota((LANES, LANES), 1)
    same = (first < 2 * SENT) == (second < 2 * SENT)
    rank = dot(mask.astype(BF16), bits(same & (first <= second)))
    number_own = jnp.sum(jnp.where(own, mask, 0.0), 1, keepdims=True)
    place = jnp.where(
        own,
        jnp.where(rank <= CAP, rank - 1.0, -1.0),
        jnp.where(rank > CAP, number_own + rank - (CAP + 1.0), -1.0),
    )
    place = jnp.where(mask > 0.0, place, -1.0)
    spot = iota((peers, 2 * owned), 1)
    rows = jnp.full(marks.shape, -1, jnp.int32)
    for k in range(CAP):
        row = jnp.sum(jnp.where(place == k, local, 0.0), 1, keepdims=True).astype(jnp.int32) - 1
        rows = jnp.where(lane == k, row, rows)
        onehot[k * peers : (k + 1) * peers, :] = bits(spot == row)
    rows_ref[...] = rows

    main = PARTS * LANES
    table = jnp.concatenate([table_ref[...], mate_table_ref[...]], 1)
    wide = jnp.concatenate([table[:main]] + [table[main:]] * PER_LINE, 0)
    wide = pieces(wide, 3)
    group = lane // TAIL
    for part in range(PARTS):
        first = part * PER_LINE
        last = min(first + PER_LINE, CAP)
        chosen = onehot[first * peers : last * peers, :]
        got = dot(chosen, wide[2], 1, 1) + dot(chosen, wide[1], 1, 1)
        got = got + dot(chosen, wide[0], 1, 1)
        line = jnp.zeros(marks.shape, F32)
        for k in range(first, last):
            mine = got[(k - first) * peers : (k - first + 1) * peers]
            for t in range(PARTS):
                out_ref[pl.ds(line_of(t, k), peers, stride=BLOCK), :] = mine[
                    :, t * LANES : (t + 1) * LANES
                ]
            line = line + jnp.where(group == k - first, mine[:, main:], 0.0)
        out_ref[pl.ds(LINES + part, peers, stride=BLOCK), :] = line
    for spare in range(LINES + PARTS, BLOCK):
        out_ref[pl.ds(spare, peers, stride=BLOCK), :] = jnp.zeros(marks.shape, F32)


def place_kernel(number, marks_ref, source_ref, target_ref, edge_ref, neg_ref):
    marks = marks_ref[...]
    peers = marks.shape[0]
    ids = jnp.concatenate([source_ref[...], target_ref[...]], 1)
    count = ids.shape[1]
    owner = shift_down(ids, 5)
    at_owner = bits(iota((LANES, count), 0) == owner)
    at_within = bits(iota((SENT, count), 0) == lax.bitwise_and(ids, SENT - 1))
    used = bits(dot(at_within, at_owner, 1, 1) > 0.0)
    upto = bits(iota((SENT, SENT), 1) <= iota((SENT, SENT), 0))
    rank = dot(upto, used)
    from_edges = rank[SENT - 1 :]
    lane = iota(marks.shape, 1)
    negs = [shift_down(slot, 5) for slot in neg_columns(marks, number)]
    at_neg = [jnp.where(lane == slot, 1.0, 0.0) for slot in negs]
    total = from_edges
    for at in at_neg:
        total = total + jnp.sum(at, 0, keepdims=True)
    first, second = iota((LANES, LANES), 0), iota((LANES, LANES), 1)
    swap = bits(first == mate_of(second))
    total = jnp.broadcast_to(total, (PER_LINE, LANES)).astype(BF16)
    mates = dot(total, swap)

    def placed(owner, order, mate):
        own = owner * REGION + order
        return jnp.where(order < CAP, own, mate_of(owner) * REGION + mate + order - CAP)

    order = jnp.sum(dot(rank.astype(BF16), at_owner) * at_within.astype(F32), 0, keepdims=True)
    mate = dot(mates.astype(BF16), at_owner)[:1]
    edge_ref[...] = placed(owner, order.astype(jnp.int32) - 1, mate.astype(jnp.int32))
    earlier = from_edges
    for n, at in enumerate(at_neg):
        order = dot(before(peers), at.astype(BF16)) + earlier
        order = jnp.sum(order * at, 1, keepdims=True)
        mate = jnp.sum(mates[:1] * at, 1, keepdims=True)
        at_place = placed(negs[n][:, :1], order.astype(jnp.int32), mate.astype(jnp.int32))
        neg_ref[n * peers : (n + 1) * peers, :] = at_place
        earlier = earlier + jnp.sum(at, 0, keepdims=True)


def unpack(ref):
    peers = ref.shape[0]
    count = peers * REGION
    ends = ref[:, EXTRA : EXTRA + PER_LINE, :], ref[:, EXTRA + PER_LINE :, :]
    rest = ends[0], pltpu.roll(ends[0], PER_LINE // 2, 1), ends[1]
    parts = []
    for t in range(PARTS):
        part = jnp.concatenate([ref[:, t * HEAD : (t + 1) * HEAD, :], rest[t]], 1)
        parts.append(part.reshape(count, LANES))
    at = LINES - EXTRA - PER_LINE
    tails = [
        jnp.broadcast_to(ends[1][:, at + t : at + t + 1, :], (peers, PER_LINE, LANES))
        for t in range(PARTS)
    ]
    tails = jnp.concatenate(tails, 1)
    own = iota(tails.shape, 2) // TAIL == iota(tails.shape, 1) % PER_LINE
    parts.append(jnp.where(own, tails, 0.0).reshape(count, LANES))
    both = [pieces(part, 2) for part in parts]
    return jnp.concatenate([p[0] for p in both], 1), jnp.concatenate([p[1] for p in both], 1)


def edges_kernel(
    block_ref, place_ref, neg_place_ref, row_place_ref, rel_hi_ref, rel_lo_ref,
    out_ref, slots_hi, slots_lo, grad_hi, grad_lo,
):
    peers = block_ref.shape[0]
    edges = place_ref.shape[0] // 2
    total = neg_place_ref.shape[0]
    kinds = rel_hi_ref.shape[0]
    per_rel = edges // kinds
    count = peers * REGION
    main = PARTS * LANES
    slots_hi[...], slots_lo[...] = unpack(block_ref)

    def rows_at(spot):
        chosen = bits(iota((spot.shape[0], count), 1) == spot)
        got = dot(chosen, slots_lo[...]) + dot(chosen, slots_hi[...])
        return jnp.concatenate([got[:, :main], spread(got[:, main:])], 1)

    def keep(start, grad):
        grad = jnp.concatenate([grad[:, :main], spread(grad[:, main:])], 1)
        hi, lo = pieces(grad, 2)
        grad_hi[start : start + grad.shape[0], :] = hi
        grad_lo[start : start + grad.shape[0], :] = lo

    negs = tuple(pieces(rows_at(neg_place_ref[...]), 2))
    shares = jnp.zeros((total, WIDE), F32)
    for kind in range(kinds):
        start = kind * per_rel
        relation = rel_hi_ref[kind], rel_lo_ref[kind]
        query = dot3(rows_at(place_ref[start : start + per_rel, :]), relation)
        tail = rows_at(place_ref[edges + start : edges + start + per_rel, :])
        positive = jnp.sum(query * tail, 1, keepdims=True)
        grad_pos = jax.nn.sigmoid(positive) - 1.0
        keep(edges + start, grad_pos * query)
        query = tuple(pieces(query, 2))
        grad_neg = jax.nn.sigmoid(dot3(query, negs, 1, 1)) / total
        grad_query = grad_pos * tail + dot3(grad_neg, negs)
        keep(start, dot3(grad_query, relation, 1, 1))
        grad_neg = jax.nn.sigmoid(dot3(negs, query, 1, 1)) / total
        shares = shares + dot3(grad_neg, query)
    keep(2 * edges, shares)

    spot = row_place_ref[...]
    half = peers // 2
    count = half * REGION
    for first in (0, half):
        chosen = bits(iota((count, spot.shape[1]), 0) + first * REGION == spot)
        got = dot(chosen, grad_lo[...]) + dot(chosen, grad_hi[...])
        span = slice(first, first + half)
        rest = []
        for t in range(PARTS):
            part = got[:, t * LANES : (t + 1) * LANES].reshape(half, REGION, LANES)
            out_ref[span, t * HEAD : (t + 1) * HEAD, :] = part[:, :HEAD]
            rest.append(part[:, HEAD:])
        out_ref[span, EXTRA : EXTRA + PER_LINE, :] = rest[0] + pltpu.roll(rest[1], PER_LINE // 2, 1)
        last = rest[2]
        line = got[:, main:].reshape(half, REGION, LANES)
        own = iota(line.shape, 2) // TAIL == iota(line.shape, 1) % PER_LINE
        line = jnp.where(own, line, 0.0)
        at = LINES - EXTRA - PER_LINE
        for t in range(PARTS):
            mine = jnp.sum(line[:, t * PER_LINE : (t + 1) * PER_LINE], 1, keepdims=True)
            here = iota(last.shape, 1) == at + t
            last = jnp.where(here, jnp.broadcast_to(mine, last.shape), last)
        out_ref[span, EXTRA + PER_LINE :, :] = last


def sum_kernel(first, block_ref, rows_ref, out_ref):
    width, owned = out_ref.shape
    main = PARTS * LANES
    hi, lo = unpack(block_ref)
    count = hi.shape[0]
    chosen = bits(iota((owned, count), 0) + first == rows_ref[...])
    got = dot(chosen, lo) + dot(chosen, hi)
    grad = jnp.concatenate([got[:, :main], spread(got[:, main:])], 1)
    out_ref[...] = grad.T[:width]


def update_kernel(own_ref, mate_ref, table_ref, state_ref, new_table_ref, new_state_ref):
    width = table_ref.shape[0]
    grad = own_ref[...] + mate_ref[...]
    state = state_ref[...] + jnp.sum(grad * grad, 0, keepdims=True) / width
    new_state_ref[...] = state
    new_table_ref[...] = table_ref[...] - LEARN_RATE * grad / (jnp.sqrt(state) + EPSILON)


def swap_mates(x):
    peers = lax.axis_size("grp")
    return lax.ppermute(x, "grp", [(p, p ^ MATE) for p in range(peers)])


def compact_path(marks, blocks, rows, source, target, number, rel_hi, rel_lo, table, state):
    peers = marks.shape[0]
    edges = source.shape[1]
    width, owned = table.shape
    blocks = exchange(blocks.reshape(peers, BLOCK, LANES))
    edge_place, neg_place = call(
        functools.partial(place_kernel, number),
        (shaped(1, 2 * edges, dtype=jnp.int32), shaped(peers * number, 1, dtype=jnp.int32)),
    )(marks, source, target)
    row_place = jnp.concatenate([edge_place, neg_place.reshape(1, -1)], 1)
    grads = call(
        edges_kernel,
        shaped(peers, BLOCK, LANES),
        scratch_shapes=[
            pltpu.VMEM((peers * REGION, WIDE), BF16),
            pltpu.VMEM((peers * REGION, WIDE), BF16),
            pltpu.VMEM((row_place.shape[1], WIDE), BF16),
            pltpu.VMEM((row_place.shape[1], WIDE), BF16),
        ],
    )(blocks, edge_place.reshape(-1, 1), neg_place, row_place, rel_hi, rel_lo)
    returned = exchange(grads)
    rows = rows[:, :REGION].reshape(1, -1)
    for_mate = call(functools.partial(sum_kernel, owned), shaped(width, owned))(returned, rows)
    from_mate = swap_mates(for_mate)
    own = call(functools.partial(sum_kernel, 0), shaped(width, owned))(returned, rows)
    return call(
        update_kernel,
        (shaped(width, owned), shaped(1, owned)),
    )(own, from_mate, table, state)


def per_device(table, row_state, relations, touched, source, target, neg_slots):
    peers, sent = touched.shape
    owned, width = table.shape
    number = neg_slots.shape[0]
    across = table.T
    mate_table = swap_mates(across)
    wide_touched = jnp.pad(touched, ((0, 0), (0, LANES - sent)))
    mate_touched = swap_mates(wide_touched)
    source_row, target_row = source.reshape(1, -1), target.reshape(1, -1)
    marks = call(
        mark_kernel, shaped(peers, LANES), in_specs=[SCALAR, VECTOR, VECTOR], out_specs=VECTOR
    )(neg_slots, source_row, target_row)
    marks = exchange(marks.reshape(peers, 1, LANES)).reshape(peers, LANES)
    wide = jnp.pad(relations, ((0, 0), (0, WIDE - width), (0, WIDE - width)))
    rel_hi = lax.reduce_precision(wide, 8, 7)
    rel_lo = (wide - rel_hi).astype(BF16)
    rel_hi = rel_hi.astype(BF16)
    blocks, rows, crowded = call(
        functools.partial(pack_kernel, number),
        (
            shaped(peers * BLOCK, LANES),
            shaped(peers, LANES, dtype=jnp.int32),
            shaped(1, dtype=jnp.int32),
        ),
        in_specs=[SCALAR] + [VECTOR] * 5,
        out_specs=(VECTOR, VECTOR, SCALAR),
        scratch_shapes=[pltpu.VMEM((CAP * peers, 2 * owned), BF16)],
    )(lax.axis_index("grp").reshape(1), marks, wide_touched, mate_touched, across, mate_table)
    new_table, new_state = lax.cond(
        crowded[0] > 0,
        lambda: full_path(table, row_state, relations, touched, source, target, neg_slots),
        lambda: compact_path(
            marks, blocks, rows, source_row, target_row, number, rel_hi, rel_lo, across,
            row_state.reshape(1, -1),
        ),
    )
    return new_table.T, new_state.reshape(-1)


def solution(mesh):
    return jax.shard_map(
        per_device,
        mesh=mesh,
        in_specs=(
            P(("grp", "rep"), None),
            P(("grp", "rep")),
            P(),
            P(("grp", "rep"), None),
            P(("grp", "rep")),
            P(("grp", "rep")),
            P(("grp", "rep")),
        ),
        out_specs=(P(("grp", "rep"), None), P(("grp", "rep"))),
        check_vma=False,
    )
```

```python
import functools

import jax
import jax.numpy as jnp
from jax import lax
from jax.experimental import pallas as pl
from jax.experimental.pallas import tpu as pltpu
from jax.sharding import PartitionSpec as P

PRECISE = lax.Precision.HIGHEST
LEARN_RATE = 0.1
EPSILON = 1e-06
LANES = 128
VMEM = 56 * 1024 * 1024
F32 = jnp.float32
BF16 = jnp.bfloat16


def exchange(blocks):
    return lax.all_to_all(blocks, "grp", split_axis=0, concat_axis=0, tiled=True)


def take_rows(rows, ids):
    return jnp.take(rows, ids, axis=0, mode="clip")


def to_lanes(rows, peers):
    width = rows.shape[1]
    wide = -(-width // LANES) * LANES
    return jnp.pad(rows, ((0, 0), (0, wide - width))).reshape(peers, -1, LANES)


def full_path(table, row_state, relations, touched, source, target, neg_slots):
    width = table.shape[1]
    peers, sent = touched.shape
    kinds = relations.shape[0]
    per_rel = source.shape[0] // kinds
    slot_count = peers * sent
    own_count = neg_slots.shape[0]
    neg_total = peers * own_count
    outgoing = take_rows(table, touched.reshape(-1))
    slots = exchange(outgoing.reshape(peers, -1, LANES)).reshape(slot_count, width)
    own_neg = to_lanes(take_rows(slots, neg_slots), 1)
    gathered = exchange(jnp.broadcast_to(own_neg, (peers,) + own_neg.shape[1:]))
    negatives = gathered.reshape(neg_total, -1)[:, :width]
    head = take_rows(slots, source)
    tail = take_rows(slots, target)
    query = jnp.einsum(
        "ked,kdf->kef", head.reshape(kinds, per_rel, width), relations, precision=PRECISE
    ).reshape(kinds * per_rel, width)
    positive = jnp.sum(query * tail, -1)
    negative = jnp.dot(query, negatives.T, precision=PRECISE)
    grad_pos = jax.nn.sigmoid(positive) - 1.0
    grad_neg = jax.nn.sigmoid(negative) / neg_total
    grad_negs = jnp.dot(grad_neg.T, query, precision=PRECISE)
    shares = exchange(to_lanes(grad_negs, peers))
    mine = jnp.sum(shares, 0).reshape(own_count, -1)[:, :width]
    grad_query = grad_pos[:, None] * tail + jnp.dot(grad_neg, negatives, precision=PRECISE)
    grad_tail = grad_pos[:, None] * query
    grad_head = jnp.einsum(
        "kef,kdf->ked", grad_query.reshape(kinds, per_rel, width), relations, precision=PRECISE
    ).reshape(kinds * per_rel, width)
    slot_grad = jnp.zeros((slot_count, width), F32).at[source].add(grad_head)
    slot_grad = slot_grad.at[target].add(grad_tail)
    slot_grad = slot_grad.at[neg_slots].add(mine)
    returned = exchange(slot_grad.reshape(peers, -1, LANES)).reshape(slot_count, width)
    row_grad = jnp.zeros(table.shape, F32).at[touched.reshape(-1)].add(returned)
    new_state = row_state + jnp.mean(row_grad * row_grad, -1)
    new_table = table - LEARN_RATE * row_grad / (jnp.sqrt(new_state)[:, None] + EPSILON)
    return new_table.T, new_state.reshape(1, -1)


CAP = 22
PARTS = 3
TAIL = 16
PER_LINE = LANES // TAIL
LINES = PARTS * CAP
BLOCK = LINES + -(-CAP // PER_LINE)
WIDE = (PARTS + 1) * LANES
MATE = 16
SENT = 32
AT_COUNTS = 2 * SENT
AT_NEGS = 3 * SENT


def iota(shape, dim):
    return lax.broadcasted_iota(jnp.int32, shape, dim)


def bits(mask):
    return jnp.where(mask, 1.0, 0.0).astype(BF16)


def shift_down(x, by):
    return lax.shift_right_logical(x, jnp.full(x.shape, by, x.dtype))


def pair_of(owner):
    return shift_down(owner, 5) * MATE + lax.bitwise_and(owner, MATE - 1)


def mate_of(owner):
    return lax.bitwise_xor(owner, MATE)


def pieces(x, count):
    out = []
    for _ in range(count):
        piece = x.astype(BF16)
        out.append(piece)
        x = x - piece.astype(F32)
    return out


def dot(a, b, a_dim=1, b_dim=0):
    return lax.dot_general(a, b, (((a_dim,), (b_dim,)), ((), ())), preferred_element_type=F32)


def dot3(a, b, a_dim=1, b_dim=0):
    a_hi, a_lo = a if isinstance(a, tuple) else pieces(a, 2)
    b_hi, b_lo = b if isinstance(b, tuple) else pieces(b, 2)
    small = dot(a_lo, b_hi, a_dim, b_dim) + dot(a_hi, b_lo, a_dim, b_dim)
    return small + dot(a_hi, b_hi, a_dim, b_dim)


def spread(x):
    step = TAIL
    while step < LANES:
        x = x + pltpu.roll(x, step, 1)
        step *= 2
    return x


def call(kernel, outs, **kw):
    return pl.pallas_call(
        kernel,
        out_shape=outs,
        compiler_params=pltpu.CompilerParams(vmem_limit_bytes=VMEM),
        **kw,
    )


def shaped(*shape, dtype=F32):
    return jax.ShapeDtypeStruct(shape, dtype)


VECTOR = pl.BlockSpec(memory_space=pltpu.VMEM)
SCALAR = pl.BlockSpec(memory_space=pltpu.SMEM)


def mark_kernel(negs_ref, source_ref, target_ref, out_ref):
    peers = out_ref.shape[0]
    ids = jnp.concatenate([source_ref[...], target_ref[...]], 1)
    count = ids.shape[1]
    owner = shift_down(ids, 5)
    within = lax.bitwise_and(ids, SENT - 1)
    row = iota((peers, count), 0)
    spot = iota((LANES, count), 0)
    marks = dot(bits(row == owner), bits(spot == within), 1, 1)
    marks = marks + dot(bits(row == mate_of(owner)), bits(spot == within + SENT), 1, 1)
    marks = jnp.where(marks > 0.0, 1.0, 0.0)
    lane = iota(marks.shape, 1)
    used = jnp.sum(jnp.where(lane < SENT, marks, 0.0), 1, keepdims=True)
    at_pair = lane == AT_COUNTS + pair_of(iota(marks.shape, 0))
    marks = marks + jnp.sum(jnp.where(at_pair, used, 0.0), 0, keepdims=True)
    for n in range(negs_ref.shape[0]):
        marks = jnp.where(lane == AT_NEGS + n, negs_ref[n].astype(F32), marks)
    out_ref[...] = marks


def neg_columns(marks, number):
    lane = iota(marks.shape, 1)
    columns = []
    for n in range(number):
        column = jnp.sum(jnp.where(lane == AT_NEGS + n, marks, 0.0), 1, keepdims=True)
        columns.append(jnp.broadcast_to(column.astype(jnp.int32), marks.shape))
    return columns


def before(count):
    return bits(iota((count, count), 1) < iota((count, count), 0))


def pack_kernel(
    number, me_ref, marks_ref, touched_ref, mate_touched_ref, table_ref, mate_table_ref,
    out_ref, rows_ref, flag_ref, onehot,
):
    marks = marks_ref[...]
    peers = marks.shape[0]
    lane = iota(marks.shape, 1)
    negs = neg_columns(marks, number)
    me = me_ref[0]

    at_pair = jnp.zeros(marks.shape, F32)
    at_owner = jnp.zeros(marks.shape, F32)
    for slot in negs:
        owner = shift_down(slot, 5)
        at_pair = at_pair + jnp.where(lane == AT_COUNTS + pair_of(owner), 1.0, 0.0)
        at_owner = at_owner + jnp.where(lane == owner, 1.0, 0.0)
    counts = marks + jnp.sum(at_pair, 0, keepdims=True)
    counts = jnp.where((lane >= AT_COUNTS) & (lane < AT_NEGS), counts, 0.0)
    over = (jnp.max(counts) > 2 * CAP) | (jnp.max(jnp.sum(at_owner, 0, keepdims=True)) > SENT)
    flag_ref[0] = over.astype(jnp.int32)

    def neg_rows(owner, touched):
        total = jnp.zeros((1, LANES), F32)
        rows = jnp.zeros((1, LANES), F32)
        for slot in negs:
            mine = shift_down(slot, 5) == owner
            row = jnp.sum(
                jnp.where(lane == lax.bitwise_and(slot, SENT - 1), touched, 0.0), 1, keepdims=True
            )
            rank = dot(before(peers), bits(mine)) + total
            total = total + jnp.sum(jnp.where(mine, 1.0, 0.0), 0, keepdims=True)
            here = mine & (lane == SENT + rank.astype(jnp.int32))
            rows = rows + jnp.sum(jnp.where(here, row + 1.0, 0.0), 0, keepdims=True)
        return rows

    owned = table_ref.shape[1]
    touched = touched_ref[...].astype(F32)
    mate_touched = mate_touched_ref[...].astype(F32)
    own_negs = jnp.broadcast_to(neg_rows(me, touched), marks.shape)
    mate_negs = jnp.broadcast_to(neg_rows(mate_of(me), mate_touched), marks.shape)
    mate_negs = pltpu.roll(mate_negs, 2 * SENT, 1)
    own = lane < 2 * SENT
    mask = jnp.where(
        lane < SENT,
        marks,
        jnp.where(
            own,
            jnp.where(own_negs > 0.0, 1.0, 0.0),
            jnp.where(
                lane < 3 * SENT,
                pltpu.roll(marks, SENT, 1),
                jnp.where(mate_negs > 0.0, 1.0, 0.0),
            ),
        ),
    )
    local = jnp.where(
        lane < SENT,
        touched + 1.0,
        jnp.where(
            own,
            own_negs,
            jnp.where(
                lane < 3 * SENT, pltpu.roll(mate_touched, 2 * SENT, 1) + 1.0, mate_negs
            )
            + owned,
        ),
    )
    first, second = iota((LANES, LANES), 0), iota((LANES, LANES), 1)
    same = (first < 2 * SENT) == (second < 2 * SENT)
    rank = dot(mask.astype(BF16), bits(same & (first <= second)))
    number_own = jnp.sum(jnp.where(own, mask, 0.0), 1, keepdims=True)
    place = jnp.where(
        own,
        jnp.where(rank <= CAP, rank - 1.0, -1.0),
        jnp.where(rank > CAP, number_own + rank - (CAP + 1.0), -1.0),
    )
    place = jnp.where(mask > 0.0, place, -1.0)
    spot = iota((peers, 2 * owned), 1)
    rows = jnp.full(marks.shape, -1, jnp.int32)
    for k in range(CAP):
        row = jnp.sum(jnp.where(place == k, local, 0.0), 1, keepdims=True).astype(jnp.int32) - 1
        rows = jnp.where(lane == k, row, rows)
        onehot[k * peers : (k + 1) * peers, :] = bits(spot == row)
    rows_ref[...] = rows

    main = PARTS * LANES
    table = jnp.concatenate([table_ref[...], mate_table_ref[...]], 1)
    wide = jnp.concatenate([table[:main]] + [table[main:]] * PER_LINE, 0)
    wide = pieces(wide, 2)
    group = lane // TAIL
    for part in range(BLOCK - LINES):
        first = part * PER_LINE
        last = min(first + PER_LINE, CAP)
        chosen = onehot[first * peers : last * peers, :]
        got = dot(chosen, wide[1], 1, 1) + dot(chosen, wide[0], 1, 1)
        line = jnp.zeros(marks.shape, F32)
        for k in range(first, last):
            mine = got[(k - first) * peers : (k - first + 1) * peers]
            for t in range(PARTS):
                out_ref[pl.ds(t * CAP + k, peers, stride=BLOCK), :] = mine[
                    :, t * LANES : (t + 1) * LANES
                ]
            line = line + jnp.where(group == k - first, mine[:, main:], 0.0)
        out_ref[pl.ds(LINES + part, peers, stride=BLOCK), :] = line


def place_kernel(number, marks_ref, source_ref, target_ref, edge_ref, neg_ref):
    marks = marks_ref[...]
    peers = marks.shape[0]
    ids = jnp.concatenate([source_ref[...], target_ref[...]], 1)
    count = ids.shape[1]
    owner = shift_down(ids, 5)
    at_owner = bits(iota((LANES, count), 0) == owner)
    at_within = bits(iota((SENT, count), 0) == lax.bitwise_and(ids, SENT - 1))
    used = bits(dot(at_within, at_owner, 1, 1) > 0.0)
    upto = bits(iota((SENT, SENT), 1) <= iota((SENT, SENT), 0))
    rank = dot(upto, used)
    from_edges = rank[SENT - 1 :]
    lane = iota(marks.shape, 1)
    negs = [shift_down(slot, 5) for slot in neg_columns(marks, number)]
    at_neg = [jnp.where(lane == slot, 1.0, 0.0) for slot in negs]
    total = from_edges
    for at in at_neg:
        total = total + jnp.sum(at, 0, keepdims=True)
    first, second = iota((LANES, LANES), 0), iota((LANES, LANES), 1)
    swap = bits(first == mate_of(second))
    total = jnp.broadcast_to(total, (PER_LINE, LANES)).astype(BF16)
    mates = dot(total, swap)

    def placed(owner, order, mate):
        at_mate = (mate + order - CAP) * peers + mate_of(owner)
        return jnp.where(order < CAP, order * peers + owner, at_mate)

    order = jnp.sum(dot(rank.astype(BF16), at_owner) * at_within.astype(F32), 0, keepdims=True)
    mate = dot(mates.astype(BF16), at_owner)[:1]
    edge_ref[...] = placed(owner, order.astype(jnp.int32) - 1, mate.astype(jnp.int32))
    earlier = from_edges
    for n, at in enumerate(at_neg):
        order = dot(before(peers), at.astype(BF16)) + earlier
        order = jnp.sum(order * at, 1, keepdims=True)
        mate = jnp.sum(mates[:1] * at, 1, keepdims=True)
        at_place = placed(negs[n][:, :1], order.astype(jnp.int32), mate.astype(jnp.int32))
        neg_ref[n * peers : (n + 1) * peers, :] = at_place
        earlier = earlier + jnp.sum(at, 0, keepdims=True)


def unpack(ref, hi_ref, lo_ref):
    peers = ref.shape[0] // BLOCK
    group = iota((peers, LANES), 1) // TAIL
    for k in range(CAP):
        tails = ref[pl.ds(LINES + k // PER_LINE, peers, stride=BLOCK), :]
        parts = [ref[pl.ds(t * CAP + k, peers, stride=BLOCK), :] for t in range(PARTS)]
        parts.append(jnp.where(group == k % PER_LINE, tails, 0.0))
        for t, part in enumerate(parts):
            hi, lo = pieces(part, 2)
            hi_ref[k * peers : (k + 1) * peers, t * LANES : (t + 1) * LANES] = hi
            lo_ref[k * peers : (k + 1) * peers, t * LANES : (t + 1) * LANES] = lo


def edges_kernel(
    block_ref, place_ref, neg_place_ref, row_place_ref, rel_hi_ref, rel_lo_ref,
    out_ref, slots_hi, slots_lo, grad_hi, grad_lo,
):
    peers = block_ref.shape[0] // BLOCK
    edges = place_ref.shape[0] // 2
    total = neg_place_ref.shape[0]
    kinds = rel_hi_ref.shape[0]
    per_rel = edges // kinds
    count = peers * CAP
    main = PARTS * LANES
    unpack(block_ref, slots_hi, slots_lo)

    def rows_at(spot):
        chosen = bits(iota((spot.shape[0], count), 1) == spot)
        got = dot(chosen, slots_lo[...]) + dot(chosen, slots_hi[...])
        return jnp.concatenate([got[:, :main], spread(got[:, main:])], 1)

    def keep(start, grad):
        grad = jnp.concatenate([grad[:, :main], spread(grad[:, main:])], 1)
        hi, lo = pieces(grad, 2)
        grad_hi[start : start + grad.shape[0], :] = hi
        grad_lo[start : start + grad.shape[0], :] = lo

    negs = tuple(pieces(rows_at(neg_place_ref[...]), 2))
    shares = jnp.zeros((total, WIDE), F32)
    for kind in range(kinds):
        start = kind * per_rel
        relation = rel_hi_ref[kind], rel_lo_ref[kind]
        query = dot3(rows_at(place_ref[start : start + per_rel, :]), relation)
        tail = rows_at(place_ref[edges + start : edges + start + per_rel, :])
        positive = jnp.sum(query * tail, 1, keepdims=True)
        grad_pos = jax.nn.sigmoid(positive) - 1.0
        keep(edges + start, grad_pos * query)
        query = tuple(pieces(query, 2))
        grad_neg = jax.nn.sigmoid(dot3(query, negs, 1, 1)) / total
        grad_query = grad_pos * tail + dot3(grad_neg, negs)
        keep(start, dot3(grad_query, relation, 1, 1))
        grad_neg = jax.nn.sigmoid(dot3(negs, query, 1, 1)) / total
        shares = shares + dot3(grad_neg, query)
    keep(2 * edges, shares)

    spot = row_place_ref[...]
    group = iota((peers, LANES), 1) // TAIL
    for part in range(BLOCK - LINES):
        first = part * PER_LINE
        last = min(first + PER_LINE, CAP)
        chosen = iota(((last - first) * peers, spot.shape[1]), 0) + first * peers
        chosen = bits(chosen == spot)
        got = dot(chosen, grad_lo[...]) + dot(chosen, grad_hi[...])
        line = jnp.zeros((peers, LANES), F32)
        for k in range(first, last):
            mine = got[(k - first) * peers : (k - first + 1) * peers]
            for t in range(PARTS):
                out_ref[pl.ds(t * CAP + k, peers, stride=BLOCK), :] = mine[
                    :, t * LANES : (t + 1) * LANES
                ]
            line = line + jnp.where(group == k - first, mine[:, main:], 0.0)
        out_ref[pl.ds(LINES + part, peers, stride=BLOCK), :] = line


def sum_kernel(first, block_ref, rows_ref, out_ref, hi_ref, lo_ref):
    width, owned = out_ref.shape
    main = PARTS * LANES
    unpack(block_ref, hi_ref, lo_ref)
    chosen = bits(iota((owned, hi_ref.shape[0]), 0) + first == rows_ref[...])
    got = dot(chosen, lo_ref[...]) + dot(chosen, hi_ref[...])
    grad = jnp.concatenate([got[:, :main], spread(got[:, main:])], 1)
    out_ref[...] = grad.T[:width]


def update_kernel(own_ref, mate_ref, table_ref, state_ref, new_table_ref, new_state_ref):
    width = table_ref.shape[0]
    grad = own_ref[...] + mate_ref[...]
    state = state_ref[...] + jnp.sum(grad * grad, 0, keepdims=True) / width
    new_state_ref[...] = state
    new_table_ref[...] = table_ref[...] - LEARN_RATE * grad / (jnp.sqrt(state) + EPSILON)


def swap_mates(x):
    peers = lax.axis_size("grp")
    return lax.ppermute(x, "grp", [(p, p ^ MATE) for p in range(peers)])


def exchange_blocks(blocks):
    peers = lax.axis_size("grp")
    return exchange(blocks.reshape(peers, BLOCK, 1, LANES)).reshape(blocks.shape)


def compact_path(marks, blocks, rows, source, target, number, rel_hi, rel_lo, table, state):
    peers = marks.shape[0]
    edges = source.shape[1]
    width, owned = table.shape
    count = peers * CAP
    split = [pltpu.VMEM((count, WIDE), BF16)] * 2
    blocks = exchange_blocks(blocks)
    edge_place, neg_place = call(
        functools.partial(place_kernel, number),
        (shaped(1, 2 * edges, dtype=jnp.int32), shaped(peers * number, 1, dtype=jnp.int32)),
    )(marks, source, target)
    row_place = jnp.concatenate([edge_place, neg_place.reshape(1, -1)], 1)
    grads = call(
        edges_kernel,
        shaped(*blocks.shape),
        scratch_shapes=split + [pltpu.VMEM((row_place.shape[1], WIDE), BF16)] * 2,
    )(blocks, edge_place.reshape(-1, 1), neg_place, row_place, rel_hi, rel_lo)
    returned = exchange_blocks(grads)
    rows = rows[:, :CAP].T.reshape(1, -1)

    def summed(first):
        kernel = functools.partial(sum_kernel, first)
        return call(kernel, shaped(width, owned), scratch_shapes=split)(returned, rows)

    from_mate = swap_mates(summed(owned))
    return call(
        update_kernel,
        (shaped(width, owned), shaped(1, owned)),
    )(summed(0), from_mate, table, state)


def per_device(table, row_state, relations, touched, source, target, neg_slots):
    peers, sent = touched.shape
    owned, width = table.shape
    number = neg_slots.shape[0]
    across = table.T
    mate_table = swap_mates(across)
    wide_touched = jnp.pad(touched, ((0, 0), (0, LANES - sent)))
    mate_touched = swap_mates(wide_touched)
    source_row, target_row = source.reshape(1, -1), target.reshape(1, -1)
    marks = call(
        mark_kernel, shaped(peers, LANES), in_specs=[SCALAR, VECTOR, VECTOR], out_specs=VECTOR
    )(neg_slots, source_row, target_row)
    marks = exchange(marks.reshape(peers, 1, LANES)).reshape(peers, LANES)
    wide = jnp.pad(relations, ((0, 0), (0, WIDE - width), (0, WIDE - width)))
    rel_hi = lax.reduce_precision(wide, 8, 7)
    rel_lo = (wide - rel_hi).astype(BF16)
    rel_hi = rel_hi.astype(BF16)
    blocks, rows, crowded = call(
        functools.partial(pack_kernel, number),
        (
            shaped(peers * BLOCK, LANES),
            shaped(peers, LANES, dtype=jnp.int32),
            shaped(1, dtype=jnp.int32),
        ),
        in_specs=[SCALAR] + [VECTOR] * 5,
        out_specs=(VECTOR, VECTOR, SCALAR),
        scratch_shapes=[pltpu.VMEM((CAP * peers, 2 * owned), BF16)],
    )(lax.axis_index("grp").reshape(1), marks, wide_touched, mate_touched, across, mate_table)
    new_table, new_state = lax.cond(
        crowded[0] > 0,
        lambda: full_path(table, row_state, relations, touched, source, target, neg_slots),
        lambda: compact_path(
            marks, blocks, rows, source_row, target_row, number, rel_hi, rel_lo, across,
            row_state.reshape(1, -1),
        ),
    )
    return new_table.T, new_state.reshape(-1)


def solution(mesh):
    return jax.shard_map(
        per_device,
        mesh=mesh,
        in_specs=(
            P(("grp", "rep"), None),
            P(("grp", "rep")),
            P(),
            P(("grp", "rep"), None),
            P(("grp", "rep")),
            P(("grp", "rep")),
            P(("grp", "rep")),
        ),
        out_specs=(P(("grp", "rep"), None), P(("grp", "rep"))),
        check_vma=False,
    )
```

```python
import functools

import jax
import jax.numpy as jnp
from jax import lax
from jax.experimental import pallas as pl
from jax.experimental.pallas import tpu as pltpu
from jax.sharding import PartitionSpec as P

PRECISE = lax.Precision.HIGHEST
LEARN_RATE = 0.1
EPSILON = 1e-06
LANES = 128
VMEM = 56 * 1024 * 1024
F32 = jnp.float32
BF16 = jnp.bfloat16


def exchange(blocks):
    return lax.all_to_all(blocks, "grp", split_axis=0, concat_axis=0, tiled=True)


def take_rows(rows, ids):
    return jnp.take(rows, ids, axis=0, mode="clip")


def to_lanes(rows, peers):
    width = rows.shape[1]
    wide = -(-width // LANES) * LANES
    return jnp.pad(rows, ((0, 0), (0, wide - width))).reshape(peers, -1, LANES)


def full_path(table, row_state, relations, touched, source, target, neg_slots):
    width = table.shape[1]
    peers, sent = touched.shape
    kinds = relations.shape[0]
    per_rel = source.shape[0] // kinds
    slot_count = peers * sent
    own_count = neg_slots.shape[0]
    neg_total = peers * own_count
    outgoing = take_rows(table, touched.reshape(-1))
    slots = exchange(outgoing.reshape(peers, -1, LANES)).reshape(slot_count, width)
    own_neg = to_lanes(take_rows(slots, neg_slots), 1)
    gathered = exchange(jnp.broadcast_to(own_neg, (peers,) + own_neg.shape[1:]))
    negatives = gathered.reshape(neg_total, -1)[:, :width]
    head = take_rows(slots, source)
    tail = take_rows(slots, target)
    query = jnp.einsum(
        "ked,kdf->kef", head.reshape(kinds, per_rel, width), relations, precision=PRECISE
    ).reshape(kinds * per_rel, width)
    positive = jnp.sum(query * tail, -1)
    negative = jnp.dot(query, negatives.T, precision=PRECISE)
    grad_pos = jax.nn.sigmoid(positive) - 1.0
    grad_neg = jax.nn.sigmoid(negative) / neg_total
    grad_negs = jnp.dot(grad_neg.T, query, precision=PRECISE)
    shares = exchange(to_lanes(grad_negs, peers))
    mine = jnp.sum(shares, 0).reshape(own_count, -1)[:, :width]
    grad_query = grad_pos[:, None] * tail + jnp.dot(grad_neg, negatives, precision=PRECISE)
    grad_tail = grad_pos[:, None] * query
    grad_head = jnp.einsum(
        "kef,kdf->ked", grad_query.reshape(kinds, per_rel, width), relations, precision=PRECISE
    ).reshape(kinds * per_rel, width)
    slot_grad = jnp.zeros((slot_count, width), F32).at[source].add(grad_head)
    slot_grad = slot_grad.at[target].add(grad_tail)
    slot_grad = slot_grad.at[neg_slots].add(mine)
    returned = exchange(slot_grad.reshape(peers, -1, LANES)).reshape(slot_count, width)
    row_grad = jnp.zeros(table.shape, F32).at[touched.reshape(-1)].add(returned)
    new_state = row_state + jnp.mean(row_grad * row_grad, -1)
    new_table = table - LEARN_RATE * row_grad / (jnp.sqrt(new_state)[:, None] + EPSILON)
    return new_table.T, new_state.reshape(1, -1)


CAP = 19
PARTS = 3
TAIL = 16
PER_LINE = LANES // TAIL
LINES = PARTS * CAP
BLOCK = LINES + -(-CAP // PER_LINE)
WIDE = (PARTS + 1) * LANES
COLUMN = 4
DEPTH = 16
SENT = 32
ROOM = 32
AT_NEGS = 64
CODE = 2048


def iota(shape, dim):
    return lax.broadcasted_iota(jnp.int32, shape, dim)


def bits(mask):
    return jnp.where(mask, 1.0, 0.0).astype(BF16)


def shift_down(x, by):
    return lax.shift_right_logical(x, jnp.full(x.shape, by, x.dtype))


def same_depth(a, b):
    return lax.bitwise_and(a, DEPTH - 1) == lax.bitwise_and(b, DEPTH - 1)


def grid(condition, size=LANES):
    return bits(condition(iota((size, size), 0), iota((size, size), 1)))


def pieces(x, count):
    out = []
    for _ in range(count):
        piece = x.astype(BF16)
        out.append(piece)
        x = x - piece.astype(F32)
    return out


def dot(a, b, a_dim=1, b_dim=0):
    return lax.dot_general(a, b, (((a_dim,), (b_dim,)), ((), ())), preferred_element_type=F32)


def dot3(a, b, a_dim=1, b_dim=0):
    a_hi, a_lo = a if isinstance(a, tuple) else pieces(a, 2)
    b_hi, b_lo = b if isinstance(b, tuple) else pieces(b, 2)
    small = dot(a_lo, b_hi, a_dim, b_dim) + dot(a_hi, b_lo, a_dim, b_dim)
    return small + dot(a_hi, b_hi, a_dim, b_dim)


def spread(x):
    step = TAIL
    while step < LANES:
        x = x + pltpu.roll(x, step, 1)
        step *= 2
    return x


def call(kernel, outs, **kw):
    return pl.pallas_call(
        kernel,
        out_shape=outs,
        compiler_params=pltpu.CompilerParams(vmem_limit_bytes=VMEM),
        **kw,
    )


def shaped(*shape, dtype=F32):
    return jax.ShapeDtypeStruct(shape, dtype)


VECTOR = pl.BlockSpec(memory_space=pltpu.VMEM)
SCALAR = pl.BlockSpec(memory_space=pltpu.SMEM)


def mark_kernel(negs_ref, source_ref, target_ref, touched_ref, table_ref, out_ref, bundle_ref):
    width = table_ref.shape[0]
    sent, wide = touched_ref.shape
    bundle_ref[:width, :] = table_ref[...]
    bundle_ref[width:, :LANES] = jnp.concatenate(
        [touched_ref[...].astype(F32), jnp.zeros((sent, LANES - wide), F32)], 1
    )
    bundle_ref[width:, LANES:] = jnp.zeros((sent, bundle_ref.shape[1] - LANES), F32)
    peers = out_ref.shape[0] // 2
    ids = jnp.concatenate([source_ref[...], target_ref[...]], 1)
    count = ids.shape[1]
    owner = shift_down(ids, 5)
    within = lax.bitwise_and(ids, SENT - 1)
    at_depth = bits(same_depth(iota((peers, count), 0), owner))
    at_slot = bits(iota((LANES, count), 0) == shift_down(owner, 4) * SENT + within)
    marks = dot(at_depth, at_slot, 1, 1)
    out_ref[pl.ds(0, peers, stride=2), :] = jnp.where(marks > 0.0, 1.0, 0.0)
    at_owner = bits(iota((LANES, count), 0) == owner)
    at_within = bits(iota((SENT, count), 0) == within)
    used = jnp.where(dot(at_within, at_owner, 1, 1) > 0.0, 1.0, 0.0)
    info = jnp.broadcast_to(jnp.sum(used, 0, keepdims=True), marks.shape)
    lane = iota(marks.shape, 1)
    for n in range(negs_ref.shape[0]):
        info = jnp.where(lane == AT_NEGS + n, negs_ref[n].astype(F32), info)
    out_ref[pl.ds(1, peers, stride=2), :] = info


def neg_columns(info, number):
    lane = iota(info.shape, 1)
    columns = []
    for n in range(number):
        column = jnp.sum(jnp.where(lane == AT_NEGS + n, info, 0.0), 1, keepdims=True)
        columns.append(jnp.broadcast_to(column.astype(jnp.int32), info.shape))
    return columns


def before(count):
    return grid(lambda a, b: b < a, count)


def pack(rows, ref):
    peers = ref.shape[0] // BLOCK
    group = iota((peers, LANES), 1) // TAIL
    for part in range(BLOCK - LINES):
        line = jnp.zeros((peers, LANES), F32)
        for k in range(part * PER_LINE, min((part + 1) * PER_LINE, CAP)):
            mine = rows[k * peers : (k + 1) * peers]
            for t in range(PARTS):
                ref[pl.ds(t * CAP + k, peers, stride=BLOCK), :] = mine[:, t * LANES : (t + 1) * LANES]
            line = line + jnp.where(group == k % PER_LINE, mine[:, PARTS * LANES :], 0.0)
        ref[pl.ds(LINES + part, peers, stride=BLOCK), :] = line


def pack_kernel(
    number, me_ref, marks_ref, own_ref, first_ref, second_ref, third_ref, out_ref, codes_ref, flag_ref, onehot
):
    peers = marks_ref.shape[0] // 2
    marks = marks_ref[pl.ds(0, peers, stride=2), :]
    info = marks_ref[pl.ds(1, peers, stride=2), :]
    lane = iota(marks.shape, 1)
    negs = neg_columns(info, number)
    me = me_ref[0]
    depth, up = lax.bitwise_and(me, DEPTH - 1), lax.shift_right_logical(me, jnp.int32(4))
    refs = own_ref, first_ref, second_ref, third_ref
    width, owned = own_ref.shape[0] - SENT, own_ref.shape[1]

    touched = jnp.zeros(marks.shape, F32)
    for d, ref in enumerate(refs):
        rows = jnp.concatenate([ref[width:, :LANES], jnp.zeros((LANES - SENT, LANES), F32)], 0)
        rows = jnp.where(lane < SENT, rows.T[:peers] + (d * owned + 1.0), 0.0)
        touched = touched + pltpu.roll(rows, SENT * lax.bitwise_xor(up, jnp.int32(d)), 1)

    earlier = jnp.zeros((1, LANES), F32)
    neg_rows = jnp.zeros((1, LANES), F32)
    for slot in negs:
        owner = shift_down(slot, 5)
        at = jnp.where(lane == owner, 1.0, 0.0)
        rank = jnp.sum((dot(before(peers), at.astype(BF16)) + earlier) * at, 1, keepdims=True)
        earlier = earlier + jnp.sum(at, 0, keepdims=True)
        base = shift_down(owner, 4) * SENT
        at_row = lane == base + lax.bitwise_and(slot, SENT - 1)
        row = jnp.sum(jnp.where(at_row, touched, 0.0), 1, keepdims=True)
        here = same_depth(owner, depth) & (lane == base + rank.astype(jnp.int32))
        neg_rows = neg_rows + jnp.sum(jnp.where(here, row, 0.0), 0, keepdims=True)

    slots = jnp.where(lane < peers, info, 0.0)
    column = grid(same_depth)
    over_slots = jnp.sum(jnp.maximum(slots - CAP, 0.0), 0, keepdims=True)
    sums = jnp.where(iota((PER_LINE, LANES), 0) == 0, earlier, over_slots).astype(BF16)
    sums = jnp.max(dot(sums, column))
    total = jnp.max(dot((slots + earlier).astype(BF16), column))
    over = (total > COLUMN * CAP) | (sums > ROOM) | (jnp.max(over_slots) > ROOM)
    flag_ref[0] = over.astype(jnp.int32)

    neg_rows = jnp.broadcast_to(neg_rows, marks.shape)
    neg_marks = jnp.where(neg_rows > 0.0, 1.0, 0.0)
    block = grid(lambda a, b: a // SENT == b // SENT)
    earlier_block = grid(lambda a, b: (a % SENT == 0) & (a // SENT < b // SENT))
    rank = dot(marks.astype(BF16), grid(lambda a, b: (a // SENT == b // SENT) & (a <= b)))
    used = dot(marks.astype(BF16), block)
    neg_rank = used + (lane % SENT).astype(F32) + 1.0
    need = used + dot(neg_marks.astype(BF16), block)
    spare = jnp.maximum(CAP - need, 0.0)
    excess_from = dot(jnp.maximum(need - CAP, 0.0).astype(BF16), earlier_block)
    spare_from = dot(spare.astype(BF16), earlier_block)
    own = lane // SENT == up

    def mine(x):
        return jnp.sum(jnp.where(lane == SENT * up, x, 0.0), 1, keepdims=True)

    need, spare, spare_from = mine(need), mine(spare), mine(spare_from)

    def placed(rank, mask):
        x = excess_from + rank - (CAP + 1.0) - spare_from
        helped = jnp.where((rank > CAP) & (x >= 0.0) & (x < spare), need + x, -1.0)
        at = jnp.where(own, jnp.where(rank <= CAP, rank - 1.0, -1.0), helped)
        return jnp.where(mask > 0.0, at, -1.0)

    place, neg_place = placed(rank, marks), placed(neg_rank, neg_marks)
    upto = grid(lambda a, b: a <= b)
    helped = jnp.where((place >= 0.0) & ~own, 1.0, 0.0)
    held = jnp.broadcast_to(jnp.sum(helped, 1, keepdims=True), marks.shape)
    entry = dot(before(peers), held.astype(BF16)) + dot(helped.astype(BF16), upto)
    codes = touched + CODE * jnp.where(helped > 0.0, entry + ROOM, 0.0)
    neg_entry = dot(neg_marks.astype(BF16), upto)
    neg_codes = neg_rows + CODE * jnp.where((neg_place >= 0.0) & ~own, neg_entry, 0.0)

    spot = iota((peers, len(refs) * owned), 1)
    out = jnp.zeros(marks.shape, jnp.int32)
    for k in range(CAP):
        code = jnp.where(place == k, codes, 0.0) + jnp.where(neg_place == k, neg_codes, 0.0)
        code = jnp.sum(code, 1, keepdims=True).astype(jnp.int32)
        out = jnp.where(lane == k, code, out)
        onehot[k * peers : (k + 1) * peers, :] = bits(spot == lax.bitwise_and(code, CODE - 1) - 1)
    codes_ref[...] = out

    main = PARTS * LANES
    table = jnp.concatenate([ref[:width] for ref in refs], 1)
    wide = jnp.concatenate([table[:main]] + [table[main:]] * PER_LINE, 0)
    wide = pieces(wide, 2)
    pack(dot(onehot[...], wide[1], 1, 1) + dot(onehot[...], wide[0], 1, 1), out_ref)


def place_kernel(number, marks_ref, source_ref, target_ref, edge_ref, neg_ref):
    peers = marks_ref.shape[0] // 2
    info = marks_ref[pl.ds(1, peers, stride=2), :]
    ids = jnp.concatenate([source_ref[...], target_ref[...]], 1)
    count = ids.shape[1]
    owner = shift_down(ids, 5)
    at_owner = bits(iota((LANES, count), 0) == owner)
    at_within = bits(iota((SENT, count), 0) == lax.bitwise_and(ids, SENT - 1))
    used = bits(dot(at_within, at_owner, 1, 1) > 0.0)
    rank = dot(grid(lambda a, b: b <= a, SENT), used)
    from_edges = rank[SENT - 1 :]
    lane = iota(info.shape, 1)
    negs = [shift_down(slot, 5) for slot in neg_columns(info, number)]
    at_neg = [jnp.where(lane == slot, 1.0, 0.0) for slot in negs]
    need = from_edges
    for at in at_neg:
        need = need + jnp.sum(at, 0, keepdims=True)

    line = iota((PER_LINE, LANES), 0)
    spare = jnp.maximum(CAP - need, 0.0)
    excess = jnp.maximum(need - CAP, 0.0)
    first = jnp.where(line == 0, need, jnp.where(line == 1, spare, jnp.where(line == 2, excess, 0.0)))
    first = first.astype(BF16)
    earlier = dot(first, grid(lambda a, b: same_depth(a, b) & (a // DEPTH < b // DEPTH)))
    excess_from = earlier[2:3]
    first = jnp.where(line == 2, jnp.broadcast_to(earlier[1:2], first.shape), first.astype(F32))
    first = first.astype(BF16)
    mates = [
        dot(first, grid(lambda a, b: same_depth(a, b) & (a // DEPTH == y))) for y in range(COLUMN)
    ]

    def placed(owner, order, value):
        owner = owner.astype(F32)
        depth = owner - DEPTH * jnp.floor(owner / DEPTH)
        place = order * peers + owner
        x = value(excess_from) + order - CAP
        for y, mate in enumerate(mates):
            need, spare, start = (value(mate[i : i + 1]) for i in range(3))
            here = (order >= CAP) & (x >= start) & (x < start + spare)
            place = jnp.where(here, (need + x - start) * peers + y * DEPTH + depth, place)
        return place.astype(jnp.int32)

    def at_edges(row):
        row = jnp.broadcast_to(row, (PER_LINE, LANES)).astype(BF16)
        return dot(row, at_owner)[:1]

    order = jnp.sum(dot(rank.astype(BF16), at_owner) * at_within.astype(F32), 0, keepdims=True)
    edge_ref[...] = placed(owner, order - 1.0, at_edges)
    for n, at in enumerate(at_neg):
        order = dot(before(peers), at.astype(BF16)) + from_edges
        order = jnp.sum(order * at, 1, keepdims=True)

        def at_these(row):
            return jnp.sum(row * at, 1, keepdims=True)

        neg_ref[n * peers : (n + 1) * peers, :] = placed(negs[n][:, :1], order, at_these)
        from_edges = from_edges + jnp.sum(at, 0, keepdims=True)


def unpack(ref, hi_ref, lo_ref):
    peers = ref.shape[0] // BLOCK
    group = iota((peers, LANES), 1) // TAIL
    for k in range(CAP):
        tails = ref[pl.ds(LINES + k // PER_LINE, peers, stride=BLOCK), :]
        parts = [ref[pl.ds(t * CAP + k, peers, stride=BLOCK), :] for t in range(PARTS)]
        parts.append(jnp.where(group == k % PER_LINE, tails, 0.0))
        for t, part in enumerate(parts):
            hi, lo = pieces(part, 2)
            hi_ref[k * peers : (k + 1) * peers, t * LANES : (t + 1) * LANES] = hi
            lo_ref[k * peers : (k + 1) * peers, t * LANES : (t + 1) * LANES] = lo


def edges_kernel(
    block_ref, place_ref, neg_place_ref, row_place_ref, rel_hi_ref, rel_lo_ref,
    out_ref, slots_hi, slots_lo, grad_hi, grad_lo,
):
    peers = block_ref.shape[0] // BLOCK
    edges = place_ref.shape[0] // 2
    total = neg_place_ref.shape[0]
    kinds = rel_hi_ref.shape[0]
    per_rel = edges // kinds
    count = peers * CAP
    main = PARTS * LANES
    unpack(block_ref, slots_hi, slots_lo)

    spot = jnp.concatenate([place_ref[...], neg_place_ref[...]], 0)
    chosen = bits(iota((spot.shape[0], count), 1) == spot)
    got = dot(chosen, slots_lo[...]) + dot(chosen, slots_hi[...])
    got = jnp.concatenate([got[:, :main], spread(got[:, main:])], 1)

    def keep(start, grad):
        grad = jnp.concatenate([grad[:, :main], spread(grad[:, main:])], 1)
        hi, lo = pieces(grad, 2)
        grad_hi[start : start + grad.shape[0], :] = hi
        grad_lo[start : start + grad.shape[0], :] = lo

    negs = tuple(pieces(got[2 * edges :], 2))
    shares = jnp.zeros((total, WIDE), F32)
    for kind in range(kinds):
        start = kind * per_rel
        relation = rel_hi_ref[kind], rel_lo_ref[kind]
        query = dot3(got[start : start + per_rel], relation)
        tail = got[edges + start : edges + start + per_rel]
        positive = jnp.sum(query * tail, 1, keepdims=True)
        grad_pos = jax.nn.sigmoid(positive) - 1.0
        keep(edges + start, grad_pos * query)
        query = tuple(pieces(query, 2))
        grad_neg = jax.nn.sigmoid(dot3(query, negs, 1, 1)) / total
        grad_query = grad_pos * tail + dot3(grad_neg, negs)
        keep(start, dot3(grad_query, relation, 1, 1))
        grad_neg = jax.nn.sigmoid(dot3(negs, query, 1, 1)) / total
        shares = shares + dot3(grad_neg, query)
    keep(2 * edges, shares)

    spot = row_place_ref[...]
    chosen = bits(iota((count, spot.shape[1]), 0) == spot)
    pack(dot(chosen, grad_lo[...]) + dot(chosen, grad_hi[...]), out_ref)


def gathered(chosen, hi_ref, lo_ref):
    got = dot(chosen, lo_ref[...]) + dot(chosen, hi_ref[...])
    main = PARTS * LANES
    return got[:, :main], spread(got[:, main:])


def help_kernel(block_ref, code_ref, out_ref, hi_ref, lo_ref):
    unpack(block_ref, hi_ref, lo_ref)
    code = code_ref[...]
    entry = shift_down(code, 11) - 1
    here = iota((out_ref.shape[0], code.shape[1]), 0) == entry
    row = jnp.where(here, (lax.bitwise_and(code, CODE - 1) - 1).astype(F32), -1.0)
    row = jnp.max(row, 1, keepdims=True)
    main, tails = gathered(bits(here), hi_ref, lo_ref)
    tails = jnp.where(iota(tails.shape, 1) < TAIL, tails, row)
    out_ref[...] = jnp.concatenate([main, tails], 1)


def sum_kernel(block_ref, code_ref, out_ref, hi_ref, lo_ref):
    unpack(block_ref, hi_ref, lo_ref)
    row = lax.bitwise_and(code_ref[...], CODE - 1) - 1
    chosen = bits(iota((out_ref.shape[0], row.shape[1]), 0) == row)
    out_ref[...] = jnp.concatenate(gathered(chosen, hi_ref, lo_ref), 1)


def update_kernel(
    own_ref, first_ref, second_ref, third_ref, table_ref, state_ref, new_table_ref, new_state_ref
):
    width, owned = table_ref.shape
    grad = own_ref[...]
    for d, ref in enumerate((first_ref, second_ref, third_ref)):
        rows = ref[...]
        at = rows[:, WIDE - 1 :].astype(jnp.int32) - (d + 1) * owned
        chosen = bits(iota((rows.shape[0], owned), 1) == at)
        hi, lo = pieces(rows, 2)
        grad = grad + (dot(chosen, lo, 0, 0) + dot(chosen, hi, 0, 0))
    grad = grad.T[:width]
    state = state_ref[...] + jnp.sum(grad * grad, 0, keepdims=True) / width
    new_state_ref[...] = state
    new_table_ref[...] = table_ref[...] - LEARN_RATE * grad / (jnp.sqrt(state) + EPSILON)


def to_mates(x):
    peers = lax.axis_size("grp")
    return [
        lax.ppermute(x, "grp", [(p, p ^ (d * DEPTH)) for p in range(peers)])
        for d in range(1, COLUMN)
    ]


def exchange_blocks(blocks):
    peers = lax.axis_size("grp")
    return exchange(blocks.reshape(peers, BLOCK, 1, LANES)).reshape(blocks.shape)


def compact_path(marks, blocks, codes, source, target, number, rel_hi, rel_lo, table, state):
    peers = marks.shape[0] // 2
    edges = source.shape[1]
    width, owned = table.shape
    count = peers * CAP
    split = [pltpu.VMEM((count, WIDE), BF16)] * 2
    blocks = exchange_blocks(blocks)
    edge_place, neg_place = call(
        functools.partial(place_kernel, number),
        (shaped(1, 2 * edges, dtype=jnp.int32), shaped(peers * number, 1, dtype=jnp.int32)),
    )(marks, source, target)
    row_place = jnp.concatenate([edge_place, neg_place.reshape(1, -1)], 1)
    grads = call(
        edges_kernel,
        shaped(*blocks.shape),
        scratch_shapes=split + [pltpu.VMEM((row_place.shape[1], WIDE), BF16)] * 2,
    )(blocks, edge_place.reshape(-1, 1), neg_place, row_place, rel_hi, rel_lo)
    returned = exchange_blocks(grads)
    codes = codes[:, :CAP].T.reshape(1, -1)
    helped = call(help_kernel, shaped(2 * ROOM, WIDE), scratch_shapes=split)(returned, codes)
    helped = to_mates(helped)
    own = call(sum_kernel, shaped(owned, WIDE), scratch_shapes=split)(returned, codes)
    return call(
        update_kernel,
        (shaped(width, owned), shaped(1, owned)),
    )(own, *helped, table, state)


def per_device(table, row_state, relations, touched, source, target, neg_slots):
    peers, sent = touched.shape
    owned, width = table.shape
    number = neg_slots.shape[0]
    across = table.T
    source_row, target_row = source.reshape(1, -1), target.reshape(1, -1)
    marks, bundle = call(
        mark_kernel,
        (shaped(2 * peers, LANES), shaped(width + sent, owned)),
        in_specs=[SCALAR] + [VECTOR] * 4,
        out_specs=(VECTOR, VECTOR),
    )(neg_slots, source_row, target_row, touched.T, across)
    marks = exchange(marks.reshape(peers, 2, 1, LANES)).reshape(2 * peers, LANES)
    bundles = [bundle] + to_mates(bundle)
    wide = jnp.pad(relations, ((0, 0), (0, WIDE - width), (0, WIDE - width)))
    rel_hi = lax.reduce_precision(wide, 8, 7)
    rel_lo = (wide - rel_hi).astype(BF16)
    rel_hi = rel_hi.astype(BF16)
    blocks, codes, crowded = call(
        functools.partial(pack_kernel, number),
        (
            shaped(peers * BLOCK, LANES),
            shaped(peers, LANES, dtype=jnp.int32),
            shaped(1, dtype=jnp.int32),
        ),
        in_specs=[SCALAR] + [VECTOR] * (1 + COLUMN),
        out_specs=(VECTOR, VECTOR, SCALAR),
        scratch_shapes=[pltpu.VMEM((CAP * peers, COLUMN * owned), BF16)],
    )(lax.axis_index("grp").reshape(1), marks, *bundles)
    new_table, new_state = lax.cond(
        crowded[0] > 0,
        lambda: full_path(table, row_state, relations, touched, source, target, neg_slots),
        lambda: compact_path(
            marks, blocks, codes, source_row, target_row, number, rel_hi, rel_lo, across,
            row_state.reshape(1, -1),
        ),
    )
    return new_table.T, new_state.reshape(-1)


def solution(mesh):
    return jax.shard_map(
        per_device,
        mesh=mesh,
        in_specs=(
            P(("grp", "rep"), None),
            P(("grp", "rep")),
            P(),
            P(("grp", "rep"), None),
            P(("grp", "rep")),
            P(("grp", "rep")),
            P(("grp", "rep")),
        ),
        out_specs=(P(("grp", "rep"), None), P(("grp", "rep"))),
        check_vma=False,
    )
```

```python
import functools

import jax
import jax.numpy as jnp
from jax import lax
from jax.experimental import pallas as pl
from jax.experimental.pallas import tpu as pltpu
from jax.sharding import PartitionSpec as P

PRECISE = lax.Precision.HIGHEST
LEARN_RATE = 0.1
EPSILON = 1e-06
LANES = 128
VMEM = 56 * 1024 * 1024
F32 = jnp.float32
BF16 = jnp.bfloat16


def exchange(blocks):
    return lax.all_to_all(blocks, "grp", split_axis=0, concat_axis=0, tiled=True)


def take_rows(rows, ids):
    return jnp.take(rows, ids, axis=0, mode="clip")


def to_lanes(rows, peers):
    width = rows.shape[1]
    wide = -(-width // LANES) * LANES
    return jnp.pad(rows, ((0, 0), (0, wide - width))).reshape(peers, -1, LANES)


def full_path(table, row_state, relations, touched, source, target, neg_slots):
    width = table.shape[1]
    peers, sent = touched.shape
    kinds = relations.shape[0]
    per_rel = source.shape[0] // kinds
    slot_count = peers * sent
    own_count = neg_slots.shape[0]
    neg_total = peers * own_count
    outgoing = take_rows(table, touched.reshape(-1))
    slots = exchange(outgoing.reshape(peers, -1, LANES)).reshape(slot_count, width)
    own_neg = to_lanes(take_rows(slots, neg_slots), 1)
    gathered = exchange(jnp.broadcast_to(own_neg, (peers,) + own_neg.shape[1:]))
    negatives = gathered.reshape(neg_total, -1)[:, :width]
    head = take_rows(slots, source)
    tail = take_rows(slots, target)
    query = jnp.einsum(
        "ked,kdf->kef", head.reshape(kinds, per_rel, width), relations, precision=PRECISE
    ).reshape(kinds * per_rel, width)
    positive = jnp.sum(query * tail, -1)
    negative = jnp.dot(query, negatives.T, precision=PRECISE)
    grad_pos = jax.nn.sigmoid(positive) - 1.0
    grad_neg = jax.nn.sigmoid(negative) / neg_total
    grad_negs = jnp.dot(grad_neg.T, query, precision=PRECISE)
    shares = exchange(to_lanes(grad_negs, peers))
    mine = jnp.sum(shares, 0).reshape(own_count, -1)[:, :width]
    grad_query = grad_pos[:, None] * tail + jnp.dot(grad_neg, negatives, precision=PRECISE)
    grad_tail = grad_pos[:, None] * query
    grad_head = jnp.einsum(
        "kef,kdf->ked", grad_query.reshape(kinds, per_rel, width), relations, precision=PRECISE
    ).reshape(kinds * per_rel, width)
    slot_grad = jnp.zeros((slot_count, width), F32).at[source].add(grad_head)
    slot_grad = slot_grad.at[target].add(grad_tail)
    slot_grad = slot_grad.at[neg_slots].add(mine)
    returned = exchange(slot_grad.reshape(peers, -1, LANES)).reshape(slot_count, width)
    row_grad = jnp.zeros(table.shape, F32).at[touched.reshape(-1)].add(returned)
    new_state = row_state + jnp.mean(row_grad * row_grad, -1)
    new_table = table - LEARN_RATE * row_grad / (jnp.sqrt(new_state)[:, None] + EPSILON)
    return new_table.T, new_state.reshape(1, -1)


CAP = 19
PARTS = 3
TAIL = 16
PER_LINE = LANES // TAIL
LINES = PARTS * CAP
BLOCK = LINES + -(-CAP // PER_LINE)
MAIN = PARTS * LANES
WIDE = MAIN + LANES
COLUMN = 4
DEPTH = 16
SENT = 32
ROOM = 32
AT_NEGS = 64
CODE = 2048


def iota(shape, dim):
    return lax.broadcasted_iota(jnp.int32, shape, dim)


def bits(mask):
    return jnp.where(mask, 1.0, 0.0).astype(BF16)


def shift_down(x, by):
    return lax.shift_right_logical(x, jnp.full(x.shape, by, x.dtype))


def same_depth(a, b):
    return lax.bitwise_and(a, DEPTH - 1) == lax.bitwise_and(b, DEPTH - 1)


def grid(condition, size=LANES):
    return bits(condition(iota((size, size), 0), iota((size, size), 1)))


def pieces(x, count):
    out = []
    for _ in range(count):
        piece = x.astype(BF16)
        out.append(piece)
        x = x - piece.astype(F32)
    return out


def dot(a, b, a_dim=1, b_dim=0):
    return lax.dot_general(a, b, (((a_dim,), (b_dim,)), ((), ())), preferred_element_type=F32)


def dot3(a, b, a_dim=1, b_dim=0):
    a_hi, a_lo = a if isinstance(a, tuple) else pieces(a, 2)
    b_hi, b_lo = b if isinstance(b, tuple) else pieces(b, 2)
    small = dot(a_lo, b_hi, a_dim, b_dim) + dot(a_hi, b_lo, a_dim, b_dim)
    return small + dot(a_hi, b_hi, a_dim, b_dim)


def halves(hi, lo):
    lane = iota(hi.shape, 1)
    return jnp.where(lane < LANES // 2, hi.astype(F32), lo.astype(F32)).astype(BF16)


def fold(x):
    return x + pltpu.roll(x, LANES // 2, 1)


def spread(x):
    step = TAIL
    while step < LANES:
        x = x + pltpu.roll(x, step, 1)
        step *= 2
    return x


def call(kernel, outs, **kw):
    return pl.pallas_call(
        kernel,
        out_shape=outs,
        compiler_params=pltpu.CompilerParams(vmem_limit_bytes=VMEM),
        **kw,
    )


def shaped(*shape, dtype=F32):
    return jax.ShapeDtypeStruct(shape, dtype)


VECTOR = pl.BlockSpec(memory_space=pltpu.VMEM)
SCALAR = pl.BlockSpec(memory_space=pltpu.SMEM)


def mark_kernel(negs_ref, source_ref, target_ref, touched_ref, table_ref, out_ref, bundle_ref):
    width = table_ref.shape[0]
    sent, wide = touched_ref.shape
    bundle_ref[:width, :] = table_ref[...]
    bundle_ref[width:, :LANES] = jnp.concatenate(
        [touched_ref[...].astype(F32), jnp.zeros((sent, LANES - wide), F32)], 1
    )
    bundle_ref[width:, LANES:] = jnp.zeros((sent, bundle_ref.shape[1] - LANES), F32)
    peers = out_ref.shape[0] // 2
    ids = jnp.concatenate([source_ref[...], target_ref[...]], 1)
    count = ids.shape[1]
    owner = shift_down(ids, 5)
    within = lax.bitwise_and(ids, SENT - 1)
    at_depth = bits(same_depth(iota((peers, count), 0), owner))
    at_slot = bits(iota((LANES, count), 0) == shift_down(owner, 4) * SENT + within)
    marks = dot(at_depth, at_slot, 1, 1)
    out_ref[pl.ds(0, peers, stride=2), :] = jnp.where(marks > 0.0, 1.0, 0.0)
    at_owner = bits(iota((LANES, count), 0) == owner)
    at_within = bits(iota((SENT, count), 0) == within)
    used = jnp.where(dot(at_within, at_owner, 1, 1) > 0.0, 1.0, 0.0)
    info = jnp.broadcast_to(jnp.sum(used, 0, keepdims=True), marks.shape)
    lane = iota(marks.shape, 1)
    for n in range(negs_ref.shape[0]):
        info = jnp.where(lane == AT_NEGS + n, negs_ref[n].astype(F32), info)
    out_ref[pl.ds(1, peers, stride=2), :] = info


def neg_columns(info, number):
    lane = iota(info.shape, 1)
    columns = []
    for n in range(number):
        column = jnp.sum(jnp.where(lane == AT_NEGS + n, info, 0.0), 1, keepdims=True)
        columns.append(jnp.broadcast_to(column.astype(jnp.int32), info.shape))
    return columns


def before(count):
    return grid(lambda a, b: b < a, count)


def pack(rows, ref):
    peers = ref.shape[0] // BLOCK
    group = iota((peers, LANES), 1) // TAIL
    for part in range(BLOCK - LINES):
        line = jnp.zeros((peers, LANES), F32)
        for k in range(part * PER_LINE, min((part + 1) * PER_LINE, CAP)):
            mine = rows[k * peers : (k + 1) * peers]
            for t in range(PARTS):
                ref[pl.ds(t * CAP + k, peers, stride=BLOCK), :] = mine[:, t * LANES : (t + 1) * LANES]
            line = line + jnp.where(group == k % PER_LINE, mine[:, PARTS * LANES :], 0.0)
        ref[pl.ds(LINES + part, peers, stride=BLOCK), :] = line


def pack_kernel(
    number, me_ref, marks_ref, own_ref, first_ref, second_ref, third_ref, out_ref, codes_ref, flag_ref, onehot
):
    peers = marks_ref.shape[0] // 2
    marks = marks_ref[pl.ds(0, peers, stride=2), :]
    info = marks_ref[pl.ds(1, peers, stride=2), :]
    lane = iota(marks.shape, 1)
    negs = neg_columns(info, number)
    me = me_ref[0]
    depth, up = lax.bitwise_and(me, DEPTH - 1), lax.shift_right_logical(me, jnp.int32(4))
    refs = own_ref, first_ref, second_ref, third_ref
    width, owned = own_ref.shape[0] - SENT, own_ref.shape[1]

    touched = jnp.zeros(marks.shape, F32)
    for d, ref in enumerate(refs):
        rows = jnp.concatenate([ref[width:, :LANES], jnp.zeros((LANES - SENT, LANES), F32)], 0)
        rows = jnp.where(lane < SENT, rows.T[:peers] + (d * owned + 1.0), 0.0)
        touched = touched + pltpu.roll(rows, SENT * lax.bitwise_xor(up, jnp.int32(d)), 1)

    earlier = jnp.zeros((1, LANES), F32)
    neg_rows = jnp.zeros((1, LANES), F32)
    for slot in negs:
        owner = shift_down(slot, 5)
        at = jnp.where(lane == owner, 1.0, 0.0)
        rank = jnp.sum((dot(before(peers), at.astype(BF16)) + earlier) * at, 1, keepdims=True)
        earlier = earlier + jnp.sum(at, 0, keepdims=True)
        base = shift_down(owner, 4) * SENT
        at_row = lane == base + lax.bitwise_and(slot, SENT - 1)
        row = jnp.sum(jnp.where(at_row, touched, 0.0), 1, keepdims=True)
        here = same_depth(owner, depth) & (lane == base + rank.astype(jnp.int32))
        neg_rows = neg_rows + jnp.sum(jnp.where(here, row, 0.0), 0, keepdims=True)

    slots = jnp.where(lane < peers, info, 0.0)
    column = grid(same_depth)
    over_slots = jnp.sum(jnp.maximum(slots - CAP, 0.0), 0, keepdims=True)
    sums = jnp.where(iota((PER_LINE, LANES), 0) == 0, earlier, over_slots).astype(BF16)
    sums = jnp.max(dot(sums, column))
    total = jnp.max(dot((slots + earlier).astype(BF16), column))
    over = (total > COLUMN * CAP) | (sums > ROOM) | (jnp.max(over_slots) > ROOM)
    flag_ref[0] = over.astype(jnp.int32)

    neg_rows = jnp.broadcast_to(neg_rows, marks.shape)
    neg_marks = jnp.where(neg_rows > 0.0, 1.0, 0.0)
    block = grid(lambda a, b: a // SENT == b // SENT)
    earlier_block = grid(lambda a, b: (a % SENT == 0) & (a // SENT < b // SENT))
    rank = dot(marks.astype(BF16), grid(lambda a, b: (a // SENT == b // SENT) & (a <= b)))
    used = dot(marks.astype(BF16), block)
    neg_rank = used + (lane % SENT).astype(F32) + 1.0
    need = used + dot(neg_marks.astype(BF16), block)
    spare = jnp.maximum(CAP - need, 0.0)
    excess_from = dot(jnp.maximum(need - CAP, 0.0).astype(BF16), earlier_block)
    spare_from = dot(spare.astype(BF16), earlier_block)
    own = lane // SENT == up

    def mine(x):
        return jnp.sum(jnp.where(lane == SENT * up, x, 0.0), 1, keepdims=True)

    need, spare, spare_from = mine(need), mine(spare), mine(spare_from)

    def placed(rank, mask):
        x = excess_from + rank - (CAP + 1.0) - spare_from
        helped = jnp.where((rank > CAP) & (x >= 0.0) & (x < spare), need + x, -1.0)
        at = jnp.where(own, jnp.where(rank <= CAP, rank - 1.0, -1.0), helped)
        return jnp.where(mask > 0.0, at, -1.0)

    place, neg_place = placed(rank, marks), placed(neg_rank, neg_marks)
    upto = grid(lambda a, b: a <= b)
    helped = jnp.where((place >= 0.0) & ~own, 1.0, 0.0)
    held = jnp.broadcast_to(jnp.sum(helped, 1, keepdims=True), marks.shape)
    entry = dot(before(peers), held.astype(BF16)) + dot(helped.astype(BF16), upto)
    codes = touched + CODE * jnp.where(helped > 0.0, entry + ROOM, 0.0)
    neg_entry = dot(neg_marks.astype(BF16), upto)
    neg_codes = neg_rows + CODE * jnp.where((neg_place >= 0.0) & ~own, neg_entry, 0.0)

    mates = len(refs) - 1
    column = iota((ROOM, LANES), 0)
    of_slots = jnp.zeros((ROOM, LANES), F32)
    for e in range(ROOM):
        row = jnp.sum(jnp.where((helped > 0.0) & (entry == e + 1.0), touched, 0.0), 0, keepdims=True)
        of_slots = jnp.where(column == e, row, of_slots)
    of_negs = jnp.where((neg_entry[:1] == column + 1.0) & (neg_marks[:1] > 0.0), neg_rows[:1], 0.0)
    row = jnp.sum(jnp.concatenate([of_negs, of_slots], 0), 1, keepdims=True).astype(jnp.int32)
    from_mates = bits(iota((2 * ROOM, mates * owned), 1) == row - (owned + 1))

    spot = iota((peers, owned + LANES), 1)
    out = jnp.zeros(marks.shape, jnp.int32)
    for k in range(CAP):
        code = jnp.where(place == k, codes, 0.0) + jnp.where(neg_place == k, neg_codes, 0.0)
        code = jnp.sum(code, 1, keepdims=True).astype(jnp.int32)
        out = jnp.where(lane == k, code, out)
        helping = shift_down(code, 11)
        own_row = lax.bitwise_and(code, CODE - 1) - 1
        at = jnp.where(helping > 0, owned - 1 + helping, own_row)
        onehot[k * peers : (k + 1) * peers, :] = bits(spot == at)
    codes_ref[...] = out

    hi, lo = pieces(jnp.concatenate([ref[:width] for ref in refs], 1), 2)
    tails = [hi[MAIN:]] * (PER_LINE // 2) + [lo[MAIN:]] * (PER_LINE // 2)
    hi, lo = jnp.concatenate([hi[:MAIN]] + tails, 0), lo[:MAIN]

    def joined(of_hi, of_lo):
        return jnp.concatenate([of_hi[:, :MAIN] + of_lo, fold(of_hi[:, MAIN:])], 1)

    held = joined(dot(from_mates, hi[:, owned:], 1, 1), dot(from_mates, lo[:, owned:], 1, 1))
    held = jnp.concatenate([held, jnp.zeros((LANES - 2 * ROOM, WIDE), F32)], 0)
    held_hi, held_lo = pieces(held, 2)
    held_hi = jnp.concatenate([held_hi[:, :MAIN], halves(held_hi[:, MAIN:], held_lo[:, MAIN:])], 1)
    held_lo = held_lo[:, :MAIN]
    own, other = onehot[:, :owned], onehot[:, owned:]
    got = joined(
        dot(own, hi[:, :owned], 1, 1) + dot(other, held_hi),
        dot(own, lo[:, :owned], 1, 1) + dot(other, held_lo),
    )
    pack(got, out_ref)


def place_kernel(number, marks_ref, source_ref, target_ref, edge_ref, neg_ref):
    peers = marks_ref.shape[0] // 2
    info = marks_ref[pl.ds(1, peers, stride=2), :]
    ids = jnp.concatenate([source_ref[...], target_ref[...]], 1)
    count = ids.shape[1]
    owner = shift_down(ids, 5)
    at_owner = bits(iota((LANES, count), 0) == owner)
    at_within = bits(iota((SENT, count), 0) == lax.bitwise_and(ids, SENT - 1))
    used = bits(dot(at_within, at_owner, 1, 1) > 0.0)
    rank = dot(grid(lambda a, b: b <= a, SENT), used)
    from_edges = rank[SENT - 1 :]
    lane = iota(info.shape, 1)
    negs = [shift_down(slot, 5) for slot in neg_columns(info, number)]
    at_neg = [jnp.where(lane == slot, 1.0, 0.0) for slot in negs]
    need = from_edges
    for at in at_neg:
        need = need + jnp.sum(at, 0, keepdims=True)

    line = iota((PER_LINE, LANES), 0)
    spare = jnp.maximum(CAP - need, 0.0)
    excess = jnp.maximum(need - CAP, 0.0)
    first = jnp.where(line == 0, need, jnp.where(line == 1, spare, jnp.where(line == 2, excess, 0.0)))
    first = first.astype(BF16)
    earlier = dot(first, grid(lambda a, b: same_depth(a, b) & (a // DEPTH < b // DEPTH)))
    excess_from = earlier[2:3]
    first = jnp.where(line == 2, jnp.broadcast_to(earlier[1:2], first.shape), first.astype(F32))
    first = first.astype(BF16)
    mates = [
        dot(first, grid(lambda a, b: same_depth(a, b) & (a // DEPTH == y))) for y in range(COLUMN)
    ]

    def placed(owner, order, value):
        owner = owner.astype(F32)
        depth = owner - DEPTH * jnp.floor(owner / DEPTH)
        place = order * peers + owner
        x = value(excess_from) + order - CAP
        for y, mate in enumerate(mates):
            need, spare, start = (value(mate[i : i + 1]) for i in range(3))
            here = (order >= CAP) & (x >= start) & (x < start + spare)
            place = jnp.where(here, (need + x - start) * peers + y * DEPTH + depth, place)
        return place.astype(jnp.int32)

    def at_edges(row):
        row = jnp.broadcast_to(row, (PER_LINE, LANES)).astype(BF16)
        return dot(row, at_owner)[:1]

    order = jnp.sum(dot(rank.astype(BF16), at_owner) * at_within.astype(F32), 0, keepdims=True)
    edge_ref[...] = placed(owner, order - 1.0, at_edges)
    for n, at in enumerate(at_neg):
        order = dot(before(peers), at.astype(BF16)) + from_edges
        order = jnp.sum(order * at, 1, keepdims=True)

        def at_these(row):
            return jnp.sum(row * at, 1, keepdims=True)

        neg_ref[n * peers : (n + 1) * peers, :] = placed(negs[n][:, :1], order, at_these)
        from_edges = from_edges + jnp.sum(at, 0, keepdims=True)


def unpack(ref, hi_ref, lo_ref):
    peers = ref.shape[0] // BLOCK
    group = iota((peers, LANES), 1) // TAIL
    for k in range(CAP):
        span = slice(k * peers, (k + 1) * peers)
        for t in range(PARTS):
            hi, lo = pieces(ref[pl.ds(t * CAP + k, peers, stride=BLOCK), :], 2)
            hi_ref[span, t * LANES : (t + 1) * LANES] = hi
            lo_ref[span, t * LANES : (t + 1) * LANES] = lo
        tails = ref[pl.ds(LINES + k // PER_LINE, peers, stride=BLOCK), :]
        hi, lo = pieces(jnp.where(group == k % PER_LINE, tails, 0.0), 2)
        both = hi.astype(F32) + pltpu.roll(lo.astype(F32), LANES // 2, 1)
        hi_ref[span, MAIN:] = both.astype(BF16)


def gathered(chosen, hi_ref, lo_ref):
    of_hi = dot(chosen, hi_ref[...])
    return of_hi[:, :MAIN] + dot(chosen, lo_ref[...]), spread(of_hi[:, MAIN:])


def edges_kernel(
    block_ref, place_ref, neg_place_ref, row_place_ref, rel_hi_ref, rel_lo_ref,
    out_ref, slots_hi, slots_lo, grad_hi, grad_lo,
):
    peers = block_ref.shape[0] // BLOCK
    edges = place_ref.shape[0] // 2
    total = neg_place_ref.shape[0]
    kinds = rel_hi_ref.shape[0]
    per_rel = edges // kinds
    count = peers * CAP
    unpack(block_ref, slots_hi, slots_lo)

    spot = jnp.concatenate([place_ref[...], neg_place_ref[...]], 0)
    chosen = bits(iota((spot.shape[0], count), 1) == spot)
    got = jnp.concatenate(gathered(chosen, slots_hi, slots_lo), 1)

    def keep(start, grad):
        span = slice(start, start + grad.shape[0])
        grad_hi[span, :MAIN], grad_lo[span, :] = pieces(grad[:, :MAIN], 2)
        grad_hi[span, MAIN:] = halves(*pieces(spread(grad[:, MAIN:]), 2))

    negs = tuple(pieces(got[2 * edges :], 2))
    shares = jnp.zeros((total, WIDE), F32)
    for kind in range(kinds):
        start = kind * per_rel
        relation = rel_hi_ref[kind], rel_lo_ref[kind]
        query = dot3(got[start : start + per_rel], relation)
        tail = got[edges + start : edges + start + per_rel]
        positive = jnp.sum(query * tail, 1, keepdims=True)
        grad_pos = jax.nn.sigmoid(positive) - 1.0
        keep(edges + start, grad_pos * query)
        query = tuple(pieces(query, 2))
        grad_neg = jax.nn.sigmoid(dot3(query, negs, 1, 1)) / total
        grad_query = grad_pos * tail + dot3(grad_neg, negs)
        keep(start, dot3(grad_query, relation, 1, 1))
        grad_neg = jax.nn.sigmoid(dot3(negs, query, 1, 1)) / total
        shares = shares + dot3(grad_neg, query)
    keep(2 * edges, shares)

    spot = row_place_ref[...]
    chosen = bits(iota((count, spot.shape[1]), 0) == spot)
    of_hi = dot(chosen, grad_hi[...])
    of_main = of_hi[:, :MAIN] + dot(chosen, grad_lo[...])
    pack(jnp.concatenate([of_main, fold(of_hi[:, MAIN:])], 1), out_ref)


def help_kernel(block_ref, code_ref, out_ref, hi_ref, lo_ref):
    unpack(block_ref, hi_ref, lo_ref)
    code = code_ref[...]
    entry = shift_down(code, 11) - 1
    here = iota((out_ref.shape[1], code.shape[1]), 0) == entry
    row = jnp.where(here, (lax.bitwise_and(code, CODE - 1) - 1).astype(F32), -1.0)
    row = jnp.max(row, 1, keepdims=True)
    main, tails = gathered(bits(here), hi_ref, lo_ref)
    tails = jnp.where(iota(tails.shape, 1) < TAIL, tails, row)
    for y in range(out_ref.shape[0]):
        out_ref[y] = jnp.concatenate([main, tails], 1)


def sum_kernel(block_ref, code_ref, out_ref, hi_ref, lo_ref):
    unpack(block_ref, hi_ref, lo_ref)
    row = lax.bitwise_and(code_ref[...], CODE - 1) - 1
    chosen = bits(iota((out_ref.shape[0], row.shape[1]), 0) == row)
    out_ref[...] = jnp.concatenate(gathered(chosen, hi_ref, lo_ref), 1)


def update_kernel(me_ref, own_ref, lists_ref, table_ref, state_ref, new_table_ref, new_state_ref):
    width, owned = table_ref.shape
    rows = lists_ref[...].reshape(-1, WIDE)
    up = lax.shift_right_logical(me_ref[0], jnp.int32(4))
    mate = iota((rows.shape[0], 1), 0) // (2 * ROOM)
    first = lax.bitwise_xor(mate, jnp.broadcast_to(up, mate.shape)) * owned
    at = rows[:, WIDE - 1 :].astype(jnp.int32) - first
    chosen = bits(iota((rows.shape[0], owned), 1) == at)
    hi, lo = pieces(rows, 2)
    grad = own_ref[...] + (dot(chosen, lo, 0, 0) + dot(chosen, hi, 0, 0))
    grad = grad.T[:width]
    state = state_ref[...] + jnp.sum(grad * grad, 0, keepdims=True) / width
    new_state_ref[...] = state
    new_table_ref[...] = table_ref[...] - LEARN_RATE * grad / (jnp.sqrt(state) + EPSILON)


def to_mates(x):
    peers = lax.axis_size("grp")
    return [
        lax.ppermute(x, "grp", [(p, p ^ (d * DEPTH)) for p in range(peers)])
        for d in range(1, COLUMN)
    ]


def exchange_blocks(blocks):
    peers = lax.axis_size("grp")
    return exchange(blocks.reshape(peers, BLOCK, 1, LANES)).reshape(blocks.shape)


def compact_path(me, marks, blocks, codes, source, target, number, rel_hi, rel_lo, table, state):
    peers = marks.shape[0] // 2
    edges = source.shape[1]
    width, owned = table.shape
    count = peers * CAP
    split = [pltpu.VMEM((count, WIDE), BF16), pltpu.VMEM((count, MAIN), BF16)]
    blocks = exchange_blocks(blocks)
    edge_place, neg_place = call(
        functools.partial(place_kernel, number),
        (shaped(1, 2 * edges, dtype=jnp.int32), shaped(peers * number, 1, dtype=jnp.int32)),
    )(marks, source, target)
    row_place = jnp.concatenate([edge_place, neg_place.reshape(1, -1)], 1)
    grads = call(
        edges_kernel,
        shaped(*blocks.shape),
        scratch_shapes=split
        + [pltpu.VMEM((row_place.shape[1], size), BF16) for size in (WIDE, MAIN)],
    )(blocks, edge_place.reshape(-1, 1), neg_place, row_place, rel_hi, rel_lo)
    returned = exchange_blocks(grads)
    codes = codes[:, :CAP].T.reshape(1, -1)
    lists = call(help_kernel, shaped(COLUMN, 2 * ROOM, WIDE), scratch_shapes=split)(returned, codes)
    lists = lax.all_to_all(
        lists, "grp", 0, 0, tiled=True,
        axis_index_groups=[list(range(z, peers, DEPTH)) for z in range(DEPTH)],
    )
    own = call(sum_kernel, shaped(owned, WIDE), scratch_shapes=split)(returned, codes)
    return call(
        update_kernel,
        (shaped(width, owned), shaped(1, owned)),
        in_specs=[SCALAR] + [VECTOR] * 4,
    )(me, own, lists, table, state)


def per_device(table, row_state, relations, touched, source, target, neg_slots):
    peers, sent = touched.shape
    owned, width = table.shape
    number = neg_slots.shape[0]
    across = table.T
    source_row, target_row = source.reshape(1, -1), target.reshape(1, -1)
    marks, bundle = call(
        mark_kernel,
        (shaped(2 * peers, LANES), shaped(width + sent, owned)),
        in_specs=[SCALAR] + [VECTOR] * 4,
        out_specs=(VECTOR, VECTOR),
    )(neg_slots, source_row, target_row, touched.T, across)
    marks = exchange(marks.reshape(peers, 2, 1, LANES)).reshape(2 * peers, LANES)
    bundles = [bundle] + to_mates(bundle)
    wide = jnp.pad(relations, ((0, 0), (0, WIDE - width), (0, WIDE - width)))
    rel_hi = lax.reduce_precision(wide, 8, 7)
    rel_lo = (wide - rel_hi).astype(BF16)
    rel_hi = rel_hi.astype(BF16)
    me = lax.axis_index("grp").reshape(1)
    blocks, codes, crowded = call(
        functools.partial(pack_kernel, number),
        (
            shaped(peers * BLOCK, LANES),
            shaped(peers, LANES, dtype=jnp.int32),
            shaped(1, dtype=jnp.int32),
        ),
        in_specs=[SCALAR] + [VECTOR] * (1 + COLUMN),
        out_specs=(VECTOR, VECTOR, SCALAR),
        scratch_shapes=[pltpu.VMEM((CAP * peers, owned + LANES), BF16)],
    )(me, marks, *bundles)
    new_table, new_state = lax.cond(
        crowded[0] > 0,
        lambda: full_path(table, row_state, relations, touched, source, target, neg_slots),
        lambda: compact_path(
            me, marks, blocks, codes, source_row, target_row, number, rel_hi, rel_lo, across,
            row_state.reshape(1, -1),
        ),
    )
    return new_table.T, new_state.reshape(-1)


def solution(mesh):
    return jax.shard_map(
        per_device,
        mesh=mesh,
        in_specs=(
            P(("grp", "rep"), None),
            P(("grp", "rep")),
            P(),
            P(("grp", "rep"), None),
            P(("grp", "rep")),
            P(("grp", "rep")),
            P(("grp", "rep")),
        ),
        out_specs=(P(("grp", "rep"), None), P(("grp", "rep"))),
        check_vma=False,
    )
```

```python
import functools

import jax
import jax.numpy as jnp
from jax import lax
from jax.experimental import pallas as pl
from jax.experimental.pallas import tpu as pltpu
from jax.sharding import PartitionSpec as P

PRECISE = lax.Precision.HIGHEST
LEARN_RATE = 0.1
EPSILON = 1e-06
LANES = 128
VMEM = 56 * 1024 * 1024
F32 = jnp.float32
BF16 = jnp.bfloat16


def exchange(blocks):
    return lax.all_to_all(blocks, "grp", split_axis=0, concat_axis=0, tiled=True)


def take_rows(rows, ids):
    return jnp.take(rows, ids, axis=0, mode="clip")


def to_lanes(rows, peers):
    width = rows.shape[1]
    wide = -(-width // LANES) * LANES
    return jnp.pad(rows, ((0, 0), (0, wide - width))).reshape(peers, -1, LANES)


def full_path(table, row_state, relations, touched, source, target, neg_slots):
    width = table.shape[1]
    peers, sent = touched.shape
    kinds = relations.shape[0]
    per_rel = source.shape[0] // kinds
    slot_count = peers * sent
    own_count = neg_slots.shape[0]
    neg_total = peers * own_count
    outgoing = take_rows(table, touched.reshape(-1))
    slots = exchange(outgoing.reshape(peers, -1, LANES)).reshape(slot_count, width)
    own_neg = to_lanes(take_rows(slots, neg_slots), 1)
    gathered = exchange(jnp.broadcast_to(own_neg, (peers,) + own_neg.shape[1:]))
    negatives = gathered.reshape(neg_total, -1)[:, :width]
    head = take_rows(slots, source)
    tail = take_rows(slots, target)
    query = jnp.einsum(
        "ked,kdf->kef", head.reshape(kinds, per_rel, width), relations, precision=PRECISE
    ).reshape(kinds * per_rel, width)
    positive = jnp.sum(query * tail, -1)
    negative = jnp.dot(query, negatives.T, precision=PRECISE)
    grad_pos = jax.nn.sigmoid(positive) - 1.0
    grad_neg = jax.nn.sigmoid(negative) / neg_total
    grad_negs = jnp.dot(grad_neg.T, query, precision=PRECISE)
    shares = exchange(to_lanes(grad_negs, peers))
    mine = jnp.sum(shares, 0).reshape(own_count, -1)[:, :width]
    grad_query = grad_pos[:, None] * tail + jnp.dot(grad_neg, negatives, precision=PRECISE)
    grad_tail = grad_pos[:, None] * query
    grad_head = jnp.einsum(
        "kef,kdf->ked", grad_query.reshape(kinds, per_rel, width), relations, precision=PRECISE
    ).reshape(kinds * per_rel, width)
    slot_grad = jnp.zeros((slot_count, width), F32).at[source].add(grad_head)
    slot_grad = slot_grad.at[target].add(grad_tail)
    slot_grad = slot_grad.at[neg_slots].add(mine)
    returned = exchange(slot_grad.reshape(peers, -1, LANES)).reshape(slot_count, width)
    row_grad = jnp.zeros(table.shape, F32).at[touched.reshape(-1)].add(returned)
    new_state = row_state + jnp.mean(row_grad * row_grad, -1)
    new_table = table - LEARN_RATE * row_grad / (jnp.sqrt(new_state)[:, None] + EPSILON)
    return new_table.T, new_state.reshape(1, -1)


CAP = 19
PARTS = 3
TAIL = 16
PER_LINE = LANES // TAIL
LINES = PARTS * CAP
BLOCK = LINES + -(-CAP // PER_LINE)
MAIN = PARTS * LANES
WIDE = MAIN + LANES
COLUMN = 4
DEPTH = 16
SENT = 32
NEG_ROOM = 24
SLOT_ROOM = 8
ROOM = NEG_ROOM + SLOT_ROOM
AT_NEGS = 64
CODE = 2048


def iota(shape, dim):
    return lax.broadcasted_iota(jnp.int32, shape, dim)


def bits(mask):
    return jnp.where(mask, 1.0, 0.0).astype(BF16)


def shift_down(x, by):
    return lax.shift_right_logical(x, jnp.full(x.shape, by, x.dtype))


def same_depth(a, b):
    return lax.bitwise_and(a, DEPTH - 1) == lax.bitwise_and(b, DEPTH - 1)


def grid(condition, size=LANES):
    return bits(condition(iota((size, size), 0), iota((size, size), 1)))


def pieces(x, count):
    out = []
    for _ in range(count):
        piece = x.astype(BF16)
        out.append(piece)
        x = x - piece.astype(F32)
    return out


def dot(a, b, a_dim=1, b_dim=0):
    return lax.dot_general(a, b, (((a_dim,), (b_dim,)), ((), ())), preferred_element_type=F32)


def dot3(a, b, a_dim=1, b_dim=0):
    a_hi, a_lo = a if isinstance(a, tuple) else pieces(a, 2)
    b_hi, b_lo = b if isinstance(b, tuple) else pieces(b, 2)
    small = dot(a_lo, b_hi, a_dim, b_dim) + dot(a_hi, b_lo, a_dim, b_dim)
    return small + dot(a_hi, b_hi, a_dim, b_dim)


def halves(hi, lo):
    lane = iota(hi.shape, 1)
    return jnp.where(lane < LANES // 2, hi.astype(F32), lo.astype(F32)).astype(BF16)


def fold(x):
    return x + pltpu.roll(x, LANES // 2, 1)


def spread(x):
    step = TAIL
    while step < LANES:
        x = x + pltpu.roll(x, step, 1)
        step *= 2
    return x


def call(kernel, outs, **kw):
    return pl.pallas_call(
        kernel,
        out_shape=outs,
        compiler_params=pltpu.CompilerParams(vmem_limit_bytes=VMEM),
        **kw,
    )


def shaped(*shape, dtype=F32):
    return jax.ShapeDtypeStruct(shape, dtype)


VECTOR = pl.BlockSpec(memory_space=pltpu.VMEM)
SCALAR = pl.BlockSpec(memory_space=pltpu.SMEM)


def mark_kernel(negs_ref, source_ref, target_ref, touched_ref, table_ref, out_ref, bundle_ref):
    width = table_ref.shape[0]
    sent, wide = touched_ref.shape
    bundle_ref[:width, :] = table_ref[...]
    bundle_ref[width:, :LANES] = jnp.concatenate(
        [touched_ref[...].astype(F32), jnp.zeros((sent, LANES - wide), F32)], 1
    )
    bundle_ref[width:, LANES:] = jnp.zeros((sent, bundle_ref.shape[1] - LANES), F32)
    peers = out_ref.shape[0] // 2
    ids = jnp.concatenate([source_ref[...], target_ref[...]], 1)
    count = ids.shape[1]
    owner = shift_down(ids, 5)
    within = lax.bitwise_and(ids, SENT - 1)
    at_depth = bits(same_depth(iota((peers, count), 0), owner))
    at_slot = bits(iota((LANES, count), 0) == shift_down(owner, 4) * SENT + within)
    marks = dot(at_depth, at_slot, 1, 1)
    out_ref[pl.ds(0, peers, stride=2), :] = jnp.where(marks > 0.0, 1.0, 0.0)
    at_owner = bits(iota((LANES, count), 0) == owner)
    at_within = bits(iota((SENT, count), 0) == within)
    used = jnp.where(dot(at_within, at_owner, 1, 1) > 0.0, 1.0, 0.0)
    info = jnp.broadcast_to(jnp.sum(used, 0, keepdims=True), marks.shape)
    lane = iota(marks.shape, 1)
    for n in range(negs_ref.shape[0]):
        info = jnp.where(lane == AT_NEGS + n, negs_ref[n].astype(F32), info)
    out_ref[pl.ds(1, peers, stride=2), :] = info


def neg_columns(info, number):
    lane = iota(info.shape, 1)
    columns = []
    for n in range(number):
        column = jnp.sum(jnp.where(lane == AT_NEGS + n, info, 0.0), 1, keepdims=True)
        columns.append(jnp.broadcast_to(column.astype(jnp.int32), info.shape))
    return columns


def before(count):
    return grid(lambda a, b: b < a, count)


def pack(rows, ref):
    peers = ref.shape[0] // BLOCK
    group = iota((peers, LANES), 1) // TAIL
    for part in range(BLOCK - LINES):
        line = jnp.zeros((peers, LANES), F32)
        for k in range(part * PER_LINE, min((part + 1) * PER_LINE, CAP)):
            mine = rows[k * peers : (k + 1) * peers]
            for t in range(PARTS):
                ref[pl.ds(t * CAP + k, peers, stride=BLOCK), :] = mine[:, t * LANES : (t + 1) * LANES]
            line = line + jnp.where(group == k % PER_LINE, mine[:, PARTS * LANES :], 0.0)
        ref[pl.ds(LINES + part, peers, stride=BLOCK), :] = line


def pack_kernel(
    number, me_ref, marks_ref, own_ref, first_ref, second_ref, third_ref, out_ref, codes_ref, flag_ref, onehot
):
    peers = marks_ref.shape[0] // 2
    marks = marks_ref[pl.ds(0, peers, stride=2), :]
    info = marks_ref[pl.ds(1, peers, stride=2), :]
    lane = iota(marks.shape, 1)
    negs = neg_columns(info, number)
    me = me_ref[0]
    depth, up = lax.bitwise_and(me, DEPTH - 1), lax.shift_right_logical(me, jnp.int32(4))
    refs = own_ref, first_ref, second_ref, third_ref
    width, owned = own_ref.shape[0] - SENT, own_ref.shape[1]

    touched = jnp.zeros(marks.shape, F32)
    for d, ref in enumerate(refs):
        rows = jnp.concatenate([ref[width:, :LANES], jnp.zeros((LANES - SENT, LANES), F32)], 0)
        rows = jnp.where(lane < SENT, rows.T[:peers] + (d * owned + 1.0), 0.0)
        touched = touched + pltpu.roll(rows, SENT * lax.bitwise_xor(up, jnp.int32(d)), 1)

    earlier = jnp.zeros((1, LANES), F32)
    neg_rows = jnp.zeros((1, LANES), F32)
    for slot in negs:
        owner = shift_down(slot, 5)
        at = jnp.where(lane == owner, 1.0, 0.0)
        rank = jnp.sum((dot(before(peers), at.astype(BF16)) + earlier) * at, 1, keepdims=True)
        earlier = earlier + jnp.sum(at, 0, keepdims=True)
        base = shift_down(owner, 4) * SENT
        at_row = lane == base + lax.bitwise_and(slot, SENT - 1)
        row = jnp.sum(jnp.where(at_row, touched, 0.0), 1, keepdims=True)
        here = same_depth(owner, depth) & (lane == base + rank.astype(jnp.int32))
        neg_rows = neg_rows + jnp.sum(jnp.where(here, row, 0.0), 0, keepdims=True)

    slots = jnp.where(lane < peers, info, 0.0)
    column = grid(same_depth)
    over_slots = jnp.sum(jnp.maximum(slots - CAP, 0.0), 0, keepdims=True)
    first = iota((PER_LINE, LANES), 0) == 0
    sums = jnp.where(first, earlier, over_slots).astype(BF16)
    sums = jnp.max(dot(sums, column) - jnp.where(first, NEG_ROOM, SLOT_ROOM))
    total = jnp.max(dot((slots + earlier).astype(BF16), column))
    over = (total > COLUMN * CAP) | (sums > 0.0)
    flag_ref[0] = over.astype(jnp.int32)

    neg_rows = jnp.broadcast_to(neg_rows, marks.shape)
    neg_marks = jnp.where(neg_rows > 0.0, 1.0, 0.0)
    block = grid(lambda a, b: a // SENT == b // SENT)
    earlier_block = grid(lambda a, b: (a % SENT == 0) & (a // SENT < b // SENT))
    rank = dot(marks.astype(BF16), grid(lambda a, b: (a // SENT == b // SENT) & (a <= b)))
    used = dot(marks.astype(BF16), block)
    neg_rank = used + (lane % SENT).astype(F32) + 1.0
    need = used + dot(neg_marks.astype(BF16), block)
    spare = jnp.maximum(CAP - need, 0.0)
    excess_from = dot(jnp.maximum(need - CAP, 0.0).astype(BF16), earlier_block)
    spare_from = dot(spare.astype(BF16), earlier_block)
    own = lane // SENT == up

    def mine(x):
        return jnp.sum(jnp.where(lane == SENT * up, x, 0.0), 1, keepdims=True)

    need, spare, spare_from = mine(need), mine(spare), mine(spare_from)

    def placed(rank, mask):
        x = excess_from + rank - (CAP + 1.0) - spare_from
        helped = jnp.where((rank > CAP) & (x >= 0.0) & (x < spare), need + x, -1.0)
        at = jnp.where(own, jnp.where(rank <= CAP, rank - 1.0, -1.0), helped)
        return jnp.where(mask > 0.0, at, -1.0)

    place, neg_place = placed(rank, marks), placed(neg_rank, neg_marks)
    upto = grid(lambda a, b: a <= b)
    helped = jnp.where((place >= 0.0) & ~own, 1.0, 0.0)
    held = jnp.broadcast_to(jnp.sum(helped, 1, keepdims=True), marks.shape)
    entry = dot(before(peers), held.astype(BF16)) + dot(helped.astype(BF16), upto)
    codes = touched + CODE * jnp.where(helped > 0.0, entry + NEG_ROOM, 0.0)
    neg_entry = dot(neg_marks.astype(BF16), upto)
    neg_codes = neg_rows + CODE * jnp.where((neg_place >= 0.0) & ~own, neg_entry, 0.0)

    mates = len(refs) - 1
    column = iota((SLOT_ROOM, LANES), 0)
    of_slots = jnp.zeros((SLOT_ROOM, LANES), F32)
    for e in range(SLOT_ROOM):
        row = jnp.sum(jnp.where((helped > 0.0) & (entry == e + 1.0), touched, 0.0), 0, keepdims=True)
        of_slots = jnp.where(column == e, row, of_slots)
    column = iota((NEG_ROOM, LANES), 0)
    of_negs = jnp.where((neg_entry[:1] == column + 1.0) & (neg_marks[:1] > 0.0), neg_rows[:1], 0.0)
    row = jnp.sum(jnp.concatenate([of_negs, of_slots], 0), 1, keepdims=True).astype(jnp.int32)
    from_mates = bits(iota((ROOM, mates * owned), 1) == row - (owned + 1))

    spot = iota((peers, owned + LANES), 1)
    out = jnp.zeros(marks.shape, jnp.int32)
    for k in range(CAP):
        code = jnp.where(place == k, codes, 0.0) + jnp.where(neg_place == k, neg_codes, 0.0)
        code = jnp.sum(code, 1, keepdims=True).astype(jnp.int32)
        out = jnp.where(lane == k, code, out)
        helping = shift_down(code, 11)
        own_row = lax.bitwise_and(code, CODE - 1) - 1
        at = jnp.where(helping > 0, owned - 1 + helping, own_row)
        onehot[k * peers : (k + 1) * peers, :] = bits(spot == at)
    codes_ref[...] = out

    hi, lo = pieces(jnp.concatenate([ref[:width] for ref in refs], 1), 2)
    tails = [hi[MAIN:]] * (PER_LINE // 2) + [lo[MAIN:]] * (PER_LINE // 2)
    hi, lo = jnp.concatenate([hi[:MAIN]] + tails, 0), lo[:MAIN]

    def joined(of_hi, of_lo):
        return jnp.concatenate([of_hi[:, :MAIN] + of_lo, fold(of_hi[:, MAIN:])], 1)

    held = joined(dot(from_mates, hi[:, owned:], 1, 1), dot(from_mates, lo[:, owned:], 1, 1))
    held = jnp.concatenate([held, jnp.zeros((LANES - ROOM, WIDE), F32)], 0)
    held_hi, held_lo = pieces(held, 2)
    held_hi = jnp.concatenate([held_hi[:, :MAIN], halves(held_hi[:, MAIN:], held_lo[:, MAIN:])], 1)
    held_lo = held_lo[:, :MAIN]
    own, other = onehot[:, :owned], onehot[:, owned:]
    got = joined(
        dot(own, hi[:, :owned], 1, 1) + dot(other, held_hi),
        dot(own, lo[:, :owned], 1, 1) + dot(other, held_lo),
    )
    pack(got, out_ref)


def place_kernel(number, marks_ref, source_ref, target_ref, edge_ref, neg_ref):
    peers = marks_ref.shape[0] // 2
    info = marks_ref[pl.ds(1, peers, stride=2), :]
    ids = jnp.concatenate([source_ref[...], target_ref[...]], 1)
    count = ids.shape[1]
    owner = shift_down(ids, 5)
    at_owner = bits(iota((LANES, count), 0) == owner)
    at_within = bits(iota((SENT, count), 0) == lax.bitwise_and(ids, SENT - 1))
    used = bits(dot(at_within, at_owner, 1, 1) > 0.0)
    rank = dot(grid(lambda a, b: b <= a, SENT), used)
    from_edges = rank[SENT - 1 :]
    lane = iota(info.shape, 1)
    negs = [shift_down(slot, 5) for slot in neg_columns(info, number)]
    at_neg = [jnp.where(lane == slot, 1.0, 0.0) for slot in negs]
    need = from_edges
    for at in at_neg:
        need = need + jnp.sum(at, 0, keepdims=True)

    line = iota((PER_LINE, LANES), 0)
    spare = jnp.maximum(CAP - need, 0.0)
    excess = jnp.maximum(need - CAP, 0.0)
    first = jnp.where(line == 0, need, jnp.where(line == 1, spare, jnp.where(line == 2, excess, 0.0)))
    first = first.astype(BF16)
    earlier = dot(first, grid(lambda a, b: same_depth(a, b) & (a // DEPTH < b // DEPTH)))
    excess_from = earlier[2:3]
    first = jnp.where(line == 2, jnp.broadcast_to(earlier[1:2], first.shape), first.astype(F32))
    first = first.astype(BF16)
    mates = [
        dot(first, grid(lambda a, b: same_depth(a, b) & (a // DEPTH == y))) for y in range(COLUMN)
    ]

    def placed(owner, order, value):
        owner = owner.astype(F32)
        depth = owner - DEPTH * jnp.floor(owner / DEPTH)
        place = order * peers + owner
        x = value(excess_from) + order - CAP
        for y, mate in enumerate(mates):
            need, spare, start = (value(mate[i : i + 1]) for i in range(3))
            here = (order >= CAP) & (x >= start) & (x < start + spare)
            place = jnp.where(here, (need + x - start) * peers + y * DEPTH + depth, place)
        return place.astype(jnp.int32)

    def at_edges(row):
        row = jnp.broadcast_to(row, (PER_LINE, LANES)).astype(BF16)
        return dot(row, at_owner)[:1]

    order = jnp.sum(dot(rank.astype(BF16), at_owner) * at_within.astype(F32), 0, keepdims=True)
    edge_ref[...] = placed(owner, order - 1.0, at_edges)
    for n, at in enumerate(at_neg):
        order = dot(before(peers), at.astype(BF16)) + from_edges
        order = jnp.sum(order * at, 1, keepdims=True)

        def at_these(row):
            return jnp.sum(row * at, 1, keepdims=True)

        neg_ref[n * peers : (n + 1) * peers, :] = placed(negs[n][:, :1], order, at_these)
        from_edges = from_edges + jnp.sum(at, 0, keepdims=True)


def unpack(ref, hi_ref, lo_ref):
    peers = ref.shape[0] // BLOCK
    group = iota((peers, LANES), 1) // TAIL
    for k in range(CAP):
        span = slice(k * peers, (k + 1) * peers)
        for t in range(PARTS):
            hi, lo = pieces(ref[pl.ds(t * CAP + k, peers, stride=BLOCK), :], 2)
            hi_ref[span, t * LANES : (t + 1) * LANES] = hi
            lo_ref[span, t * LANES : (t + 1) * LANES] = lo
        tails = ref[pl.ds(LINES + k // PER_LINE, peers, stride=BLOCK), :]
        hi, lo = pieces(jnp.where(group == k % PER_LINE, tails, 0.0), 2)
        both = hi.astype(F32) + pltpu.roll(lo.astype(F32), LANES // 2, 1)
        hi_ref[span, MAIN:] = both.astype(BF16)


def gathered(chosen, hi_ref, lo_ref):
    of_hi = dot(chosen, hi_ref[...])
    return of_hi[:, :MAIN] + dot(chosen, lo_ref[...]), spread(of_hi[:, MAIN:])


def edges_kernel(
    block_ref, place_ref, neg_place_ref, row_place_ref, rel_hi_ref, rel_lo_ref,
    out_ref, slots_hi, slots_lo, grad_hi, grad_lo,
):
    peers = block_ref.shape[0] // BLOCK
    edges = place_ref.shape[0] // 2
    total = neg_place_ref.shape[0]
    kinds = rel_hi_ref.shape[0]
    per_rel = edges // kinds
    count = peers * CAP
    unpack(block_ref, slots_hi, slots_lo)

    spot = jnp.concatenate([place_ref[...], neg_place_ref[...]], 0)
    chosen = bits(iota((spot.shape[0], count), 1) == spot)
    got = jnp.concatenate(gathered(chosen, slots_hi, slots_lo), 1)

    def keep(start, grad):
        span = slice(start, start + grad.shape[0])
        grad_hi[span, :MAIN], grad_lo[span, :] = pieces(grad[:, :MAIN], 2)
        grad_hi[span, MAIN:] = halves(*pieces(spread(grad[:, MAIN:]), 2))

    negs = tuple(pieces(got[2 * edges :], 2))
    shares = jnp.zeros((total, WIDE), F32)
    for kind in range(kinds):
        start = kind * per_rel
        relation = rel_hi_ref[kind], rel_lo_ref[kind]
        query = dot3(got[start : start + per_rel], relation)
        tail = got[edges + start : edges + start + per_rel]
        positive = jnp.sum(query * tail, 1, keepdims=True)
        grad_pos = jax.nn.sigmoid(positive) - 1.0
        keep(edges + start, grad_pos * query)
        query = tuple(pieces(query, 2))
        grad_neg = jax.nn.sigmoid(dot3(query, negs, 1, 1)) / total
        grad_query = grad_pos * tail + dot3(grad_neg, negs)
        keep(start, dot3(grad_query, relation, 1, 1))
        grad_neg = jax.nn.sigmoid(dot3(negs, query, 1, 1)) / total
        shares = shares + dot3(grad_neg, query)
    keep(2 * edges, shares)

    spot = row_place_ref[...]
    chosen = bits(iota((count, spot.shape[1]), 0) == spot)
    of_hi = dot(chosen, grad_hi[...])
    of_main = of_hi[:, :MAIN] + dot(chosen, grad_lo[...])
    pack(jnp.concatenate([of_main, fold(of_hi[:, MAIN:])], 1), out_ref)


def sum_kernel(block_ref, code_ref, list_ref, own_ref, hi_ref, lo_ref):
    unpack(block_ref, hi_ref, lo_ref)
    code = code_ref[...]
    row = lax.bitwise_and(code, CODE - 1) - 1
    entry = shift_down(code, 11) - 1
    listed = iota((ROOM, code.shape[1]), 0) == entry
    number = jnp.max(jnp.where(listed, row.astype(F32), -1.0), 1, keepdims=True)
    mine = iota((own_ref.shape[0], code.shape[1]), 0) == row
    chosen = jnp.concatenate([jnp.where(mine, 1.0, 0.0), jnp.where(listed, 1.0, 0.0)], 0)
    main, tails = gathered(chosen.astype(BF16), hi_ref, lo_ref)
    owned = own_ref.shape[0]
    own_ref[...] = jnp.concatenate([main[:owned], tails[:owned]], 1)
    tails = tails[owned:]
    tails = jnp.where(iota(tails.shape, 1) < TAIL, tails, number)
    for y in range(COLUMN):
        list_ref[y] = jnp.concatenate([main[owned:], tails], 1)


def update_kernel(me_ref, own_ref, lists_ref, table_ref, state_ref, new_table_ref, new_state_ref):
    width, owned = table_ref.shape
    rows = lists_ref[...].reshape(-1, WIDE)
    up = lax.shift_right_logical(me_ref[0], jnp.int32(4))
    mate = iota((rows.shape[0], 1), 0) // ROOM
    first = lax.bitwise_xor(mate, jnp.broadcast_to(up, mate.shape)) * owned
    at = rows[:, WIDE - 1 :].astype(jnp.int32) - first
    chosen = bits(iota((rows.shape[0], owned), 1) == at)
    hi, lo = pieces(rows, 2)
    grad = own_ref[...] + (dot(chosen, lo, 0, 0) + dot(chosen, hi, 0, 0))
    grad = grad.T[:width]
    state = state_ref[...] + jnp.sum(grad * grad, 0, keepdims=True) / width
    new_state_ref[...] = state
    new_table_ref[...] = table_ref[...] - LEARN_RATE * grad / (jnp.sqrt(state) + EPSILON)


def to_mates(x):
    peers = lax.axis_size("grp")
    return [
        lax.ppermute(x, "grp", [(p, p ^ (d * DEPTH)) for p in range(peers)])
        for d in range(1, COLUMN)
    ]


def exchange_blocks(blocks):
    peers = lax.axis_size("grp")
    return exchange(blocks.reshape(peers, BLOCK, 1, LANES)).reshape(blocks.shape)


def compact_path(me, marks, blocks, codes, source, target, number, rel_hi, rel_lo, table, state):
    peers = marks.shape[0] // 2
    edges = source.shape[1]
    width, owned = table.shape
    count = peers * CAP
    split = [pltpu.VMEM((count, WIDE), BF16), pltpu.VMEM((count, MAIN), BF16)]
    blocks = exchange_blocks(blocks)
    edge_place, neg_place = call(
        functools.partial(place_kernel, number),
        (shaped(1, 2 * edges, dtype=jnp.int32), shaped(peers * number, 1, dtype=jnp.int32)),
    )(marks, source, target)
    row_place = jnp.concatenate([edge_place, neg_place.reshape(1, -1)], 1)
    grads = call(
        edges_kernel,
        shaped(*blocks.shape),
        scratch_shapes=split
        + [pltpu.VMEM((row_place.shape[1], size), BF16) for size in (WIDE, MAIN)],
    )(blocks, edge_place.reshape(-1, 1), neg_place, row_place, rel_hi, rel_lo)
    returned = exchange_blocks(grads)
    codes = codes[:, :CAP].T.reshape(1, -1)
    lists, own = call(
        sum_kernel,
        (shaped(COLUMN, ROOM, WIDE), shaped(owned, WIDE)),
        scratch_shapes=split,
    )(returned, codes)
    lists = lax.all_to_all(
        lists, "grp", 0, 0, tiled=True,
        axis_index_groups=[list(range(z, peers, DEPTH)) for z in range(DEPTH)],
    )
    return call(
        update_kernel,
        (shaped(width, owned), shaped(1, owned)),
        in_specs=[SCALAR] + [VECTOR] * 4,
    )(me, own, lists, table, state)


def per_device(table, row_state, relations, touched, source, target, neg_slots):
    peers, sent = touched.shape
    owned, width = table.shape
    number = neg_slots.shape[0]
    across = table.T
    source_row, target_row = source.reshape(1, -1), target.reshape(1, -1)
    marks, bundle = call(
        mark_kernel,
        (shaped(2 * peers, LANES), shaped(width + sent, owned)),
        in_specs=[SCALAR] + [VECTOR] * 4,
        out_specs=(VECTOR, VECTOR),
    )(neg_slots, source_row, target_row, touched.T, across)
    marks = exchange(marks.reshape(peers, 2, 1, LANES)).reshape(2 * peers, LANES)
    bundles = [bundle] + to_mates(bundle)
    wide = jnp.pad(relations, ((0, 0), (0, WIDE - width), (0, WIDE - width)))
    rel_hi = lax.reduce_precision(wide, 8, 7)
    rel_lo = (wide - rel_hi).astype(BF16)
    rel_hi = rel_hi.astype(BF16)
    me = lax.axis_index("grp").reshape(1)
    blocks, codes, crowded = call(
        functools.partial(pack_kernel, number),
        (
            shaped(peers * BLOCK, LANES),
            shaped(peers, LANES, dtype=jnp.int32),
            shaped(1, dtype=jnp.int32),
        ),
        in_specs=[SCALAR] + [VECTOR] * (1 + COLUMN),
        out_specs=(VECTOR, VECTOR, SCALAR),
        scratch_shapes=[pltpu.VMEM((CAP * peers, owned + LANES), BF16)],
    )(me, marks, *bundles)
    new_table, new_state = lax.cond(
        crowded[0] > 0,
        lambda: full_path(table, row_state, relations, touched, source, target, neg_slots),
        lambda: compact_path(
            me, marks, blocks, codes, source_row, target_row, number, rel_hi, rel_lo, across,
            row_state.reshape(1, -1),
        ),
    )
    return new_table.T, new_state.reshape(-1)


def solution(mesh):
    return jax.shard_map(
        per_device,
        mesh=mesh,
        in_specs=(
            P(("grp", "rep"), None),
            P(("grp", "rep")),
            P(),
            P(("grp", "rep"), None),
            P(("grp", "rep")),
            P(("grp", "rep")),
            P(("grp", "rep")),
        ),
        out_specs=(P(("grp", "rep"), None), P(("grp", "rep"))),
        check_vma=False,
    )
```

```python
import functools

import jax
import jax.numpy as jnp
from jax import lax
from jax.experimental import pallas as pl
from jax.experimental.pallas import tpu as pltpu
from jax.sharding import PartitionSpec as P

PRECISE = lax.Precision.HIGHEST
LEARN_RATE = 0.1
EPSILON = 1e-06
LANES = 128
VMEM = 56 * 1024 * 1024
F32 = jnp.float32
BF16 = jnp.bfloat16


def exchange(blocks):
    return lax.all_to_all(blocks, "grp", split_axis=0, concat_axis=0, tiled=True)


def take_rows(rows, ids):
    return jnp.take(rows, ids, axis=0, mode="clip")


def to_lanes(rows, peers):
    width = rows.shape[1]
    wide = -(-width // LANES) * LANES
    return jnp.pad(rows, ((0, 0), (0, wide - width))).reshape(peers, -1, LANES)


def full_path(table, row_state, relations, touched, source, target, neg_slots):
    width = table.shape[1]
    peers, sent = touched.shape
    kinds = relations.shape[0]
    per_rel = source.shape[0] // kinds
    slot_count = peers * sent
    own_count = neg_slots.shape[0]
    neg_total = peers * own_count
    outgoing = take_rows(table, touched.reshape(-1))
    slots = exchange(outgoing.reshape(peers, -1, LANES)).reshape(slot_count, width)
    own_neg = to_lanes(take_rows(slots, neg_slots), 1)
    gathered = exchange(jnp.broadcast_to(own_neg, (peers,) + own_neg.shape[1:]))
    negatives = gathered.reshape(neg_total, -1)[:, :width]
    head = take_rows(slots, source)
    tail = take_rows(slots, target)
    query = jnp.einsum(
        "ked,kdf->kef", head.reshape(kinds, per_rel, width), relations, precision=PRECISE
    ).reshape(kinds * per_rel, width)
    positive = jnp.sum(query * tail, -1)
    negative = jnp.dot(query, negatives.T, precision=PRECISE)
    grad_pos = jax.nn.sigmoid(positive) - 1.0
    grad_neg = jax.nn.sigmoid(negative) / neg_total
    grad_negs = jnp.dot(grad_neg.T, query, precision=PRECISE)
    shares = exchange(to_lanes(grad_negs, peers))
    mine = jnp.sum(shares, 0).reshape(own_count, -1)[:, :width]
    grad_query = grad_pos[:, None] * tail + jnp.dot(grad_neg, negatives, precision=PRECISE)
    grad_tail = grad_pos[:, None] * query
    grad_head = jnp.einsum(
        "kef,kdf->ked", grad_query.reshape(kinds, per_rel, width), relations, precision=PRECISE
    ).reshape(kinds * per_rel, width)
    slot_grad = jnp.zeros((slot_count, width), F32).at[source].add(grad_head)
    slot_grad = slot_grad.at[target].add(grad_tail)
    slot_grad = slot_grad.at[neg_slots].add(mine)
    returned = exchange(slot_grad.reshape(peers, -1, LANES)).reshape(slot_count, width)
    row_grad = jnp.zeros(table.shape, F32).at[touched.reshape(-1)].add(returned)
    new_state = row_state + jnp.mean(row_grad * row_grad, -1)
    new_table = table - LEARN_RATE * row_grad / (jnp.sqrt(new_state)[:, None] + EPSILON)
    return new_table.T, new_state.reshape(1, -1)


CAP = 19
PARTS = 3
TAIL = 16
PER_LINE = LANES // TAIL
LINES = PARTS * CAP
BLOCK = LINES + -(-CAP // PER_LINE)
MAIN = PARTS * LANES
WIDE = MAIN + LANES
COLUMN = 4
DEPTH = 16
SENT = 32
NEG_ROOM = 24
SLOT_ROOM = 8
ROOM = NEG_ROOM + SLOT_ROOM
AT_NEGS = 64
CODE = 2048


def iota(shape, dim):
    return lax.broadcasted_iota(jnp.int32, shape, dim)


def bits(mask):
    return jnp.where(mask, 1.0, 0.0).astype(BF16)


def shift_down(x, by):
    return lax.shift_right_logical(x, jnp.full(x.shape, by, x.dtype))


def same_depth(a, b):
    return lax.bitwise_and(a, DEPTH - 1) == lax.bitwise_and(b, DEPTH - 1)


def grid(condition, size=LANES):
    return bits(condition(iota((size, size), 0), iota((size, size), 1)))


def pieces(x, count):
    out = []
    for _ in range(count):
        piece = x.astype(BF16)
        out.append(piece)
        x = x - piece.astype(F32)
    return out


def dot(a, b, a_dim=1, b_dim=0):
    return lax.dot_general(a, b, (((a_dim,), (b_dim,)), ((), ())), preferred_element_type=F32)


def dot3(a, b, a_dim=1, b_dim=0):
    a_hi, a_lo = a if isinstance(a, tuple) else pieces(a, 2)
    b_hi, b_lo = b if isinstance(b, tuple) else pieces(b, 2)
    rows = a_hi.shape[0]
    both = dot(jnp.concatenate([a_lo, a_hi], 0), b_hi, a_dim, b_dim)
    return both[:rows] + dot(a_hi, b_lo, a_dim, b_dim) + both[rows:]


def halves(hi, lo):
    lane = iota(hi.shape, 1)
    return jnp.where(lane < LANES // 2, hi.astype(F32), lo.astype(F32)).astype(BF16)


def fold(x):
    return x + pltpu.roll(x, LANES // 2, 1)


def spread(x):
    step = TAIL
    while step < LANES:
        x = x + pltpu.roll(x, step, 1)
        step *= 2
    return x


def call(kernel, outs, **kw):
    return pl.pallas_call(
        kernel,
        out_shape=outs,
        compiler_params=pltpu.CompilerParams(vmem_limit_bytes=VMEM),
        **kw,
    )


def shaped(*shape, dtype=F32):
    return jax.ShapeDtypeStruct(shape, dtype)


VECTOR = pl.BlockSpec(memory_space=pltpu.VMEM)
SCALAR = pl.BlockSpec(memory_space=pltpu.SMEM)


def mark_kernel(negs_ref, source_ref, target_ref, touched_ref, table_ref, out_ref, bundle_ref):
    width = table_ref.shape[0]
    sent, wide = touched_ref.shape
    bundle_ref[:width, :] = table_ref[...]
    bundle_ref[width:, :LANES] = jnp.concatenate(
        [touched_ref[...].astype(F32), jnp.zeros((sent, LANES - wide), F32)], 1
    )
    bundle_ref[width:, LANES:] = jnp.zeros((sent, bundle_ref.shape[1] - LANES), F32)
    peers = out_ref.shape[0] // 2
    ids = jnp.concatenate([source_ref[...], target_ref[...]], 1)
    count = ids.shape[1]
    owner = shift_down(ids, 5)
    within = lax.bitwise_and(ids, SENT - 1)
    at_depth = bits(same_depth(iota((peers, count), 0), owner))
    at_slot = bits(iota((LANES, count), 0) == shift_down(owner, 4) * SENT + within)
    marks = dot(at_depth, at_slot, 1, 1)
    out_ref[pl.ds(0, peers, stride=2), :] = jnp.where(marks > 0.0, 1.0, 0.0)
    at_owner = bits(iota((LANES, count), 0) == owner)
    at_within = bits(iota((SENT, count), 0) == within)
    used = jnp.where(dot(at_within, at_owner, 1, 1) > 0.0, 1.0, 0.0)
    info = jnp.broadcast_to(jnp.sum(used, 0, keepdims=True), marks.shape)
    lane = iota(marks.shape, 1)
    for n in range(negs_ref.shape[0]):
        info = jnp.where(lane == AT_NEGS + n, negs_ref[n].astype(F32), info)
    out_ref[pl.ds(1, peers, stride=2), :] = info


def neg_columns(info, number):
    lane = iota(info.shape, 1)
    columns = []
    for n in range(number):
        column = jnp.sum(jnp.where(lane == AT_NEGS + n, info, 0.0), 1, keepdims=True)
        columns.append(jnp.broadcast_to(column.astype(jnp.int32), info.shape))
    return columns


def before(count):
    return grid(lambda a, b: b < a, count)


def pack(rows, ref):
    peers = ref.shape[0] // BLOCK
    group = iota((peers, LANES), 1) // TAIL
    for part in range(BLOCK - LINES):
        line = jnp.zeros((peers, LANES), F32)
        for k in range(part * PER_LINE, min((part + 1) * PER_LINE, CAP)):
            mine = rows[k * peers : (k + 1) * peers]
            for t in range(PARTS):
                ref[pl.ds(t * CAP + k, peers, stride=BLOCK), :] = mine[:, t * LANES : (t + 1) * LANES]
            line = line + jnp.where(group == k % PER_LINE, mine[:, PARTS * LANES :], 0.0)
        ref[pl.ds(LINES + part, peers, stride=BLOCK), :] = line


def pack_kernel(
    number, me_ref, marks_ref, own_ref, first_ref, second_ref, third_ref, out_ref, codes_ref, flag_ref, onehot
):
    peers = marks_ref.shape[0] // 2
    marks = marks_ref[pl.ds(0, peers, stride=2), :]
    info = marks_ref[pl.ds(1, peers, stride=2), :]
    lane = iota(marks.shape, 1)
    negs = neg_columns(info, number)
    me = me_ref[0]
    depth, up = lax.bitwise_and(me, DEPTH - 1), lax.shift_right_logical(me, jnp.int32(4))
    refs = own_ref, first_ref, second_ref, third_ref
    width, owned = own_ref.shape[0] - SENT, own_ref.shape[1]

    touched = jnp.zeros(marks.shape, F32)
    for d, ref in enumerate(refs):
        rows = jnp.concatenate([ref[width:, :LANES], jnp.zeros((LANES - SENT, LANES), F32)], 0)
        rows = jnp.where(lane < SENT, rows.T[:peers] + (d * owned + 1.0), 0.0)
        touched = touched + pltpu.roll(rows, SENT * lax.bitwise_xor(up, jnp.int32(d)), 1)

    earlier = jnp.zeros((1, LANES), F32)
    neg_rows = jnp.zeros((1, LANES), F32)
    for slot in negs:
        owner = shift_down(slot, 5)
        at = jnp.where(lane == owner, 1.0, 0.0)
        rank = jnp.sum((dot(before(peers), at.astype(BF16)) + earlier) * at, 1, keepdims=True)
        earlier = earlier + jnp.sum(at, 0, keepdims=True)
        base = shift_down(owner, 4) * SENT
        at_row = lane == base + lax.bitwise_and(slot, SENT - 1)
        row = jnp.sum(jnp.where(at_row, touched, 0.0), 1, keepdims=True)
        here = same_depth(owner, depth) & (lane == base + rank.astype(jnp.int32))
        neg_rows = neg_rows + jnp.sum(jnp.where(here, row, 0.0), 0, keepdims=True)

    slots = jnp.where(lane < peers, info, 0.0)
    column = grid(same_depth)
    over_slots = jnp.sum(jnp.maximum(slots - CAP, 0.0), 0, keepdims=True)
    first = iota((PER_LINE, LANES), 0) == 0
    sums = jnp.where(first, earlier, over_slots).astype(BF16)
    sums = jnp.max(dot(sums, column) - jnp.where(first, NEG_ROOM, SLOT_ROOM))
    total = jnp.max(dot((slots + earlier).astype(BF16), column))
    over = (total > COLUMN * CAP) | (sums > 0.0)
    flag_ref[0] = over.astype(jnp.int32)

    neg_rows = jnp.broadcast_to(neg_rows, marks.shape)
    neg_marks = jnp.where(neg_rows > 0.0, 1.0, 0.0)
    block = grid(lambda a, b: a // SENT == b // SENT)
    earlier_block = grid(lambda a, b: (a % SENT == 0) & (a // SENT < b // SENT))
    rank = dot(marks.astype(BF16), grid(lambda a, b: (a // SENT == b // SENT) & (a <= b)))
    used = dot(marks.astype(BF16), block)
    neg_rank = used + (lane % SENT).astype(F32) + 1.0
    need = used + dot(neg_marks.astype(BF16), block)
    spare = jnp.maximum(CAP - need, 0.0)
    excess_from = dot(jnp.maximum(need - CAP, 0.0).astype(BF16), earlier_block)
    spare_from = dot(spare.astype(BF16), earlier_block)
    own = lane // SENT == up

    def mine(x):
        return jnp.sum(jnp.where(lane == SENT * up, x, 0.0), 1, keepdims=True)

    need, spare, spare_from = mine(need), mine(spare), mine(spare_from)

    def placed(rank, mask):
        x = excess_from + rank - (CAP + 1.0) - spare_from
        helped = jnp.where((rank > CAP) & (x >= 0.0) & (x < spare), need + x, -1.0)
        at = jnp.where(own, jnp.where(rank <= CAP, rank - 1.0, -1.0), helped)
        return jnp.where(mask > 0.0, at, -1.0)

    place, neg_place = placed(rank, marks), placed(neg_rank, neg_marks)
    upto = grid(lambda a, b: a <= b)
    helped = jnp.where((place >= 0.0) & ~own, 1.0, 0.0)
    held = jnp.broadcast_to(jnp.sum(helped, 1, keepdims=True), marks.shape)
    entry = dot(before(peers), held.astype(BF16)) + dot(helped.astype(BF16), upto)
    codes = touched + CODE * jnp.where(helped > 0.0, entry + NEG_ROOM, 0.0)
    neg_entry = dot(neg_marks.astype(BF16), upto)
    neg_codes = neg_rows + CODE * jnp.where((neg_place >= 0.0) & ~own, neg_entry, 0.0)

    mates = len(refs) - 1
    column = iota((SLOT_ROOM, LANES), 0)
    of_slots = jnp.zeros((SLOT_ROOM, LANES), F32)
    for e in range(SLOT_ROOM):
        row = jnp.sum(jnp.where((helped > 0.0) & (entry == e + 1.0), touched, 0.0), 0, keepdims=True)
        of_slots = jnp.where(column == e, row, of_slots)
    column = iota((NEG_ROOM, LANES), 0)
    of_negs = jnp.where((neg_entry[:1] == column + 1.0) & (neg_marks[:1] > 0.0), neg_rows[:1], 0.0)
    row = jnp.sum(jnp.concatenate([of_negs, of_slots], 0), 1, keepdims=True).astype(jnp.int32)
    from_mates = bits(iota((ROOM, mates * owned), 1) == row - (owned + 1))

    spot = iota((peers, owned + LANES), 1)
    out = jnp.zeros(marks.shape, jnp.int32)
    for k in range(CAP):
        code = jnp.where(place == k, codes, 0.0) + jnp.where(neg_place == k, neg_codes, 0.0)
        code = jnp.sum(code, 1, keepdims=True).astype(jnp.int32)
        out = jnp.where(lane == k, code, out)
        helping = shift_down(code, 11)
        own_row = lax.bitwise_and(code, CODE - 1) - 1
        at = jnp.where(helping > 0, owned - 1 + helping, own_row)
        onehot[k * peers : (k + 1) * peers, :] = bits(spot == at)
    codes_ref[...] = out

    def split(rows):
        hi, lo = pieces(rows, 2)
        return jnp.concatenate([hi[:, :MAIN], halves(hi[:, MAIN:], lo[:, MAIN:])], 1), lo[:, :MAIN]

    def fetched(chosen, hi, lo):
        of_hi = dot(chosen, hi)
        return jnp.concatenate([of_hi[:, :MAIN] + dot(chosen, lo), fold(of_hi[:, MAIN:])], 1)

    tables = [jnp.concatenate([ref[:MAIN]] + [ref[MAIN:width]] * PER_LINE, 0).T for ref in refs]
    held = fetched(from_mates, *split(jnp.concatenate(tables[1:], 0)))
    held = jnp.concatenate([tables[0], held, jnp.zeros((LANES - ROOM, WIDE), F32)], 0)
    got = fetched(onehot[...], *split(held))
    pack(got, out_ref)


def place_kernel(number, marks_ref, source_ref, target_ref, edge_ref, neg_ref):
    peers = marks_ref.shape[0] // 2
    info = marks_ref[pl.ds(1, peers, stride=2), :]
    ids = jnp.concatenate([source_ref[...], target_ref[...]], 1)
    count = ids.shape[1]
    owner = shift_down(ids, 5)
    at_owner = bits(iota((LANES, count), 0) == owner)
    at_within = bits(iota((SENT, count), 0) == lax.bitwise_and(ids, SENT - 1))
    used = bits(dot(at_within, at_owner, 1, 1) > 0.0)
    rank = dot(grid(lambda a, b: b <= a, SENT), used)
    from_edges = rank[SENT - 1 :]
    lane = iota(info.shape, 1)
    negs = [shift_down(slot, 5) for slot in neg_columns(info, number)]
    at_neg = [jnp.where(lane == slot, 1.0, 0.0) for slot in negs]
    need = from_edges
    for at in at_neg:
        need = need + jnp.sum(at, 0, keepdims=True)

    line = iota((PER_LINE, LANES), 0)
    spare = jnp.maximum(CAP - need, 0.0)
    excess = jnp.maximum(need - CAP, 0.0)
    first = jnp.where(line == 0, need, jnp.where(line == 1, spare, jnp.where(line == 2, excess, 0.0)))
    first = first.astype(BF16)
    earlier = dot(first, grid(lambda a, b: same_depth(a, b) & (a // DEPTH < b // DEPTH)))
    excess_from = earlier[2:3]
    first = jnp.where(line == 2, jnp.broadcast_to(earlier[1:2], first.shape), first.astype(F32))
    first = first.astype(BF16)
    mates = [
        dot(first, grid(lambda a, b: same_depth(a, b) & (a // DEPTH == y))) for y in range(COLUMN)
    ]

    def placed(owner, order, value):
        owner = owner.astype(F32)
        depth = owner - DEPTH * jnp.floor(owner / DEPTH)
        place = order * peers + owner
        x = value(excess_from) + order - CAP
        for y, mate in enumerate(mates):
            need, spare, start = (value(mate[i : i + 1]) for i in range(3))
            here = (order >= CAP) & (x >= start) & (x < start + spare)
            place = jnp.where(here, (need + x - start) * peers + y * DEPTH + depth, place)
        return place.astype(jnp.int32)

    def at_edges(row):
        row = jnp.broadcast_to(row, (PER_LINE, LANES)).astype(BF16)
        return dot(row, at_owner)[:1]

    order = jnp.sum(dot(rank.astype(BF16), at_owner) * at_within.astype(F32), 0, keepdims=True)
    edge_ref[...] = placed(owner, order - 1.0, at_edges)
    for n, at in enumerate(at_neg):
        order = dot(before(peers), at.astype(BF16)) + from_edges
        order = jnp.sum(order * at, 1, keepdims=True)

        def at_these(row):
            return jnp.sum(row * at, 1, keepdims=True)

        neg_ref[n * peers : (n + 1) * peers, :] = placed(negs[n][:, :1], order, at_these)
        from_edges = from_edges + jnp.sum(at, 0, keepdims=True)


def unpack(ref, hi_ref, lo_ref):
    peers = ref.shape[0] // BLOCK
    group = iota((peers, LANES), 1) // TAIL
    for k in range(CAP):
        span = slice(k * peers, (k + 1) * peers)
        for t in range(PARTS):
            hi, lo = pieces(ref[pl.ds(t * CAP + k, peers, stride=BLOCK), :], 2)
            hi_ref[span, t * LANES : (t + 1) * LANES] = hi
            lo_ref[span, t * LANES : (t + 1) * LANES] = lo
        tails = ref[pl.ds(LINES + k // PER_LINE, peers, stride=BLOCK), :]
        hi, lo = pieces(jnp.where(group == k % PER_LINE, tails, 0.0), 2)
        both = hi.astype(F32) + pltpu.roll(lo.astype(F32), LANES // 2, 1)
        hi_ref[span, MAIN:] = both.astype(BF16)


def gathered(chosen, hi_ref, lo_ref):
    of_hi = dot(chosen, hi_ref[...])
    return of_hi[:, :MAIN] + dot(chosen, lo_ref[...]), spread(of_hi[:, MAIN:])


def edges_kernel(
    block_ref, place_ref, neg_place_ref, row_place_ref, rel_hi_ref, rel_lo_ref,
    out_ref, slots_hi, slots_lo, grad_hi, grad_lo,
):
    peers = block_ref.shape[0] // BLOCK
    edges = place_ref.shape[0] // 2
    total = neg_place_ref.shape[0]
    kinds = rel_hi_ref.shape[0]
    per_rel = edges // kinds
    count = peers * CAP
    unpack(block_ref, slots_hi, slots_lo)

    spot = jnp.concatenate([place_ref[...], neg_place_ref[...]], 0)
    chosen = bits(iota((spot.shape[0], count), 1) == spot)
    got = jnp.concatenate(gathered(chosen, slots_hi, slots_lo), 1)

    def keep(start, grad):
        span = slice(start, start + grad.shape[0])
        grad_hi[span, :MAIN], grad_lo[span, :] = pieces(grad[:, :MAIN], 2)
        grad_hi[span, MAIN:] = halves(*pieces(spread(grad[:, MAIN:]), 2))

    spans = [slice(kind * per_rel, (kind + 1) * per_rel) for kind in range(kinds)]
    relations = [(rel_hi_ref[kind], rel_lo_ref[kind]) for kind in range(kinds)]
    query = jnp.concatenate([dot3(got[span], to) for span, to in zip(spans, relations)], 0)
    tail, negs = got[edges : 2 * edges], tuple(pieces(got[2 * edges :], 2))
    positive = jnp.sum(query * tail, 1, keepdims=True)
    grad_pos = jax.nn.sigmoid(positive) - 1.0
    keep(edges, grad_pos * query)
    query = tuple(pieces(query, 2))
    grad_neg = jax.nn.sigmoid(dot3(query, negs, 1, 1)) / total
    grad_query = grad_pos * tail + dot3(grad_neg, negs)
    for span, to in zip(spans, relations):
        keep(span.start, dot3(grad_query[span], to, 1, 1))
    grad_neg = jax.nn.sigmoid(dot3(negs, query, 1, 1)) / total
    keep(2 * edges, dot3(grad_neg, query))

    spot = row_place_ref[...]
    chosen = bits(iota((count, spot.shape[1]), 0) == spot)
    of_hi = dot(chosen, grad_hi[...])
    of_main = of_hi[:, :MAIN] + dot(chosen, grad_lo[...])
    pack(jnp.concatenate([of_main, fold(of_hi[:, MAIN:])], 1), out_ref)


def sum_kernel(block_ref, code_ref, list_ref, own_ref, hi_ref, lo_ref):
    unpack(block_ref, hi_ref, lo_ref)
    code = code_ref[...]
    row = lax.bitwise_and(code, CODE - 1) - 1
    entry = shift_down(code, 11) - 1
    listed = iota((ROOM, code.shape[1]), 0) == entry
    number = jnp.max(jnp.where(listed, row.astype(F32), -1.0), 1, keepdims=True)
    mine = iota((own_ref.shape[0], code.shape[1]), 0) == row
    chosen = jnp.concatenate([jnp.where(mine, 1.0, 0.0), jnp.where(listed, 1.0, 0.0)], 0)
    main, tails = gathered(chosen.astype(BF16), hi_ref, lo_ref)
    owned = own_ref.shape[0]
    own_ref[...] = jnp.concatenate([main[:owned], tails[:owned]], 1)
    tails = tails[owned:]
    tails = jnp.where(iota(tails.shape, 1) < TAIL, tails, number)
    for y in range(COLUMN):
        list_ref[y] = jnp.concatenate([main[owned:], tails], 1)


def update_kernel(me_ref, own_ref, lists_ref, table_ref, state_ref, new_table_ref, new_state_ref):
    width, owned = table_ref.shape
    rows = lists_ref[...].reshape(-1, WIDE)
    up = lax.shift_right_logical(me_ref[0], jnp.int32(4))
    mate = iota((rows.shape[0], 1), 0) // ROOM
    first = lax.bitwise_xor(mate, jnp.broadcast_to(up, mate.shape)) * owned
    at = rows[:, WIDE - 1 :].astype(jnp.int32) - first
    chosen = bits(iota((rows.shape[0], owned), 1) == at)
    hi, lo = pieces(rows, 2)
    grad = own_ref[...] + (dot(chosen, lo, 0, 0) + dot(chosen, hi, 0, 0))
    grad = grad.T[:width]
    state = state_ref[...] + jnp.sum(grad * grad, 0, keepdims=True) / width
    new_state_ref[...] = state
    new_table_ref[...] = table_ref[...] - LEARN_RATE * grad / (jnp.sqrt(state) + EPSILON)


def to_mates(x):
    peers = lax.axis_size("grp")
    return [
        lax.ppermute(x, "grp", [(p, p ^ (d * DEPTH)) for p in range(peers)])
        for d in range(1, COLUMN)
    ]


def exchange_blocks(blocks):
    peers = lax.axis_size("grp")
    return exchange(blocks.reshape(peers, BLOCK, 1, LANES)).reshape(blocks.shape)


def compact_path(me, marks, blocks, codes, source, target, number, rel_hi, rel_lo, table, state):
    peers = marks.shape[0] // 2
    edges = source.shape[1]
    width, owned = table.shape
    count = peers * CAP
    split = [pltpu.VMEM((count, WIDE), BF16), pltpu.VMEM((count, MAIN), BF16)]
    blocks = exchange_blocks(blocks)
    edge_place, neg_place = call(
        functools.partial(place_kernel, number),
        (shaped(1, 2 * edges, dtype=jnp.int32), shaped(peers * number, 1, dtype=jnp.int32)),
    )(marks, source, target)
    row_place = jnp.concatenate([edge_place, neg_place.reshape(1, -1)], 1)
    grads = call(
        edges_kernel,
        shaped(*blocks.shape),
        scratch_shapes=split
        + [pltpu.VMEM((row_place.shape[1], size), BF16) for size in (WIDE, MAIN)],
    )(blocks, edge_place.reshape(-1, 1), neg_place, row_place, rel_hi, rel_lo)
    returned = exchange_blocks(grads)
    codes = codes[:, :CAP].T.reshape(1, -1)
    lists, own = call(
        sum_kernel,
        (shaped(COLUMN, ROOM, WIDE), shaped(owned, WIDE)),
        scratch_shapes=split,
    )(returned, codes)
    lists = lax.all_to_all(
        lists, "grp", 0, 0, tiled=True,
        axis_index_groups=[list(range(z, peers, DEPTH)) for z in range(DEPTH)],
    )
    return call(
        update_kernel,
        (shaped(width, owned), shaped(1, owned)),
        in_specs=[SCALAR] + [VECTOR] * 4,
    )(me, own, lists, table, state)


def per_device(table, row_state, relations, touched, source, target, neg_slots):
    peers, sent = touched.shape
    owned, width = table.shape
    number = neg_slots.shape[0]
    across = table.T
    source_row, target_row = source.reshape(1, -1), target.reshape(1, -1)
    marks, bundle = call(
        mark_kernel,
        (shaped(2 * peers, LANES), shaped(width + sent, owned)),
        in_specs=[SCALAR] + [VECTOR] * 4,
        out_specs=(VECTOR, VECTOR),
    )(neg_slots, source_row, target_row, touched.T, across)
    marks = exchange(marks.reshape(peers, 2, 1, LANES)).reshape(2 * peers, LANES)
    bundles = [bundle] + to_mates(bundle)
    wide = jnp.pad(relations, ((0, 0), (0, WIDE - width), (0, WIDE - width)))
    rel_hi = lax.reduce_precision(wide, 8, 7)
    rel_lo = (wide - rel_hi).astype(BF16)
    rel_hi = rel_hi.astype(BF16)
    me = lax.axis_index("grp").reshape(1)
    blocks, codes, crowded = call(
        functools.partial(pack_kernel, number),
        (
            shaped(peers * BLOCK, LANES),
            shaped(peers, LANES, dtype=jnp.int32),
            shaped(1, dtype=jnp.int32),
        ),
        in_specs=[SCALAR] + [VECTOR] * (1 + COLUMN),
        out_specs=(VECTOR, VECTOR, SCALAR),
        scratch_shapes=[pltpu.VMEM((CAP * peers, owned + LANES), BF16)],
    )(me, marks, *bundles)
    new_table, new_state = lax.cond(
        crowded[0] > 0,
        lambda: full_path(table, row_state, relations, touched, source, target, neg_slots),
        lambda: compact_path(
            me, marks, blocks, codes, source_row, target_row, number, rel_hi, rel_lo, across,
            row_state.reshape(1, -1),
        ),
    )
    return new_table.T, new_state.reshape(-1)


def solution(mesh):
    return jax.shard_map(
        per_device,
        mesh=mesh,
        in_specs=(
            P(("grp", "rep"), None),
            P(("grp", "rep")),
            P(),
            P(("grp", "rep"), None),
            P(("grp", "rep")),
            P(("grp", "rep")),
            P(("grp", "rep")),
        ),
        out_specs=(P(("grp", "rep"), None), P(("grp", "rep"))),
        check_vma=False,
    )
```

```python
import functools

import jax
import jax.numpy as jnp
from jax import lax
from jax.experimental import pallas as pl
from jax.experimental.pallas import tpu as pltpu
from jax.sharding import PartitionSpec as P

PRECISE = lax.Precision.HIGHEST
LEARN_RATE = 0.1
EPSILON = 1e-06
LANES = 128
VMEM = 56 * 1024 * 1024
F32 = jnp.float32
BF16 = jnp.bfloat16


def exchange(blocks):
    return lax.all_to_all(blocks, "grp", split_axis=0, concat_axis=0, tiled=True)


def take_rows(rows, ids):
    return jnp.take(rows, ids, axis=0, mode="clip")


def to_lanes(rows, peers):
    width = rows.shape[1]
    wide = -(-width // LANES) * LANES
    return jnp.pad(rows, ((0, 0), (0, wide - width))).reshape(peers, -1, LANES)


def full_path(table, row_state, relations, touched, source, target, neg_slots):
    width = table.shape[1]
    peers, sent = touched.shape
    kinds = relations.shape[0]
    per_rel = source.shape[0] // kinds
    slot_count = peers * sent
    own_count = neg_slots.shape[0]
    neg_total = peers * own_count
    outgoing = take_rows(table, touched.reshape(-1))
    slots = exchange(outgoing.reshape(peers, -1, LANES)).reshape(slot_count, width)
    own_neg = to_lanes(take_rows(slots, neg_slots), 1)
    gathered = exchange(jnp.broadcast_to(own_neg, (peers,) + own_neg.shape[1:]))
    negatives = gathered.reshape(neg_total, -1)[:, :width]
    head = take_rows(slots, source)
    tail = take_rows(slots, target)
    query = jnp.einsum(
        "ked,kdf->kef", head.reshape(kinds, per_rel, width), relations, precision=PRECISE
    ).reshape(kinds * per_rel, width)
    positive = jnp.sum(query * tail, -1)
    negative = jnp.dot(query, negatives.T, precision=PRECISE)
    grad_pos = jax.nn.sigmoid(positive) - 1.0
    grad_neg = jax.nn.sigmoid(negative) / neg_total
    grad_negs = jnp.dot(grad_neg.T, query, precision=PRECISE)
    shares = exchange(to_lanes(grad_negs, peers))
    mine = jnp.sum(shares, 0).reshape(own_count, -1)[:, :width]
    grad_query = grad_pos[:, None] * tail + jnp.dot(grad_neg, negatives, precision=PRECISE)
    grad_tail = grad_pos[:, None] * query
    grad_head = jnp.einsum(
        "kef,kdf->ked", grad_query.reshape(kinds, per_rel, width), relations, precision=PRECISE
    ).reshape(kinds * per_rel, width)
    slot_grad = jnp.zeros((slot_count, width), F32).at[source].add(grad_head)
    slot_grad = slot_grad.at[target].add(grad_tail)
    slot_grad = slot_grad.at[neg_slots].add(mine)
    returned = exchange(slot_grad.reshape(peers, -1, LANES)).reshape(slot_count, width)
    row_grad = jnp.zeros(table.shape, F32).at[touched.reshape(-1)].add(returned)
    new_state = row_state + jnp.mean(row_grad * row_grad, -1)
    new_table = table - LEARN_RATE * row_grad / (jnp.sqrt(new_state)[:, None] + EPSILON)
    return new_table.T, new_state.reshape(1, -1)


CAP = 19
PARTS = 3
TAIL = 16
PER_LINE = LANES // TAIL
LINES = PARTS * CAP
BLOCK = LINES + -(-CAP // PER_LINE)
MAIN = PARTS * LANES
WIDE = MAIN + LANES
COLUMN = 4
DEPTH = 16
SENT = 32
NEG_ROOM = 24
SLOT_ROOM = 8
ROOM = NEG_ROOM + SLOT_ROOM
AT_NEGS = 64
CODE = 2048


def iota(shape, dim):
    return lax.broadcasted_iota(jnp.int32, shape, dim)


def bits(mask):
    return jnp.where(mask, 1.0, 0.0).astype(BF16)


def shift_down(x, by):
    return lax.shift_right_logical(x, jnp.full(x.shape, by, x.dtype))


def same_depth(a, b):
    return lax.bitwise_and(a, DEPTH - 1) == lax.bitwise_and(b, DEPTH - 1)


def grid(condition, size=LANES):
    return bits(condition(iota((size, size), 0), iota((size, size), 1)))


def pieces(x, count):
    out = []
    for _ in range(count):
        piece = x.astype(BF16)
        out.append(piece)
        x = x - piece.astype(F32)
    return out


def dot(a, b, a_dim=1, b_dim=0):
    return lax.dot_general(a, b, (((a_dim,), (b_dim,)), ((), ())), preferred_element_type=F32)


def dot3(a, b, a_dim=1, b_dim=0):
    a_hi, a_lo = a if isinstance(a, tuple) else pieces(a, 2)
    b_hi, b_lo = b if isinstance(b, tuple) else pieces(b, 2)
    rows = a_hi.shape[0]
    both = dot(jnp.concatenate([a_lo, a_hi], 0), b_hi, a_dim, b_dim)
    return both[:rows] + dot(a_hi, b_lo, a_dim, b_dim) + both[rows:]


def halves(hi, lo):
    lane = iota(hi.shape, 1)
    return jnp.where(lane < LANES // 2, hi.astype(F32), lo.astype(F32)).astype(BF16)


def fold(x):
    return x + pltpu.roll(x, LANES // 2, 1)


def spread(x):
    step = TAIL
    while step < LANES:
        x = x + pltpu.roll(x, step, 1)
        step *= 2
    return x


def call(kernel, outs, **kw):
    return pl.pallas_call(
        kernel,
        out_shape=outs,
        compiler_params=pltpu.CompilerParams(vmem_limit_bytes=VMEM),
        **kw,
    )


def shaped(*shape, dtype=F32):
    return jax.ShapeDtypeStruct(shape, dtype)


VECTOR = pl.BlockSpec(memory_space=pltpu.VMEM)
SCALAR = pl.BlockSpec(memory_space=pltpu.SMEM)


def mark_kernel(negs_ref, source_ref, target_ref, touched_ref, table_ref, out_ref, bundle_ref):
    width = table_ref.shape[0]
    sent, wide = touched_ref.shape
    bundle_ref[:width, :] = table_ref[...]
    bundle_ref[width:, :LANES] = jnp.concatenate(
        [touched_ref[...].astype(F32), jnp.zeros((sent, LANES - wide), F32)], 1
    )
    bundle_ref[width:, LANES:] = jnp.zeros((sent, bundle_ref.shape[1] - LANES), F32)
    peers = out_ref.shape[0] // 2
    ids = jnp.concatenate([source_ref[...], target_ref[...]], 1)
    count = ids.shape[1]
    owner = shift_down(ids, 5)
    within = lax.bitwise_and(ids, SENT - 1)
    at_depth = bits(same_depth(iota((peers, count), 0), owner))
    at_slot = bits(iota((LANES, count), 0) == shift_down(owner, 4) * SENT + within)
    marks = dot(at_depth, at_slot, 1, 1)
    out_ref[pl.ds(0, peers, stride=2), :] = jnp.where(marks > 0.0, 1.0, 0.0)
    at_owner = bits(iota((LANES, count), 0) == owner)
    at_within = bits(iota((SENT, count), 0) == within)
    used = jnp.where(dot(at_within, at_owner, 1, 1) > 0.0, 1.0, 0.0)
    info = jnp.broadcast_to(jnp.sum(used, 0, keepdims=True), marks.shape)
    lane = iota(marks.shape, 1)
    for n in range(negs_ref.shape[0]):
        info = jnp.where(lane == AT_NEGS + n, negs_ref[n].astype(F32), info)
    out_ref[pl.ds(1, peers, stride=2), :] = info


def neg_columns(info, number):
    lane = iota(info.shape, 1)
    columns = []
    for n in range(number):
        column = jnp.sum(jnp.where(lane == AT_NEGS + n, info, 0.0), 1, keepdims=True)
        columns.append(jnp.broadcast_to(column.astype(jnp.int32), info.shape))
    return columns


def before(count):
    return grid(lambda a, b: b < a, count)


def pack(rows, ref):
    peers = ref.shape[0] // BLOCK
    group = iota((peers, LANES), 1) // TAIL
    for part in range(BLOCK - LINES):
        line = jnp.zeros((peers, LANES), F32)
        for k in range(part * PER_LINE, min((part + 1) * PER_LINE, CAP)):
            mine = rows[k * peers : (k + 1) * peers]
            for t in range(PARTS):
                ref[pl.ds(t * CAP + k, peers, stride=BLOCK), :] = mine[:, t * LANES : (t + 1) * LANES]
            line = line + jnp.where(group == k % PER_LINE, mine[:, PARTS * LANES :], 0.0)
        ref[pl.ds(LINES + part, peers, stride=BLOCK), :] = line


def pack_kernel(
    number, me_ref, marks_ref, own_ref, first_ref, second_ref, third_ref, out_ref, codes_ref, flag_ref, onehot
):
    peers = marks_ref.shape[0] // 2
    marks = marks_ref[pl.ds(0, peers, stride=2), :]
    info = marks_ref[pl.ds(1, peers, stride=2), :]
    lane = iota(marks.shape, 1)
    negs = neg_columns(info, number)
    me = me_ref[0]
    depth, up = lax.bitwise_and(me, DEPTH - 1), lax.shift_right_logical(me, jnp.int32(4))
    refs = own_ref, first_ref, second_ref, third_ref
    width, owned = own_ref.shape[0] - SENT, own_ref.shape[1]

    touched = jnp.zeros(marks.shape, F32)
    for d, ref in enumerate(refs):
        rows = jnp.concatenate([ref[width:, :LANES], jnp.zeros((LANES - SENT, LANES), F32)], 0)
        rows = jnp.where(lane < SENT, rows.T[:peers] + (d * owned + 1.0), 0.0)
        touched = touched + pltpu.roll(rows, SENT * lax.bitwise_xor(up, jnp.int32(d)), 1)

    earlier = jnp.zeros((1, LANES), F32)
    neg_rows = jnp.zeros((1, LANES), F32)
    for slot in negs:
        owner = shift_down(slot, 5)
        at = jnp.where(lane == owner, 1.0, 0.0)
        rank = jnp.sum((dot(before(peers), at.astype(BF16)) + earlier) * at, 1, keepdims=True)
        earlier = earlier + jnp.sum(at, 0, keepdims=True)
        base = shift_down(owner, 4) * SENT
        at_row = lane == base + lax.bitwise_and(slot, SENT - 1)
        row = jnp.sum(jnp.where(at_row, touched, 0.0), 1, keepdims=True)
        here = same_depth(owner, depth) & (lane == base + rank.astype(jnp.int32))
        neg_rows = neg_rows + jnp.sum(jnp.where(here, row, 0.0), 0, keepdims=True)

    slots = jnp.where(lane < peers, info, 0.0)
    column = grid(same_depth)
    over_slots = jnp.sum(jnp.maximum(slots - CAP, 0.0), 0, keepdims=True)
    first = iota((PER_LINE, LANES), 0) == 0
    sums = jnp.where(first, earlier, over_slots).astype(BF16)
    sums = jnp.max(dot(sums, column) - jnp.where(first, NEG_ROOM, SLOT_ROOM))
    total = jnp.max(dot((slots + earlier).astype(BF16), column))
    over = (total > COLUMN * CAP) | (sums > 0.0)
    flag_ref[0] = over.astype(jnp.int32)

    neg_rows = jnp.broadcast_to(neg_rows, marks.shape)
    neg_marks = jnp.where(neg_rows > 0.0, 1.0, 0.0)
    block = grid(lambda a, b: a // SENT == b // SENT)
    earlier_block = grid(lambda a, b: (a % SENT == 0) & (a // SENT < b // SENT))
    rank = dot(marks.astype(BF16), grid(lambda a, b: (a // SENT == b // SENT) & (a <= b)))
    used = dot(marks.astype(BF16), block)
    neg_rank = used + (lane % SENT).astype(F32) + 1.0
    need = used + dot(neg_marks.astype(BF16), block)
    spare = jnp.maximum(CAP - need, 0.0)
    excess_from = dot(jnp.maximum(need - CAP, 0.0).astype(BF16), earlier_block)
    spare_from = dot(spare.astype(BF16), earlier_block)
    own = lane // SENT == up

    def mine(x):
        return jnp.sum(jnp.where(lane == SENT * up, x, 0.0), 1, keepdims=True)

    need, spare, spare_from = mine(need), mine(spare), mine(spare_from)

    def placed(rank, mask):
        x = excess_from + rank - (CAP + 1.0) - spare_from
        helped = jnp.where((rank > CAP) & (x >= 0.0) & (x < spare), need + x, -1.0)
        at = jnp.where(own, jnp.where(rank <= CAP, rank - 1.0, -1.0), helped)
        return jnp.where(mask > 0.0, at, -1.0)

    place, neg_place = placed(rank, marks), placed(neg_rank, neg_marks)
    upto = grid(lambda a, b: a <= b)
    helped = jnp.where((place >= 0.0) & ~own, 1.0, 0.0)
    held = jnp.broadcast_to(jnp.sum(helped, 1, keepdims=True), marks.shape)
    entry = dot(before(peers), held.astype(BF16)) + dot(helped.astype(BF16), upto)
    codes = touched + CODE * jnp.where(helped > 0.0, entry + NEG_ROOM, 0.0)
    neg_entry = dot(neg_marks.astype(BF16), upto)
    neg_codes = neg_rows + CODE * jnp.where((neg_place >= 0.0) & ~own, neg_entry, 0.0)

    mates = len(refs) - 1
    column = iota((SLOT_ROOM, LANES), 0)
    of_slots = jnp.zeros((SLOT_ROOM, LANES), F32)
    for e in range(SLOT_ROOM):
        row = jnp.sum(jnp.where((helped > 0.0) & (entry == e + 1.0), touched, 0.0), 0, keepdims=True)
        of_slots = jnp.where(column == e, row, of_slots)
    column = iota((NEG_ROOM, LANES), 0)
    of_negs = jnp.where((neg_entry[:1] == column + 1.0) & (neg_marks[:1] > 0.0), neg_rows[:1], 0.0)
    row = jnp.sum(jnp.concatenate([of_negs, of_slots], 0), 1, keepdims=True).astype(jnp.int32)
    from_mates = bits(iota((ROOM, mates * owned), 1) == row - (owned + 1))

    spot = iota((peers, owned + LANES), 1)
    out = jnp.zeros(marks.shape, jnp.int32)
    for k in range(CAP):
        code = jnp.where(place == k, codes, 0.0) + jnp.where(neg_place == k, neg_codes, 0.0)
        code = jnp.sum(code, 1, keepdims=True).astype(jnp.int32)
        out = jnp.where(lane == k, code, out)
        helping = shift_down(code, 11)
        own_row = lax.bitwise_and(code, CODE - 1) - 1
        at = jnp.where(helping > 0, owned - 1 + helping, own_row)
        onehot[k * peers : (k + 1) * peers, :] = bits(spot == at)
    codes_ref[...] = out

    def split(rows):
        hi, lo = pieces(rows, 2)
        return jnp.concatenate([hi[:, :MAIN], halves(hi[:, MAIN:], lo[:, MAIN:])], 1), lo[:, :MAIN]

    def fetched(chosen, hi, lo):
        of_hi = dot(chosen, hi)
        return jnp.concatenate([of_hi[:, :MAIN] + dot(chosen, lo), fold(of_hi[:, MAIN:])], 1)

    tables = [jnp.concatenate([ref[:MAIN]] + [ref[MAIN:width]] * PER_LINE, 0).T for ref in refs]
    held = fetched(from_mates, *split(jnp.concatenate(tables[1:], 0)))
    held = jnp.concatenate([tables[0], held, jnp.zeros((LANES - ROOM, WIDE), F32)], 0)
    got = fetched(onehot[...], *split(held))
    pack(got, out_ref)


def place_kernel(number, marks_ref, source_ref, target_ref, edge_ref, neg_ref):
    peers = marks_ref.shape[0] // 2
    info = marks_ref[pl.ds(1, peers, stride=2), :]
    ids = jnp.concatenate([source_ref[...], target_ref[...]], 1)
    count = ids.shape[1]
    owner = shift_down(ids, 5)
    at_owner = bits(iota((LANES, count), 0) == owner)
    at_within = bits(iota((SENT, count), 0) == lax.bitwise_and(ids, SENT - 1))
    used = bits(dot(at_within, at_owner, 1, 1) > 0.0)
    rank = dot(grid(lambda a, b: b <= a, SENT), used)
    from_edges = rank[SENT - 1 :]
    lane = iota(info.shape, 1)
    negs = [shift_down(slot, 5) for slot in neg_columns(info, number)]
    at_neg = [jnp.where(lane == slot, 1.0, 0.0) for slot in negs]
    need = from_edges
    for at in at_neg:
        need = need + jnp.sum(at, 0, keepdims=True)

    line = iota((PER_LINE, LANES), 0)
    spare = jnp.maximum(CAP - need, 0.0)
    excess = jnp.maximum(need - CAP, 0.0)
    first = jnp.where(line == 0, need, jnp.where(line == 1, spare, jnp.where(line == 2, excess, 0.0)))
    first = first.astype(BF16)
    earlier = dot(first, grid(lambda a, b: same_depth(a, b) & (a // DEPTH < b // DEPTH)))
    excess_from = earlier[2:3]
    first = jnp.where(line == 2, jnp.broadcast_to(earlier[1:2], first.shape), first.astype(F32))
    first = first.astype(BF16)
    mates = [
        dot(first, grid(lambda a, b: same_depth(a, b) & (a // DEPTH == y))) for y in range(COLUMN)
    ]

    def placed(owner, order, value):
        owner = owner.astype(F32)
        depth = owner - DEPTH * jnp.floor(owner / DEPTH)
        place = order * peers + owner
        x = value(excess_from) + order - CAP
        for y, mate in enumerate(mates):
            need, spare, start = (value(mate[i : i + 1]) for i in range(3))
            here = (order >= CAP) & (x >= start) & (x < start + spare)
            place = jnp.where(here, (need + x - start) * peers + y * DEPTH + depth, place)
        return place.astype(jnp.int32)

    def at_edges(row):
        row = jnp.broadcast_to(row, (PER_LINE, LANES)).astype(BF16)
        return dot(row, at_owner)[:1]

    order = jnp.sum(dot(rank.astype(BF16), at_owner) * at_within.astype(F32), 0, keepdims=True)
    edge_ref[...] = placed(owner, order - 1.0, at_edges)
    for n, at in enumerate(at_neg):
        order = dot(before(peers), at.astype(BF16)) + from_edges
        order = jnp.sum(order * at, 1, keepdims=True)

        def at_these(row):
            return jnp.sum(row * at, 1, keepdims=True)

        neg_ref[n * peers : (n + 1) * peers, :] = placed(negs[n][:, :1], order, at_these)
        from_edges = from_edges + jnp.sum(at, 0, keepdims=True)


def unpack(ref, hi_ref, lo_ref):
    peers = ref.shape[0] // BLOCK
    group = iota((peers, LANES), 1) // TAIL
    for k in range(CAP):
        span = slice(k * peers, (k + 1) * peers)
        for t in range(PARTS):
            hi, lo = pieces(ref[pl.ds(t * CAP + k, peers, stride=BLOCK), :], 2)
            hi_ref[span, t * LANES : (t + 1) * LANES] = hi
            lo_ref[span, t * LANES : (t + 1) * LANES] = lo
        tails = ref[pl.ds(LINES + k // PER_LINE, peers, stride=BLOCK), :]
        hi, lo = pieces(jnp.where(group == k % PER_LINE, tails, 0.0), 2)
        both = hi.astype(F32) + pltpu.roll(lo.astype(F32), LANES // 2, 1)
        hi_ref[span, MAIN:] = both.astype(BF16)


def gathered(chosen, hi_ref, lo_ref):
    of_hi = dot(chosen, hi_ref[...])
    return of_hi[:, :MAIN] + dot(chosen, lo_ref[...]), spread(of_hi[:, MAIN:])


def edges_kernel(
    block_ref, place_ref, neg_place_ref, row_place_ref, rel_hi_ref, rel_lo_ref,
    out_ref, slots_hi, slots_lo, grad_hi, grad_lo,
):
    peers = block_ref.shape[0] // BLOCK
    edges = place_ref.shape[0] // 2
    total = neg_place_ref.shape[0]
    kinds = rel_hi_ref.shape[0]
    per_rel = edges // kinds
    count = peers * CAP
    unpack(block_ref, slots_hi, slots_lo)

    spot = jnp.concatenate([place_ref[...], neg_place_ref[...]], 0)
    chosen = bits(iota((spot.shape[0], count), 1) == spot)
    got = jnp.concatenate(gathered(chosen, slots_hi, slots_lo), 1)

    def keep(start, grad):
        span = slice(start, start + grad.shape[0])
        grad_hi[span, :MAIN], grad_lo[span, :] = pieces(grad[:, :MAIN], 2)
        grad_hi[span, MAIN:] = halves(*pieces(spread(grad[:, MAIN:]), 2))

    spans = [slice(kind * per_rel, (kind + 1) * per_rel) for kind in range(kinds)]
    relations = [(rel_hi_ref[kind], rel_lo_ref[kind]) for kind in range(kinds)]
    query = jnp.concatenate([dot3(got[span], to) for span, to in zip(spans, relations)], 0)
    tail, negs = got[edges : 2 * edges], tuple(pieces(got[2 * edges :], 2))
    positive = jnp.sum(query * tail, 1, keepdims=True)
    grad_pos = jax.nn.sigmoid(positive) - 1.0
    keep(edges, grad_pos * query)
    query = tuple(pieces(query, 2))
    grad_neg = jax.nn.sigmoid(dot3(query, negs, 1, 1)) / total
    grad_query = grad_pos * tail + dot3(grad_neg, negs)
    for span, to in zip(spans, relations):
        keep(span.start, dot3(grad_query[span], to, 1, 1))
    keep(2 * edges, dot3(grad_neg.T, query))

    spot = row_place_ref[...]
    chosen = bits(iota((count, spot.shape[1]), 0) == spot)
    of_hi = dot(chosen, grad_hi[...])
    of_main = of_hi[:, :MAIN] + dot(chosen, grad_lo[...])
    pack(jnp.concatenate([of_main, fold(of_hi[:, MAIN:])], 1), out_ref)


def sum_kernel(block_ref, code_ref, list_ref, own_ref, hi_ref, lo_ref):
    unpack(block_ref, hi_ref, lo_ref)
    code = code_ref[...]
    row = lax.bitwise_and(code, CODE - 1) - 1
    entry = shift_down(code, 11) - 1
    listed = iota((ROOM, code.shape[1]), 0) == entry
    number = jnp.max(jnp.where(listed, row.astype(F32), -1.0), 1, keepdims=True)
    mine = iota((own_ref.shape[0], code.shape[1]), 0) == row
    chosen = jnp.concatenate([jnp.where(mine, 1.0, 0.0), jnp.where(listed, 1.0, 0.0)], 0)
    main, tails = gathered(chosen.astype(BF16), hi_ref, lo_ref)
    owned = own_ref.shape[0]
    own_ref[...] = jnp.concatenate([main[:owned], tails[:owned]], 1)
    tails = tails[owned:]
    tails = jnp.where(iota(tails.shape, 1) < TAIL, tails, number)
    for y in range(COLUMN):
        list_ref[y] = jnp.concatenate([main[owned:], tails], 1)


def update_kernel(me_ref, own_ref, lists_ref, table_ref, state_ref, new_table_ref, new_state_ref):
    width, owned = table_ref.shape
    rows = lists_ref[...].reshape(-1, WIDE)
    up = lax.shift_right_logical(me_ref[0], jnp.int32(4))
    mate = iota((rows.shape[0], 1), 0) // ROOM
    first = lax.bitwise_xor(mate, jnp.broadcast_to(up, mate.shape)) * owned
    at = rows[:, WIDE - 1 :].astype(jnp.int32) - first
    chosen = bits(iota((rows.shape[0], owned), 1) == at)
    hi, lo = pieces(rows, 2)
    grad = own_ref[...] + (dot(chosen, lo, 0, 0) + dot(chosen, hi, 0, 0))
    grad = grad.T[:width]
    state = state_ref[...] + jnp.sum(grad * grad, 0, keepdims=True) / width
    new_state_ref[...] = state
    new_table_ref[...] = table_ref[...] - LEARN_RATE * grad / (jnp.sqrt(state) + EPSILON)


def to_mates(x):
    peers = lax.axis_size("grp")
    return [
        lax.ppermute(x, "grp", [(p, p ^ (d * DEPTH)) for p in range(peers)])
        for d in range(1, COLUMN)
    ]


def exchange_blocks(blocks):
    peers = lax.axis_size("grp")
    return exchange(blocks.reshape(peers, BLOCK, 1, LANES)).reshape(blocks.shape)


def compact_path(me, marks, blocks, codes, source, target, number, rel_hi, rel_lo, table, state):
    peers = marks.shape[0] // 2
    edges = source.shape[1]
    width, owned = table.shape
    count = peers * CAP
    split = [pltpu.VMEM((count, WIDE), BF16), pltpu.VMEM((count, MAIN), BF16)]
    blocks = exchange_blocks(blocks)
    edge_place, neg_place = call(
        functools.partial(place_kernel, number),
        (shaped(1, 2 * edges, dtype=jnp.int32), shaped(peers * number, 1, dtype=jnp.int32)),
    )(marks, source, target)
    row_place = jnp.concatenate([edge_place, neg_place.reshape(1, -1)], 1)
    grads = call(
        edges_kernel,
        shaped(*blocks.shape),
        scratch_shapes=split
        + [pltpu.VMEM((row_place.shape[1], size), BF16) for size in (WIDE, MAIN)],
    )(blocks, edge_place.reshape(-1, 1), neg_place, row_place, rel_hi, rel_lo)
    returned = exchange_blocks(grads)
    codes = codes[:, :CAP].T.reshape(1, -1)
    lists, own = call(
        sum_kernel,
        (shaped(COLUMN, ROOM, WIDE), shaped(owned, WIDE)),
        scratch_shapes=split,
    )(returned, codes)
    lists = lax.all_to_all(
        lists, "grp", 0, 0, tiled=True,
        axis_index_groups=[list(range(z, peers, DEPTH)) for z in range(DEPTH)],
    )
    return call(
        update_kernel,
        (shaped(width, owned), shaped(1, owned)),
        in_specs=[SCALAR] + [VECTOR] * 4,
    )(me, own, lists, table, state)


def per_device(table, row_state, relations, touched, source, target, neg_slots):
    peers, sent = touched.shape
    owned, width = table.shape
    number = neg_slots.shape[0]
    across = table.T
    source_row, target_row = source.reshape(1, -1), target.reshape(1, -1)
    marks, bundle = call(
        mark_kernel,
        (shaped(2 * peers, LANES), shaped(width + sent, owned)),
        in_specs=[SCALAR] + [VECTOR] * 4,
        out_specs=(VECTOR, VECTOR),
    )(neg_slots, source_row, target_row, touched.T, across)
    marks = exchange(marks.reshape(peers, 2, 1, LANES)).reshape(2 * peers, LANES)
    bundles = [bundle] + to_mates(bundle)
    wide = jnp.pad(relations, ((0, 0), (0, WIDE - width), (0, WIDE - width)))
    rel_hi = lax.reduce_precision(wide, 8, 7)
    rel_lo = (wide - rel_hi).astype(BF16)
    rel_hi = rel_hi.astype(BF16)
    me = lax.axis_index("grp").reshape(1)
    blocks, codes, crowded = call(
        functools.partial(pack_kernel, number),
        (
            shaped(peers * BLOCK, LANES),
            shaped(peers, LANES, dtype=jnp.int32),
            shaped(1, dtype=jnp.int32),
        ),
        in_specs=[SCALAR] + [VECTOR] * (1 + COLUMN),
        out_specs=(VECTOR, VECTOR, SCALAR),
        scratch_shapes=[pltpu.VMEM((CAP * peers, owned + LANES), BF16)],
    )(me, marks, *bundles)
    new_table, new_state = lax.cond(
        crowded[0] > 0,
        lambda: full_path(table, row_state, relations, touched, source, target, neg_slots),
        lambda: compact_path(
            me, marks, blocks, codes, source_row, target_row, number, rel_hi, rel_lo, across,
            row_state.reshape(1, -1),
        ),
    )
    return new_table.T, new_state.reshape(-1)


def solution(mesh):
    return jax.shard_map(
        per_device,
        mesh=mesh,
        in_specs=(
            P(("grp", "rep"), None),
            P(("grp", "rep")),
            P(),
            P(("grp", "rep"), None),
            P(("grp", "rep")),
            P(("grp", "rep")),
            P(("grp", "rep")),
        ),
        out_specs=(P(("grp", "rep"), None), P(("grp", "rep"))),
        check_vma=False,
    )
```
